256 devices in a mesh: gx: 4 (over z_hi, core), gy: 16 (over x, y), gz: 4 (over z_lo).
Axes of the slice: x: 4, y: 4, z: 8 (z_hi: 2, z_lo: 4; z = z_hi * 4 + z_lo), core: 2. Of those that a mesh axis runs over, the one named last changes fastest.
Arguments:
- features: bfloat16 [4, 16, 8, 128, 128], P('gx', 'gy', 'gz'), may hold values from -24 to 24
- frac: bfloat16 [4, 16, 8, 3, 128], P('gx', 'gy', 'gz'), may hold values from -0.5 to 0.5
- subpoint: int32 [4, 16, 8, 3, 128], P('gx', 'gy', 'gz'), may hold values from 0 to 5
- counts: int32 [4, 16, 8], P('gx', 'gy', 'gz'), may hold values from 32 to 128, as said below
- w_query: bfloat16 [128, 128], replicated, may hold values from -1 to 1
- w_key: bfloat16 [128, 128], replicated, may hold values from -1 to 1
- w_value: bfloat16 [128, 128], replicated, may hold values from -0.5 to 0.5
- rbf_coef: float32 [8], replicated, may hold values from -3 to 3
- w_out: bfloat16 [128, 128], replicated, may hold values from -0.5 to 0.5
- w_charge: bfloat16 [128, 128], replicated, may hold values from -0.5 to 0.5
- mode_weight: bfloat16 [2, 96, 48, 3072], P(None, 'gx', 'gy', 'gz'), may hold values from -18 to 18
- mesh_gain: float32 [128], replicated, may hold values from 0.1 to 1.9
- w_up: bfloat16 [128, 256], replicated, may hold values from -0.5 to 0.5
- w_down: bfloat16 [256, 128], replicated, may hold values from -0.375 to 0.375
Outputs:
- atoms_out: bfloat16 [4, 16, 8, 128, 128], P('gx', 'gy', 'gz')
The draws below stay inside these ranges and needn't reach their ends.
Inputs may be any that keep to these rules, and one draw needn't show every extreme that they name: `counts`: a cell's atoms fill its first slots; at least 32 atoms in every cell, and some cell holds 128.
All inputs are finite; a program needn't handle non-finite values.
Results may differ from the reference program's by a relative error of at most 0.012.
Values may be sent and summed in bfloat16 or wider, within the bound.
A program may use at most 64 MiB of HBM per device.

```python
import math
import jax
import jax.numpy as jnp
from jax import lax

D = 128
C = 128
FF = 256
A = 128
R = 6
NRBF = 8
NCX = 4
NCY = 16
NCZ = 8
MX = 24
MY = 96
MZ = 48


def projection_pair(key):
    base_key = jax.random.fold_in(key, 7)
    query_w = jax.random.normal(jax.random.fold_in(base_key, 1), (D, D), jnp.float32) / math.sqrt(D)
    key_w = jax.random.normal(jax.random.fold_in(base_key, 3), (D, D), jnp.float32) / math.sqrt(D)
    return (jnp.clip(query_w, -1.0, 1.0), jnp.clip(key_w, -1.0, 1.0))


def draw_w_query(key, part):
    return projection_pair(key)[0].astype(jnp.bfloat16)


def draw_w_key(key, part):
    return projection_pair(key)[1].astype(jnp.bfloat16)


def draw_features(key, part):
    shape_all = (NCX, NCY, NCZ, A, D)
    values = jnp.clip(jax.random.normal(jax.random.fold_in(key, 30), shape_all, jnp.float32), -6.0, 6.0)
    return values.astype(jnp.bfloat16)


def draw_counts(key, part):
    filled = jax.random.randint(jax.random.fold_in(key, 51), (NCX, NCY, NCZ), A // 4, A + 1)
    chosen = jax.random.randint(jax.random.fold_in(key, 52), (), 0, NCX * NCY * NCZ)
    flat_index = lax.broadcasted_iota(jnp.int32, (NCX, NCY, NCZ), 0) * (NCY * NCZ)
    flat_index = flat_index + lax.broadcasted_iota(jnp.int32, (NCX, NCY, NCZ), 1) * NCZ
    flat_index = flat_index + lax.broadcasted_iota(jnp.int32, (NCX, NCY, NCZ), 2)
    return jnp.where(flat_index == chosen, A, filled).astype(jnp.int32)


def draw_mode_weight(key, part):
    shape_all = (2, MY, MZ, C, MX)
    values = jnp.clip(jax.random.normal(jax.random.fold_in(key, 60), shape_all, jnp.float32), -4.0, 4.0)
    values = jnp.clip(values, -18.0, 18.0)
    return values.reshape(2, MY, MZ, C * MX).astype(jnp.bfloat16)


def touch_ends(values, rng, smallest, top_value):
    longest = values.shape.index(max(values.shape))
    spots = []
    for shift in (0, 1):
        where = [jax.random.randint(jax.random.fold_in(rng, axis), (), 0, length) for axis, length in enumerate(values.shape)]
        where[longest] = (where[longest] + shift) % values.shape[longest]
        spots.append(tuple(where))
    return values.at[spots[0]].set(smallest).at[spots[1]].set(top_value)


def shard_levels(stream_key, dims, shards, smallest, largest):
    gain = 1.0
    for dim, parts in shards:
        heights = jax.random.uniform(jax.random.fold_in(jax.random.fold_in(stream_key, 6), dim), (parts,), jnp.float32, smallest / len(shards), largest / len(shards))
        gain = gain * jnp.repeat(jnp.exp(heights), dims[dim] // parts).reshape((-1,) + (1,) * (len(dims) - 1 - dim))
    return gain


def bell_draw(stream_key, dims, deviation, reach, kind=jnp.bfloat16):
    drawn = deviation * jax.random.normal(stream_key, dims, jnp.float32)
    return jnp.clip(drawn, min=-reach, max=reach).astype(kind)


def setup_inputs(seed: int = 0) -> dict:
    key_list = jax.random.split(jax.random.key(seed), 15)
    features = draw_features(jax.random.fold_in(key_list[14], 71), 0)
    frac = jnp.clip(jax.random.uniform(key_list[1], (NCX, NCY, NCZ, 3, A), jnp.float32, -0.5, 0.5) * shard_levels(key_list[1], (NCX, NCY, NCZ, 3, A), ((0, 4), (1, 16), (2, 4)), -0.4, 0.0), -0.5, 0.5).astype(jnp.bfloat16)
    subpoint = touch_ends(jax.random.randint(key_list[2], (NCX, NCY, NCZ, 3, A), 0, R), jax.random.fold_in(key_list[2], 1), 0, R - 1).astype(jnp.int32)
    counts = draw_counts(jax.random.fold_in(key_list[14], 71), 0)
    w_query = draw_w_query(jax.random.fold_in(key_list[14], 71), 0)
    w_key = draw_w_key(jax.random.fold_in(key_list[14], 71), 0)
    w_value = bell_draw(key_list[6], (D, D), D ** -0.5, 0.5)
    rbf_coef = bell_draw(key_list[7], (NRBF,), 1.0, 3.0, jnp.float32)
    w_out = bell_draw(key_list[8], (D, D), D ** -0.5, 0.5)
    w_charge = bell_draw(key_list[9], (D, C), D ** -0.5, 0.5)
    mode_weight = draw_mode_weight(jax.random.fold_in(key_list[14], 71), 0)
    mesh_gain = jnp.clip(1.0 + 0.18 * jax.random.normal(key_list[11], (C,), jnp.float32), 0.1, 1.9)
    w_up = bell_draw(key_list[12], (D, FF), D ** -0.5, 0.5)
    w_down = bell_draw(key_list[13], (FF, D), FF ** -0.5, 0.375)
    return {"features": features, "frac": frac, "subpoint": subpoint, "counts": counts, "w_query": w_query, "w_key": w_key, "w_value": w_value, "rbf_coef": rbf_coef, "w_out": w_out, "w_charge": w_charge, "mode_weight": mode_weight, "mesh_gain": mesh_gain, "w_up": w_up, "w_down": w_down}


OFFSETS = [(step_x, step_y, step_z) for step_x in (-1, 0, 1) for step_y in (-1, 0, 1) for step_z in (-1, 0, 1)]

def radial_bias(dist_sq, rbf_coef):
    bias_total = jnp.zeros_like(dist_sq)
    for basis_index in range(NRBF):
        bias_total = bias_total + rbf_coef[basis_index] * jnp.exp(-(0.08 * 2.0 ** basis_index) * dist_sq)
    return bias_total

def attend(queries, key_rows, value_rows, query_pos, key_pos, key_valid, rbf_coef):
    raw_scores = jnp.einsum('nad,nkd->nak', queries.astype(jnp.float32), key_rows.astype(jnp.float32))
    dist_sq = jnp.zeros_like(raw_scores)
    for coordinate in range(3):
        coord_gap = key_pos[:, coordinate, None, :] - query_pos[:, coordinate, :, None]
        dist_sq = dist_sq + coord_gap * coord_gap
    scores = raw_scores * (1.0 / math.sqrt(D)) + radial_bias(dist_sq, rbf_coef)
    scores = jnp.where(key_valid[:, None, :], scores, -jnp.inf)
    row_top = lax.optimization_barrier(jnp.max(scores, axis=-1, keepdims=True))
    exp_scores = jnp.exp(scores - row_top)
    weights = (exp_scores / lax.optimization_barrier(jnp.sum(exp_scores, axis=-1, keepdims=True))).astype(jnp.bfloat16)
    mixed_rows = jnp.einsum('nak,nkd->nad', weights.astype(jnp.float32), value_rows.astype(jnp.float32))
    return mixed_rows.astype(jnp.bfloat16)

def stencil_weights(subpoint, frac):
    points = jnp.arange(R + 2, dtype=jnp.int32)
    offset = points - 1 - subpoint[..., None]
    shifted = frac.astype(jnp.float32)[..., None]
    lower_w = 0.5 * (0.5 - shifted) ** 2
    centre_w = 0.75 - shifted * shifted
    upper_w = 0.5 * (0.5 + shifted) ** 2
    zeroes = jnp.zeros_like(lower_w)
    return jnp.where(offset == -1, lower_w, jnp.where(offset == 0, centre_w, jnp.where(offset == 1, upper_w, zeroes)))

def combine(weights_dim):
    weight_x = weights_dim[..., 0, :, :]
    weight_y = weights_dim[..., 1, :, :]
    weight_z = weights_dim[..., 2, :, :]
    return weight_x[..., :, None, None] * weight_y[..., None, :, None] * weight_z[..., None, None, :]

def fold_line(blocks, dim_index):
    cell_count = blocks.shape[dim_index]
    head_part = lax.slice_in_dim(blocks, 0, R, axis=dim_index + 1)
    tail_part = lax.slice_in_dim(blocks, R, R + 2, axis=dim_index + 1)
    head_pad = [(0, 0)] * blocks.ndim
    head_pad[dim_index] = (0, 1)
    tail_pad = [(0, 0)] * blocks.ndim
    tail_pad[dim_index] = (1, 0)
    tail_pad[dim_index + 1] = (0, R - 2)
    summed = jnp.pad(head_part, head_pad) + jnp.pad(tail_part, tail_pad)
    shape_now = summed.shape
    merged = summed.reshape(shape_now[:dim_index] + ((cell_count + 1) * R,) + shape_now[dim_index + 2:])
    return lax.slice_in_dim(merged, 0, cell_count * R + 2, axis=dim_index)

def wrap_line(line_data, dim_index):
    inner_len = line_data.shape[dim_index] - 2
    middle = lax.slice_in_dim(line_data, 1, inner_len + 1, axis=dim_index)
    front_rim = lax.slice_in_dim(line_data, inner_len + 1, inner_len + 2, axis=dim_index)
    back_rim = lax.slice_in_dim(line_data, 0, 1, axis=dim_index)
    front_pad = [(0, 0)] * line_data.ndim
    front_pad[dim_index] = (0, inner_len - 1)
    back_pad = [(0, 0)] * line_data.ndim
    back_pad[dim_index] = (inner_len - 1, 0)
    return middle + jnp.pad(front_rim, front_pad) + jnp.pad(back_rim, back_pad)

def line_blocks(line_data, dim_index):
    cell_count = (line_data.shape[dim_index] - 2) // R
    widths = [(0, 0)] * line_data.ndim
    widths[dim_index] = (0, R - 2)
    extended = jnp.pad(line_data, widths)
    shape_now = extended.shape
    reshaped = extended.reshape(shape_now[:dim_index] + (cell_count + 1, R) + shape_now[dim_index + 1:])
    head_part = lax.slice_in_dim(reshaped, 0, cell_count, axis=dim_index)
    tail_part = lax.slice_in_dim(lax.slice_in_dim(reshaped, 1, cell_count + 1, axis=dim_index), 0, 2, axis=dim_index + 1)
    return jnp.concatenate([head_part, tail_part], axis=dim_index + 1)

def neighbour_rows(table_data, index_x, index_y):
    pieces = []
    for step_x, step_y, step_z in OFFSETS:
        plane_rows = lax.dynamic_index_in_dim(table_data, (index_x + step_x) % NCX, 0, keepdims=False)
        line_rows = lax.dynamic_index_in_dim(plane_rows, (index_y + step_y) % NCY, 0, keepdims=False)
        pieces.append(jnp.roll(line_rows, -step_z, axis=0))
    return jnp.stack(pieces, axis=1)

def reference(features, frac, subpoint, counts, w_query, w_key, w_value, rbf_coef, w_out, w_charge, mode_weight, mesh_gain, w_up, w_down):
    slot_index = lax.broadcasted_iota(jnp.int32, (NCX, NCY, NCZ, A), 3)
    valid_mask = slot_index < counts[..., None]
    coords = ((subpoint.astype(jnp.float32) + 0.5 + frac.astype(jnp.float32)) / R).astype(jnp.bfloat16)
    queries = jnp.dot(features, w_query, preferred_element_type=jnp.float32).astype(jnp.bfloat16)
    key_rows = jnp.dot(features, w_key, preferred_element_type=jnp.float32).astype(jnp.bfloat16)
    value_rows = jnp.dot(features, w_value, preferred_element_type=jnp.float32).astype(jnp.bfloat16)
    offsets = jnp.array(OFFSETS, dtype=jnp.float32)

    def plane_block(index_x):

        def line_block(index_y):
            near_keys = neighbour_rows(key_rows, index_x, index_y).reshape(NCZ, 27 * A, D)
            near_values = neighbour_rows(value_rows, index_x, index_y).reshape(NCZ, 27 * A, D)
            near_pos = neighbour_rows(coords, index_x, index_y).astype(jnp.float32) + offsets[None, :, :, None]
            near_pos = jnp.transpose(near_pos, (0, 2, 1, 3)).reshape(NCZ, 3, 27 * A)
            near_valid = neighbour_rows(valid_mask, index_x, index_y).reshape(NCZ, 27 * A)
            own_queries = lax.dynamic_index_in_dim(lax.dynamic_index_in_dim(queries, index_x, 0, keepdims=False), index_y, 0, keepdims=False)
            own_pos = lax.dynamic_index_in_dim(lax.dynamic_index_in_dim(coords, index_x, 0, keepdims=False), index_y, 0, keepdims=False).astype(jnp.float32)
            return attend(own_queries, near_keys, near_values, own_pos, near_pos, near_valid, rbf_coef)
        return lax.map(line_block, jnp.arange(NCY, dtype=jnp.int32))
    attended = lax.map(plane_block, jnp.arange(NCX, dtype=jnp.int32))
    after_attn = features.astype(jnp.float32) + jnp.dot(attended, w_out, preferred_element_type=jnp.float32)
    charges = jnp.dot(features, w_charge, preferred_element_type=jnp.float32) * valid_mask[..., None].astype(jnp.float32)
    weights_dim = stencil_weights(subpoint, frac)

    def deposit(carry, index_x):
        slab_weight = combine(lax.dynamic_index_in_dim(weights_dim, index_x, 0, keepdims=False))
        slab_charge = lax.dynamic_index_in_dim(charges, index_x, 0, keepdims=False)
        blocks = jnp.einsum('yzapqr,yzac->pyqzrc', slab_weight, slab_charge, precision=lax.Precision.HIGHEST)
        folded = wrap_line(fold_line(blocks, 1), 1)
        folded = wrap_line(fold_line(folded, 2), 2)
        current = lax.dynamic_slice_in_dim(carry, R * index_x, R + 2, 0)
        carry = lax.dynamic_update_slice_in_dim(carry, current + folded, R * index_x, 0)
        return (carry, None)
    padded = jnp.zeros((MX + 2, MY, MZ, C), jnp.float32)
    padded, unused = lax.scan(deposit, padded, jnp.arange(NCX, dtype=jnp.int32))
    density = wrap_line(padded, 0)
    mode_full = jnp.transpose(mode_weight.reshape(2, MY, MZ, C, MX), (0, 4, 1, 2, 3))

    def filter_group(index_c):
        first_chan = index_c * 16
        density_part = lax.dynamic_slice_in_dim(density, first_chan, 16, 3)
        real_weight = lax.dynamic_slice_in_dim(mode_full[0], first_chan, 16, 3).astype(jnp.float32)
        imag_weight = lax.dynamic_slice_in_dim(mode_full[1], first_chan, 16, 3).astype(jnp.float32)
        spectrum = jnp.fft.fftn(density_part, axes=(0, 1, 2))
        spectrum = spectrum * (real_weight + 1j * imag_weight)
        return jnp.real(jnp.fft.ifftn(spectrum, axes=(0, 1, 2)))
    potential = lax.map(filter_group, jnp.arange(C // 16, dtype=jnp.int32))
    potential = jnp.moveaxis(potential, 0, 3).reshape(MX, MY, MZ, C)
    padded_pot = jnp.pad(potential, ((1, 1), (1, 1), (1, 1), (0, 0)), mode='wrap')

    def sample_plane(index_x):
        slab_rows = lax.dynamic_slice_in_dim(padded_pot, R * index_x, R + 2, 0)
        blocks = line_blocks(line_blocks(slab_rows, 1), 3)
        slab_weight = combine(lax.dynamic_index_in_dim(weights_dim, index_x, 0, keepdims=False))
        return jnp.einsum('yzapqr,pyqzrc->yzac', slab_weight, blocks, precision=lax.Precision.HIGHEST)
    sampled = lax.map(sample_plane, jnp.arange(NCX, dtype=jnp.int32))
    norm_scale = lax.rsqrt(lax.optimization_barrier(jnp.mean(sampled * sampled, axis=-1, keepdims=True)) + 1e-06)
    joined = after_attn + sampled * norm_scale * mesh_gain
    joined_in = joined.astype(jnp.bfloat16)
    inner_act = jax.nn.silu(jnp.dot(joined_in, w_up, preferred_element_type=jnp.float32)).astype(jnp.bfloat16)
    result = joined + jnp.dot(inner_act, w_down, preferred_element_type=jnp.float32)
    return jnp.where(valid_mask[..., None], result, 0.0).astype(jnp.bfloat16)
```

```python
import functools
import math

import jax
import jax.numpy as jnp
import numpy as np
from jax import lax
from jax.experimental import pallas as pl
from jax.experimental.pallas import tpu as pltpu
from jax.sharding import PartitionSpec as P

MESH = pl.DeviceIdType.MESH
F32 = jnp.float32
BF16 = jnp.bfloat16

D = 128
R = 6
NRBF = 8
MX, MY, MZ = 24, 96, 48
NL = 256
LOG2E = math.log2(math.e)


def tables():
    gx, ch, px = np.meshgrid(np.arange(4), np.arange(8), np.arange(8), indexing="ij")
    x_pos, x_ch = (6 * gx + px - 1).reshape(-1), ch.reshape(-1)
    lane = np.arange(NL)
    l_ch, l_kx, l_ok = lane // MX, lane % MX, lane < 8 * MX
    ang = 2 * np.pi / MX * ((x_pos[:, None] * l_kx[None, :]) % MX)
    same = (x_ch[:, None] == l_ch[None, :]) & l_ok[None, :]
    cos_x, sin_x = np.where(same, np.cos(ang), 0.0), np.where(same, np.sin(ang), 0.0)
    fwd_x = np.concatenate([cos_x, -sin_x], axis=1)
    inv_x = np.concatenate([cos_x.T, -sin_x.T], axis=0)

    gz, cell, pz = np.meshgrid(np.arange(4), np.arange(2), np.arange(8), indexing="ij")
    z_pos = (12 * gz + 6 * cell + pz - 1).reshape(-1)
    ang = 2 * np.pi / MZ * ((z_pos[None, :] * np.arange(MZ)[:, None]) % MZ)
    c, s = np.cos(ang), np.sin(ang)
    mat = np.stack([np.stack([c, s], 1), np.stack([-s, c], 1)], axis=1)
    eye = np.eye(8)
    fwd_z = np.einsum("kciz,pq->kcpizq", mat, eye).reshape(MZ * 2 * 8, 2 * 64 * 8)
    mat = np.stack([np.stack([c.T, -s.T], -1), np.stack([s.T, c.T], -1)], axis=0)
    inv_z = np.einsum("czki,pq->czpkiq", mat, eye).reshape(2 * 64 * 8, MZ * 2 * 8)

    gy, py = np.meshgrid(np.arange(16), np.arange(8), indexing="ij")
    y_pos = (6 * gy + py - 1)
    ang = 2 * np.pi / MY * ((y_pos[None] * np.arange(MY)[:, None, None]) % MY)
    c, s = np.cos(ang), np.sin(ang)
    fwd_y = np.stack([np.stack([c, s], 2), np.stack([-s, c], 2)], axis=0)
    fwd_y = fwd_y.reshape(2 * MY, 256)
    ct, st = np.moveaxis(c, 0, -1), np.moveaxis(s, 0, -1)
    inv_y = np.stack([np.stack([ct, -st], 2), np.stack([st, ct], 2)], axis=1)
    inv_y = inv_y.reshape(256, 2 * MY)
    return [jnp.asarray(t, dtype=BF16) for t in (fwd_x, fwd_z, fwd_y, inv_y, inv_z, inv_x)]


def dot_nn(a, b):
    return lax.dot_general(a, b, (((1,), (0,)), ((), ())), preferred_element_type=F32)


def dot_nt(a, b):
    return lax.dot_general(a, b, (((1,), (1,)), ((), ())), preferred_element_type=F32)


def dot_tn(a, b):
    return lax.dot_general(a, b, (((0,), (0,)), ((), ())), preferred_element_type=F32)


def swap_halves(first, second):
    low = lax.broadcasted_iota(jnp.int32, first.shape, 1) < 64
    return (
        jnp.where(low, first, pltpu.roll(second, 64, 1)),
        jnp.where(low, pltpu.roll(first, 64, 1), second),
    )


def stencil(point, sub, frac):
    offset = point - 1.0 - sub
    lower_w = 0.5 * (0.5 - frac) * (0.5 - frac)
    centre_w = 0.75 - frac * frac
    upper_w = 0.5 * (0.5 + frac) * (0.5 + frac)
    zero = jnp.zeros_like(offset)
    return jnp.where(
        offset == -1.0,
        lower_w,
        jnp.where(offset == 0.0, centre_w, jnp.where(offset == 1.0, upper_w, zero)),
    )


def split3(value):
    high = value.astype(BF16).astype(F32)
    rest = value - high
    middle = rest.astype(BF16).astype(F32)
    return high, middle, rest - middle


def kernel(
    feat_ref,
    frac_ref,
    sub_ref,
    counts_ref,
    coef_ref,
    wq_ref,
    wk_ref,
    wv_ref,
    wo_ref,
    wch_ref,
    wsend_ref,
    gain_ref,
    wup_ref,
    wdown_ref,
    fx_ref,
    fz_ref,
    fy_ref,
    iy_ref,
    iz_ref,
    ix_ref,
    out_ref,
    halo,
    s1,
    r1,
    s2,
    r2,
    s3,
    r3,
    s4,
    r4,
    wrecv,
    wf,
    aux,
    x1,
    t2,
    v2,
    wyz,
    wx,
    rep,
    cols,
    qs,
    qaug,
    kaug,
    scores,
    dist,
    vext,
    smax,
    send_sem,
    recv_sem,
    hsend,
    hrecv,
    wsem,
    wrsem,
):
    gx, gy, gz = lax.axis_index("gx"), lax.axis_index("gy"), lax.axis_index("gz")
    me_xz = gz * 4 + gx

    def dev_xz(p):
        return {"gx": lax.rem(p, 4), "gz": lax.div(p, 4)}

    def dev_y(p):
        return {"gy": p}

    def remote(src, dst, ssem, rsem, device):
        return pltpu.make_async_remote_copy(
            src_ref=src, dst_ref=dst, send_sem=ssem, recv_sem=rsem, device_id=device, device_id_type=MESH
        )

    barrier = pltpu.get_barrier_semaphore()
    for off in range(1, 16):
        pl.semaphore_signal(barrier, inc=1, device_id=dev_xz(lax.rem(me_xz + off, 16)), device_id_type=MESH)
        pl.semaphore_signal(barrier, inc=1, device_id=dev_y(lax.rem(gy + off, 16)), device_id_type=MESH)

    lane_row = lax.broadcasted_iota(jnp.int32, (1, 128), 1)
    aux[...] = jnp.zeros_like(aux)
    for c in range(2):
        sub = sub_ref[c].astype(F32)
        frac = frac_ref[c].astype(F32)
        aux[c, 0:3, :] = ((sub + 0.5 + frac) / R).astype(BF16).astype(F32)
        aux[c, 3:4, :] = (lane_row < counts_ref[c]).astype(F32)
        aux[c, 4:7, :] = frac
        aux[c, 7:10, :] = sub
        halo[1, 1, 1 + c, 0:128, :] = feat_ref[c]
        halo[1, 1, 1 + c, 128:144, :] = aux[c].astype(BF16)

    pl.semaphore_wait(barrier, 30)

    def halo_pair(stage, src_up, dst_up, src_down, dst_down, axis, index, count):
        up = remote(src_up, dst_up, hsend.at[stage, 0], hrecv.at[stage, 0], {axis: lax.rem(index + 1, count)})
        down = remote(
            src_down, dst_down, hsend.at[stage, 1], hrecv.at[stage, 1], {axis: lax.rem(index + count - 1, count)}
        )
        up.start()
        down.start()
        return [up, down]

    own = halo.at[1, 1, pl.ds(1, 2)]
    halo_x = halo_pair(
        0, own, halo.at[1, 0, pl.ds(1, 2)], own, halo.at[1, 2, pl.ds(1, 2)], "gx", gx, 4
    )

    row_i = lax.broadcasted_iota(jnp.int32, (128, 1024), 0)
    lane_i = lax.broadcasted_iota(jnp.int32, (128, 1024), 1)
    rep[...] = (lax.shift_right_logical(lane_i, 3) == row_i).astype(F32).astype(BF16)
    eye = (
        lax.broadcasted_iota(jnp.int32, (128, 128), 0) == lax.broadcasted_iota(jnp.int32, (128, 128), 1)
    ).astype(F32).astype(BF16)
    wch = dot_nn(wch_ref[...], rep[...]).astype(BF16)
    point_rows = lax.broadcasted_iota(jnp.int32, (8, 128), 0).astype(F32)
    point_lanes = lax.bitwise_and(lax.broadcasted_iota(jnp.int32, (128, 128), 1), 7).astype(F32)
    spread = []
    for c in range(2):
        cols[c] = dot_nt(eye, aux[c].astype(BF16))
        col = cols[c]
        wy = stencil(point_rows, aux[c, 8:9, :], aux[c, 5:6, :])
        wz = stencil(point_rows, aux[c, 9:10, :], aux[c, 6:7, :])
        wyz[c] = jnp.concatenate([wz[p : p + 1, :] * wy for p in range(8)], axis=0).astype(BF16)
        wx[c] = stencil(point_lanes, col[:, 7:8], col[:, 4:5])
        wxv = wx[c] * col[:, 3:4]
        charge = dot_nn(feat_ref[c], wch)
        scaled = jnp.concatenate(
            [charge[:, 128 * t : 128 * t + 128] * wxv for t in range(8)], axis=1
        ).astype(BF16)
        spread.append(dot_nn(wyz[c], scaled))
    for t in range(8):
        even, odd = swap_halves(
            spread[0][:, 128 * t : 128 * t + 128], spread[1][:, 128 * t : 128 * t + 128]
        )
        s1[2 * t] = even.astype(BF16)
        s1[2 * t + 1] = odd.astype(BF16)

    def exchange(phase, src, dst, me, device):
        copies = []
        for off in range(1, 16):
            p = lax.rem(me + off, 16)
            copy = remote(src.at[p], dst.at[me], send_sem.at[phase, off], recv_sem.at[phase, off], device(p))
            copy.start()
            copies.append(copy)
        dst[me] = src[me]
        return copies

    phase1 = exchange(0, s1, r1, me_xz, dev_xz)

    weights = []
    for off in range(1, 4):
        p = lax.rem(gx + off, 4)
        copy = remote(wsend_ref.at[p], wrecv.at[gx], wsem.at[off], wrsem.at[off], {"gx": p})
        copy.start()
        weights.append(copy)
    wrecv[gx] = wsend_ref[gx]

    for c in range(2):
        qs[c] = dot_nn(feat_ref[c], wq_ref[...]).astype(BF16)
        pos = aux[c, 0:3, :]
        qx, qy, qz = pos[0:1, :], pos[1:2, :], pos[2:3, :] + float(c)
        norm = split3(qx * qx + qy * qy + qz * qz)
        one = jnp.ones((1, 128), F32)
        rows = jnp.concatenate(
            [-2.0 * pos, -2.0 * pos, one, one, one, *norm, -2.0 * c * one, -2.0 * c * one, 0.0 * one, 0.0 * one],
            axis=0,
        )
        qaug[c] = dot_nt(eye, rows.astype(BF16)).astype(BF16)
        smax[c] = jnp.full((128, 128), -jnp.inf, F32)

    for copy in halo_x:
        copy.wait_recv()
    halo_z = halo_pair(
        1, halo.at[1, :, 2], halo.at[1, :, 0], halo.at[1, :, 1], halo.at[1, :, 3], "gz", gz, 4
    )

    for copy in phase1:
        copy.wait_recv()
    for g in range(4):
        for t in range(2):
            first, second = swap_halves(r1[4 * g + 2 * t].astype(F32), r1[4 * g + 2 * t + 1].astype(F32))
            x1[128 * g : 128 * g + 64, 128 * t : 128 * t + 128] = first.astype(BF16)
            x1[128 * g + 64 : 128 * g + 128, 128 * t : 128 * t + 128] = second.astype(BF16)
    field = dot_nn(x1[...], fx_ref[...]).astype(BF16)
    t2[0:512, :] = field[:, 0:NL]
    t2[512:1024, :] = field[:, NL : 2 * NL]
    s2[...] = dot_nn(fz_ref[...], t2[...]).astype(BF16).reshape(16, 48, NL)
    phase2 = exchange(1, s2, r2, gy, dev_y)

    for copy in halo_z:
        copy.wait_recv()
    halo_y = halo_pair(2, halo.at[1], halo.at[0], halo.at[1], halo.at[2], "gy", gy, 16)

    coef = [coef_ref[k] * LOG2E for k in range(NRBF)]
    scale = LOG2E / math.sqrt(D)

    def score_slab(y, x):
        slab = 3 * y + x
        feats = halo[y, x, :, 0:128, :].reshape(512, 128)
        keys = dot_nn(feats, wk_ref[...]).astype(BF16)
        vext[slab, :, 0:128] = dot_nn(feats, wv_ref[...]).astype(BF16)
        vext[slab, :, 128:256] = jnp.ones((512, 128), BF16)
        off_x = (x - 1).astype(F32) if not isinstance(x, int) else float(x - 1)
        off_y = float(y - 1)
        one = jnp.ones((1, 128), F32)
        masks = []
        for z in range(4):
            rows = halo[y, x, z, 128:144, :].astype(F32)
            pos = rows[0:3, :]
            kx, ky, kz = pos[0:1, :] + off_x, pos[1:2, :] + off_y, pos[2:3, :] + float(z - 1)
            norm = split3(kx * kx + ky * ky + kz * kz)
            kaug[:, 128 * z : 128 * z + 128] = jnp.concatenate(
                [
                    pos, off_x * one, off_y * one, float(z - 1) * one, *norm, one, one, one,
                    pos[2:3, :], float(z - 1) * one, 0.0 * one, 0.0 * one,
                ],
                axis=0,
            ).astype(BF16)
            masks.append(jnp.where(rows[3:4, :] > 0.5, 0.0, -jnp.inf))
        mask = jnp.concatenate(masks, axis=1)
        for c in range(2):
            scores[slab, c] = dot_nt(qs[c], keys[128 * c : 128 * c + 384, :])
            dist[c] = dot_nn(qaug[c], kaug[:, 128 * c : 128 * c + 384])
            for r in range(0, 128, 16):
                t = jnp.exp2(dist[c, r : r + 16, :] * (-0.08 * LOG2E))
                powers = [t]
                for k in range(NRBF - 2):
                    powers.append(powers[-1] * powers[-1])
                bias = coef[NRBF - 1] * powers[-1] + coef[NRBF - 2]
                for k in range(NRBF - 3, -1, -1):
                    bias = bias * powers[k] + coef[k]
                bias = bias * t
                full = scores[slab, c, r : r + 16, :] * scale + bias + mask[:, 128 * c : 128 * c + 384]
                scores[slab, c, r : r + 16, :] = full
                top = jnp.maximum(jnp.maximum(full[:, 0:128], full[:, 128:256]), full[:, 256:384])
                smax[c, r : r + 16, :] = jnp.maximum(smax[c, r : r + 16, :], top)

    def score_row(y):
        lax.fori_loop(0, 3, lambda x, carry: (score_slab(y, x), carry)[1], 0)

    score_row(1)

    for copy in weights:
        copy.wait_recv()
    for q in range(4):
        wf[:, :, q] = wrecv[q].astype(F32).reshape(2, 3, 24, NL) * (1.0 / (MX * MY * MZ))
    for copy in phase2:
        copy.wait_recv()
    for j in range(3):
        spectrum = dot_nn(fy_ref[...], r2[:, 16 * j : 16 * j + 16, :].reshape(256, NL))
        real, imag = spectrum[0:MY, :], spectrum[MY : 2 * MY, :]
        w_real, w_imag = wf[0, j].reshape(MY, NL), wf[1, j].reshape(MY, NL)
        mixed = jnp.concatenate(
            [real * w_real - imag * w_imag, real * w_imag + imag * w_real], axis=0
        ).astype(BF16)
        s3[:, 16 * j : 16 * j + 16, :] = dot_nn(iy_ref[...], mixed).astype(BF16).reshape(16, 16, NL)
    phase3 = exchange(2, s3, r3, gy, dev_y)

    for copy in halo_y:
        copy.wait_recv()
    score_row(0)

    for copy in phase3:
        copy.wait_recv()
    back = dot_nn(iz_ref[...], r3[...].reshape(768, NL)).astype(BF16)
    v2[:, 0:NL] = back[0:512, :]
    v2[:, NL : 2 * NL] = back[512:1024, :]
    potential = dot_nn(v2[...], ix_ref[...])
    for g in range(4):
        for t in range(2):
            even, odd = swap_halves(
                potential[128 * g : 128 * g + 64, 128 * t : 128 * t + 128],
                potential[128 * g + 64 : 128 * g + 128, 128 * t : 128 * t + 128],
            )
            s4[4 * g + 2 * t] = even.astype(BF16)
            s4[4 * g + 2 * t + 1] = odd.astype(BF16)
    phase4 = exchange(3, s4, r4, me_xz, dev_xz)

    score_row(2)
    after = []
    for c in range(2):
        top = jnp.max(smax[c], axis=1, keepdims=True)

        def mix(slab, acc, c=c, top=top):
            probs = jnp.exp2(scores[slab, c] - top).astype(BF16)
            return acc + dot_nn(probs, vext[slab, 128 * c : 128 * c + 384, :])

        acc = lax.fori_loop(0, 9, mix, jnp.zeros((128, 256), F32))
        attended = (acc[:, 0:128] / acc[:, 128:256]).astype(BF16)
        after.append(feat_ref[c].astype(F32) + dot_nn(attended, wo_ref[...]))

    for copy in phase4:
        copy.wait_recv()
    fields = [[], []]
    for t in range(8):
        first, second = swap_halves(r4[2 * t].astype(F32), r4[2 * t + 1].astype(F32))
        fields[0].append(first.astype(BF16))
        fields[1].append(second.astype(BF16))
    for c in range(2):
        lines = dot_tn(wyz[c], jnp.concatenate(fields[c], axis=1))
        lines = jnp.concatenate(
            [lines[:, 128 * t : 128 * t + 128] * wx[c] for t in range(8)], axis=1
        ).astype(BF16)
        sampled = dot_nt(lines, rep[...])
        norm_scale = lax.rsqrt(jnp.mean(sampled * sampled, axis=1, keepdims=True) + 1e-06)
        joined = after[c] + sampled * norm_scale * gain_ref[...]
        inner = dot_nn(joined.astype(BF16), wup_ref[...])
        inner = (inner * jax.nn.sigmoid(inner)).astype(BF16)
        result = joined + dot_nn(inner, wdown_ref[...])
        out_ref[c] = jnp.where(cols[c][:, 3:4] > 0.5, result, 0.0).astype(BF16)

    for copy in phase1 + phase2 + phase3 + phase4 + weights + halo_x + halo_z + halo_y:
        copy.wait_send()


def per_device(
    features,
    frac,
    subpoint,
    counts,
    w_query,
    w_key,
    w_value,
    rbf_coef,
    w_out,
    w_charge,
    mode_weight,
    mesh_gain,
    w_up,
    w_down,
):
    wsend = mode_weight.reshape(2, 24, 3, 4, 192)
    wsend = jnp.pad(jnp.transpose(wsend, (3, 0, 2, 1, 4)), ((0, 0),) * 4 + ((0, NL - 192),))
    wsend = wsend.reshape(4, 144, NL)
    vmem = pl.BlockSpec(memory_space=pltpu.VMEM)
    smem = pl.BlockSpec(memory_space=pltpu.SMEM)
    out = pl.pallas_call(
        kernel,
        out_shape=jax.ShapeDtypeStruct((2, 128, 128), BF16),
        in_specs=[vmem, vmem, vmem, smem, smem] + [vmem] * 15,
        out_specs=vmem,
        scratch_shapes=[
            pltpu.VMEM((3, 3, 4, 144, 128), BF16),
            pltpu.VMEM((16, 64, 128), BF16),
            pltpu.VMEM((16, 64, 128), BF16),
            pltpu.VMEM((16, 48, NL), BF16),
            pltpu.VMEM((16, 48, NL), BF16),
            pltpu.VMEM((16, 48, NL), BF16),
            pltpu.VMEM((16, 48, NL), BF16),
            pltpu.VMEM((16, 64, 128), BF16),
            pltpu.VMEM((16, 64, 128), BF16),
            pltpu.VMEM((4, 144, NL), BF16),
            pltpu.VMEM((2, 3, 4, 24, NL), F32),
            pltpu.VMEM((2, 16, 128), F32),
            pltpu.VMEM((512, 256), BF16),
            pltpu.VMEM((1024, NL), BF16),
            pltpu.VMEM((512, 2 * NL), BF16),
            pltpu.VMEM((2, 64, 128), BF16),
            pltpu.VMEM((2, 128, 128), F32),
            pltpu.VMEM((128, 1024), BF16),
            pltpu.VMEM((2, 128, 16), F32),
            pltpu.VMEM((2, 128, 128), BF16),
            pltpu.VMEM((2, 128, 16), BF16),
            pltpu.VMEM((16, 512), BF16),
            pltpu.VMEM((9, 2, 128, 384), F32),
            pltpu.VMEM((2, 128, 384), F32),
            pltpu.VMEM((9, 512, 256), BF16),
            pltpu.VMEM((2, 128, 128), F32),
            pltpu.SemaphoreType.DMA((4, 16)),
            pltpu.SemaphoreType.DMA((4, 16)),
            pltpu.SemaphoreType.DMA((3, 2)),
            pltpu.SemaphoreType.DMA((3, 2)),
            pltpu.SemaphoreType.DMA((4,)),
            pltpu.SemaphoreType.DMA((4,)),
        ],
        compiler_params=pltpu.CompilerParams(
            collective_id=0, has_side_effects=True, vmem_limit_bytes=48 * 1024 * 1024
        ),
    )(
        features.reshape(2, 128, 128),
        frac.reshape(2, 3, 128),
        subpoint.reshape(2, 3, 128),
        counts.reshape(2),
        rbf_coef,
        w_query,
        w_key,
        w_value,
        w_out,
        w_charge,
        wsend,
        mesh_gain.reshape(1, 128),
        w_up,
        w_down,
        *tables(),
    )
    return out.reshape(features.shape)


def solution(mesh):
    return jax.shard_map(
        per_device,
        mesh=mesh,
        in_specs=(
            P("gx", "gy", "gz", None, None),
            P("gx", "gy", "gz", None, None),
            P("gx", "gy", "gz", None, None),
            P("gx", "gy", "gz"),
            P(),
            P(),
            P(),
            P(),
            P(),
            P(),
            P(None, "gx", "gy", "gz"),
            P(),
            P(),
            P(),
        ),
        out_specs=P("gx", "gy", "gz", None, None),
        check_vma=False,
    )
```

```python
import functools
import math

import jax
import jax.numpy as jnp
import numpy as np
from jax import lax
from jax.experimental import pallas as pl
from jax.experimental.pallas import tpu as pltpu
from jax.sharding import PartitionSpec as P

MESH = pl.DeviceIdType.MESH
F32 = jnp.float32
BF16 = jnp.bfloat16

D = 128
R = 6
NRBF = 8
MX, MY, MZ = 24, 96, 48
NL = 256
LOG2E = math.log2(math.e)


def tables():
    gx, ch, px = np.meshgrid(np.arange(4), np.arange(8), np.arange(8), indexing="ij")
    x_pos, x_ch = (6 * gx + px - 1).reshape(-1), ch.reshape(-1)
    fwd_x, inv_x = [], []
    for first in (0, 64):
        lane = np.arange(NL) - first
        l_ch, l_kx, l_ok = lane // MX, lane % MX, (lane >= 0) & (lane < 8 * MX)
        ang = 2 * np.pi / MX * ((x_pos[:, None] * l_kx[None, :]) % MX)
        same = (x_ch[:, None] == l_ch[None, :]) & l_ok[None, :]
        cos_x, sin_x = np.where(same, np.cos(ang), 0.0), np.where(same, np.sin(ang), 0.0)
        fwd_x.append(np.concatenate([cos_x, -sin_x], axis=1))
        inv_x.append(np.concatenate([cos_x.T, -sin_x.T], axis=0))
    fwd_x, inv_x = np.stack(fwd_x), np.stack(inv_x)

    gz, cell, pz = np.meshgrid(np.arange(4), np.arange(2), np.arange(8), indexing="ij")
    z_pos = (12 * gz + 6 * cell + pz - 1).reshape(-1)
    ang = 2 * np.pi / MZ * ((z_pos[None, :] * np.arange(MZ)[:, None]) % MZ)
    c, s = np.cos(ang), np.sin(ang)
    mat = np.stack([np.stack([c, s], 1), np.stack([-s, c], 1)], axis=1)
    eye = np.eye(8)
    fwd_z = np.einsum("kciz,pq->kcpizq", mat, eye).reshape(MZ * 2 * 8, 2 * 64 * 8)
    mat = np.stack([np.stack([c.T, -s.T], -1), np.stack([s.T, c.T], -1)], axis=0)
    inv_z = np.einsum("czki,pq->czpkiq", mat, eye).reshape(2 * 64 * 8, MZ * 2 * 8)

    gy, py = np.meshgrid(np.arange(16), np.arange(8), indexing="ij")
    y_pos = (6 * gy + py - 1)
    ang = 2 * np.pi / MY * ((y_pos[None] * np.arange(MY)[:, None, None]) % MY)
    c, s = np.cos(ang), np.sin(ang)
    fwd_y = np.stack([np.stack([c, s], 2), np.stack([-s, c], 2)], axis=0)
    fwd_y = fwd_y.reshape(2 * MY, 256)
    ct, st = np.moveaxis(c, 0, -1), np.moveaxis(s, 0, -1)
    inv_y = np.stack([np.stack([ct, -st], 2), np.stack([st, ct], 2)], axis=1)
    inv_y = inv_y.reshape(256, 2 * MY)
    return [jnp.asarray(t, dtype=BF16) for t in (fwd_x, fwd_z, fwd_y, inv_y, inv_z, inv_x)]


def dot_nn(a, b):
    return lax.dot_general(a, b, (((1,), (0,)), ((), ())), preferred_element_type=F32)


def dot_nt(a, b):
    return lax.dot_general(a, b, (((1,), (1,)), ((), ())), preferred_element_type=F32)


def dot_tn(a, b):
    return lax.dot_general(a, b, (((0,), (0,)), ((), ())), preferred_element_type=F32)


def swap_halves(first, second):
    low = lax.broadcasted_iota(jnp.int32, first.shape, 1) < 64
    return (
        jnp.where(low, first, pltpu.roll(second, 64, 1)),
        jnp.where(low, pltpu.roll(first, 64, 1), second),
    )


def stencil(point, sub, frac):
    offset = point - 1.0 - sub
    lower_w = 0.5 * (0.5 - frac) * (0.5 - frac)
    centre_w = 0.75 - frac * frac
    upper_w = 0.5 * (0.5 + frac) * (0.5 + frac)
    zero = jnp.zeros_like(offset)
    return jnp.where(
        offset == -1.0,
        lower_w,
        jnp.where(offset == 0.0, centre_w, jnp.where(offset == 1.0, upper_w, zero)),
    )


def split3(value):
    high = value.astype(BF16).astype(F32)
    rest = value - high
    middle = rest.astype(BF16).astype(F32)
    return high, middle, rest - middle


def kernel(
    feat_hbm,
    frac_ref,
    sub_ref,
    counts_ref,
    coef_ref,
    gain_ref,
    wq_hbm,
    wk_hbm,
    wv_hbm,
    wo_hbm,
    wch_hbm,
    wup_hbm,
    wdown_hbm,
    mode_hbm,
    fx_hbm,
    fz_hbm,
    fy_hbm,
    iy_hbm,
    iz_hbm,
    ix_hbm,
    out_ref,
    feat_ref,
    wq_ref,
    wk_ref,
    wv_ref,
    wo_ref,
    wch_ref,
    wup_ref,
    wdown_ref,
    fx_ref,
    fz_ref,
    fy_ref,
    iy_ref,
    iz_ref,
    ix_ref,
    halo,
    s1,
    r1,
    s2,
    r2,
    s3,
    r3,
    s4,
    r4,
    wrecv,
    wf,
    aux,
    x1,
    t2,
    v2,
    wyz,
    wx,
    rep,
    cols,
    qs,
    qaug,
    kaug,
    scores,
    dist,
    vext,
    smax,
    send_sem,
    recv_sem,
    hsend,
    hrecv,
    wsem,
    wrsem,
    lsem,
):
    gx, gy, gz = lax.axis_index("gx"), lax.axis_index("gy"), lax.axis_index("gz")
    me_xz = gz * 4 + gx

    def dev_xz(p):
        return {"gx": lax.rem(p, 4), "gz": lax.div(p, 4)}

    def dev_y(p):
        return {"gy": p}

    def remote(src, dst, ssem, rsem, device):
        return pltpu.make_async_remote_copy(
            src_ref=src, dst_ref=dst, send_sem=ssem, recv_sem=rsem, device_id=device, device_id_type=MESH
        )

    barrier = pltpu.get_barrier_semaphore()
    for off in range(1, 16):
        pl.semaphore_signal(barrier, inc=1, device_id=dev_xz(lax.rem(me_xz + off, 16)), device_id_type=MESH)
        pl.semaphore_signal(barrier, inc=1, device_id=dev_y(lax.rem(gy + off, 16)), device_id_type=MESH)

    loads = {}

    def load(index, name, src, dst):
        loads[name] = pltpu.make_async_copy(src, dst, lsem.at[index])
        loads[name].start()

    def window(p):
        start = 128 * (lax.div(p, 2) * 3 + lax.rem(p, 2))
        return mode_hbm.at[:, pl.ds(pl.multiple_of(start, 128), NL)]

    parity = lax.rem(gx, 2)
    load(0, "feat", feat_hbm, feat_ref)
    load(1, "wch", wch_hbm, wch_ref)
    load(2, "wq", wq_hbm, wq_ref)
    load(3, "fx", fx_hbm.at[parity], fx_ref)
    load(4, "fz", fz_hbm, fz_ref)
    load(5, "wk", wk_hbm, wk_ref)
    load(6, "wv", wv_hbm, wv_ref)
    load(7, "mode", window(gx), wrecv.at[gx])
    load(8, "fy", fy_hbm, fy_ref)
    load(9, "iy", iy_hbm, iy_ref)
    load(10, "iz", iz_hbm, iz_ref)
    load(11, "ix", ix_hbm.at[parity], ix_ref)
    load(12, "wo", wo_hbm, wo_ref)
    load(13, "wup", wup_hbm, wup_ref)
    load(14, "wdown", wdown_hbm, wdown_ref)

    lane_row = lax.broadcasted_iota(jnp.int32, (1, 128), 1)
    aux[...] = jnp.zeros_like(aux)
    for c in range(2):
        sub = jnp.concatenate([sub_ref[d, c : c + 1, :] for d in range(3)], axis=0).astype(F32)
        frac = jnp.concatenate([frac_ref[d, c : c + 1, :].astype(F32) for d in range(3)], axis=0)
        aux[c, 0:3, :] = ((sub + 0.5 + frac) / R).astype(BF16).astype(F32)
        aux[c, 3:4, :] = (lane_row < counts_ref[c]).astype(F32)
        aux[c, 4:7, :] = frac
        aux[c, 7:10, :] = sub
        halo[1, 1, 1 + c, 128:144, :] = aux[c].astype(BF16)
    loads["feat"].wait()
    for c in range(2):
        halo[1, 1, 1 + c, 0:128, :] = feat_ref[c]

    pl.semaphore_wait(barrier, 30)

    def halo_pair(stage, src_up, dst_up, src_down, dst_down, axis, index, count):
        up = remote(src_up, dst_up, hsend.at[stage, 0], hrecv.at[stage, 0], {axis: lax.rem(index + 1, count)})
        down = remote(
            src_down, dst_down, hsend.at[stage, 1], hrecv.at[stage, 1], {axis: lax.rem(index + count - 1, count)}
        )
        up.start()
        down.start()
        return [up, down]

    own = halo.at[1, 1, pl.ds(1, 2)]
    halo_x = halo_pair(
        0, own, halo.at[1, 0, pl.ds(1, 2)], own, halo.at[1, 2, pl.ds(1, 2)], "gx", gx, 4
    )

    row_i = lax.broadcasted_iota(jnp.int32, (128, 1024), 0)
    lane_i = lax.broadcasted_iota(jnp.int32, (128, 1024), 1)
    rep[...] = (lax.shift_right_logical(lane_i, 3) == row_i).astype(F32).astype(BF16)
    eye = (
        lax.broadcasted_iota(jnp.int32, (128, 128), 0) == lax.broadcasted_iota(jnp.int32, (128, 128), 1)
    ).astype(F32).astype(BF16)
    loads["wch"].wait()
    wch = dot_nn(wch_ref[...], rep[...]).astype(BF16)
    point_rows = lax.broadcasted_iota(jnp.int32, (8, 128), 0).astype(F32)
    point_lanes = lax.bitwise_and(lax.broadcasted_iota(jnp.int32, (128, 128), 1), 7).astype(F32)
    spread = []
    for c in range(2):
        cols[c] = dot_nt(eye, aux[c].astype(BF16))
        col = cols[c]
        wy = stencil(point_rows, aux[c, 8:9, :], aux[c, 5:6, :])
        wz = stencil(point_rows, aux[c, 9:10, :], aux[c, 6:7, :])
        wyz[c] = jnp.concatenate([wz[p : p + 1, :] * wy for p in range(8)], axis=0).astype(BF16)
        wx[c] = stencil(point_lanes, col[:, 7:8], col[:, 4:5])
        wxv = wx[c] * col[:, 3:4]
        charge = dot_nn(feat_ref[c], wch)
        scaled = jnp.concatenate(
            [charge[:, 128 * t : 128 * t + 128] * wxv for t in range(8)], axis=1
        ).astype(BF16)
        spread.append(dot_nn(wyz[c], scaled))
    for t in range(8):
        even, odd = swap_halves(
            spread[0][:, 128 * t : 128 * t + 128], spread[1][:, 128 * t : 128 * t + 128]
        )
        s1[2 * t] = even.astype(BF16)
        s1[2 * t + 1] = odd.astype(BF16)

    def exchange(phase, src, dst, me, device):
        copies = []
        for off in range(1, 16):
            p = lax.rem(me + off, 16)
            copy = remote(src.at[p], dst.at[me], send_sem.at[phase, off], recv_sem.at[phase, off], device(p))
            copy.start()
            copies.append(copy)
        dst[me] = src[me]
        return copies

    phase1 = exchange(0, s1, r1, me_xz, dev_xz)

    weights = []
    for off in range(1, 4):
        p = lax.rem(gx + off, 4)
        copy = remote(window(p), wrecv.at[gx], wsem.at[off], wrsem.at[off], {"gx": p})
        copy.start()
        weights.append(copy)

    loads["wq"].wait()
    for c in range(2):
        qs[c] = dot_nn(feat_ref[c], wq_ref[...]).astype(BF16)
        pos = aux[c, 0:3, :]
        qx, qy, qz = pos[0:1, :], pos[1:2, :], pos[2:3, :] + float(c)
        norm = split3(qx * qx + qy * qy + qz * qz)
        one = jnp.ones((1, 128), F32)
        rows = jnp.concatenate(
            [-2.0 * pos, -2.0 * pos, one, one, one, *norm, -2.0 * c * one, -2.0 * c * one, 0.0 * one, 0.0 * one],
            axis=0,
        )
        qaug[c] = dot_nt(eye, rows.astype(BF16)).astype(BF16)
        smax[c] = jnp.full((128, 128), -jnp.inf, F32)

    for copy in halo_x:
        copy.wait_recv()
    halo_z = halo_pair(
        1, halo.at[1, :, 2], halo.at[1, :, 0], halo.at[1, :, 1], halo.at[1, :, 3], "gz", gz, 4
    )

    for copy in phase1:
        copy.wait_recv()
    for g in range(4):
        for t in range(2):
            first, second = swap_halves(r1[4 * g + 2 * t].astype(F32), r1[4 * g + 2 * t + 1].astype(F32))
            x1[128 * g : 128 * g + 64, 128 * t : 128 * t + 128] = first.astype(BF16)
            x1[128 * g + 64 : 128 * g + 128, 128 * t : 128 * t + 128] = second.astype(BF16)
    loads["fx"].wait()
    loads["fz"].wait()
    field = dot_nn(x1[...], fx_ref[...]).astype(BF16)
    t2[0:512, :] = field[:, 0:NL]
    t2[512:1024, :] = field[:, NL : 2 * NL]
    s2[...] = dot_nn(fz_ref[...], t2[...]).astype(BF16).reshape(16, 48, NL)
    phase2 = exchange(1, s2, r2, gy, dev_y)

    for copy in halo_z:
        copy.wait_recv()
    halo_y = halo_pair(2, halo.at[1], halo.at[0], halo.at[1], halo.at[2], "gy", gy, 16)

    coef = [coef_ref[k] * LOG2E for k in range(NRBF)]
    scale = LOG2E / math.sqrt(D)

    def score_slab(y, x):
        slab = 3 * y + x
        feats = halo[y, x, :, 0:128, :].reshape(512, 128)
        keys = dot_nn(feats, wk_ref[...]).astype(BF16)
        vext[slab, :, 0:128] = dot_nn(feats, wv_ref[...]).astype(BF16)
        vext[slab, :, 128:256] = jnp.ones((512, 128), BF16)
        off_x = (x - 1).astype(F32) if not isinstance(x, int) else float(x - 1)
        off_y = float(y - 1)
        one = jnp.ones((1, 128), F32)
        masks = []
        for z in range(4):
            rows = halo[y, x, z, 128:144, :].astype(F32)
            pos = rows[0:3, :]
            kx, ky, kz = pos[0:1, :] + off_x, pos[1:2, :] + off_y, pos[2:3, :] + float(z - 1)
            norm = split3(kx * kx + ky * ky + kz * kz)
            kaug[:, 128 * z : 128 * z + 128] = jnp.concatenate(
                [
                    pos, off_x * one, off_y * one, float(z - 1) * one, *norm, one, one, one,
                    pos[2:3, :], float(z - 1) * one, 0.0 * one, 0.0 * one,
                ],
                axis=0,
            ).astype(BF16)
            masks.append(jnp.where(rows[3:4, :] > 0.5, 0.0, -jnp.inf))
        mask = jnp.concatenate(masks, axis=1)
        for c in range(2):
            scores[slab, c] = dot_nt(qs[c], keys[128 * c : 128 * c + 384, :])
            dist[c] = dot_nn(qaug[c], kaug[:, 128 * c : 128 * c + 384])
            for r in range(0, 128, 16):
                t = jnp.exp2(dist[c, r : r + 16, :] * (-0.08 * LOG2E))
                powers = [t]
                for k in range(NRBF - 2):
                    powers.append(powers[-1] * powers[-1])
                bias = coef[NRBF - 1] * powers[-1] + coef[NRBF - 2]
                for k in range(NRBF - 3, -1, -1):
                    bias = bias * powers[k] + coef[k]
                bias = bias * t
                full = scores[slab, c, r : r + 16, :] * scale + bias + mask[:, 128 * c : 128 * c + 384]
                scores[slab, c, r : r + 16, :] = full
                top = jnp.maximum(jnp.maximum(full[:, 0:128], full[:, 128:256]), full[:, 256:384])
                smax[c, r : r + 16, :] = jnp.maximum(smax[c, r : r + 16, :], top)

    def score_row(y):
        lax.fori_loop(0, 3, lambda x, carry: (score_slab(y, x), carry)[1], 0)

    loads["wk"].wait()
    loads["wv"].wait()
    score_row(1)

    for copy in weights:
        copy.wait_recv()
    for name in ("mode", "fy", "iy"):
        loads[name].wait()
    for q in range(4):
        wf[:, :, q] = wrecv[q].astype(F32).reshape(2, 3, 24, NL) * (1.0 / (MX * MY * MZ))
    for copy in phase2:
        copy.wait_recv()
    for j in range(3):
        spectrum = dot_nn(fy_ref[...], r2[:, 16 * j : 16 * j + 16, :].reshape(256, NL))
        real, imag = spectrum[0:MY, :], spectrum[MY : 2 * MY, :]
        w_real, w_imag = wf[0, j].reshape(MY, NL), wf[1, j].reshape(MY, NL)
        mixed = jnp.concatenate(
            [real * w_real - imag * w_imag, real * w_imag + imag * w_real], axis=0
        ).astype(BF16)
        s3[:, 16 * j : 16 * j + 16, :] = dot_nn(iy_ref[...], mixed).astype(BF16).reshape(16, 16, NL)
    phase3 = exchange(2, s3, r3, gy, dev_y)

    for copy in halo_y:
        copy.wait_recv()
    score_row(0)

    for copy in phase3:
        copy.wait_recv()
    loads["iz"].wait()
    loads["ix"].wait()
    back = dot_nn(iz_ref[...], r3[...].reshape(768, NL)).astype(BF16)
    v2[:, 0:NL] = back[0:512, :]
    v2[:, NL : 2 * NL] = back[512:1024, :]
    potential = dot_nn(v2[...], ix_ref[...])
    for g in range(4):
        for t in range(2):
            even, odd = swap_halves(
                potential[128 * g : 128 * g + 64, 128 * t : 128 * t + 128],
                potential[128 * g + 64 : 128 * g + 128, 128 * t : 128 * t + 128],
            )
            s4[4 * g + 2 * t] = even.astype(BF16)
            s4[4 * g + 2 * t + 1] = odd.astype(BF16)
    phase4 = exchange(3, s4, r4, me_xz, dev_xz)

    score_row(2)
    after = []
    for name in ("wo", "wup", "wdown"):
        loads[name].wait()
    for c in range(2):
        top = jnp.max(smax[c], axis=1, keepdims=True)

        def mix(slab, acc, c=c, top=top):
            probs = jnp.exp2(scores[slab, c] - top).astype(BF16)
            return acc + dot_nn(probs, vext[slab, 128 * c : 128 * c + 384, :])

        acc = lax.fori_loop(0, 9, mix, jnp.zeros((128, 256), F32))
        attended = (acc[:, 0:128] / acc[:, 128:256]).astype(BF16)
        after.append(feat_ref[c].astype(F32) + dot_nn(attended, wo_ref[...]))

    for copy in phase4:
        copy.wait_recv()
    fields = [[], []]
    for t in range(8):
        first, second = swap_halves(r4[2 * t].astype(F32), r4[2 * t + 1].astype(F32))
        fields[0].append(first.astype(BF16))
        fields[1].append(second.astype(BF16))
    for c in range(2):
        lines = dot_tn(wyz[c], jnp.concatenate(fields[c], axis=1))
        lines = jnp.concatenate(
            [lines[:, 128 * t : 128 * t + 128] * wx[c] for t in range(8)], axis=1
        ).astype(BF16)
        sampled = dot_nt(lines, rep[...])
        norm_scale = lax.rsqrt(jnp.mean(sampled * sampled, axis=1, keepdims=True) + 1e-06)
        joined = after[c] + sampled * norm_scale * gain_ref[...]
        inner = dot_nn(joined.astype(BF16), wup_ref[...])
        inner = (inner * jax.nn.sigmoid(inner)).astype(BF16)
        result = joined + dot_nn(inner, wdown_ref[...])
        out_ref[c] = jnp.where(cols[c][:, 3:4] > 0.5, result, 0.0).astype(BF16)

    for copy in phase1 + phase2 + phase3 + phase4 + weights + halo_x + halo_z + halo_y:
        copy.wait_send()


def per_device(
    features,
    frac,
    subpoint,
    counts,
    w_query,
    w_key,
    w_value,
    rbf_coef,
    w_out,
    w_charge,
    mode_weight,
    mesh_gain,
    w_up,
    w_down,
):
    mode_rows = jnp.transpose(mode_weight, (0, 2, 1, 3)).reshape(144, 768)
    vmem = pl.BlockSpec(memory_space=pltpu.VMEM)
    smem = pl.BlockSpec(memory_space=pltpu.SMEM)
    hbm = pl.BlockSpec(memory_space=pltpu.HBM)
    out = pl.pallas_call(
        kernel,
        out_shape=jax.ShapeDtypeStruct((2, 128, 128), BF16),
        in_specs=[hbm, vmem, vmem, smem, smem, vmem] + [hbm] * 14,
        out_specs=vmem,
        scratch_shapes=[
            pltpu.VMEM((2, 128, 128), BF16),
            pltpu.VMEM((128, 128), BF16),
            pltpu.VMEM((128, 128), BF16),
            pltpu.VMEM((128, 128), BF16),
            pltpu.VMEM((128, 128), BF16),
            pltpu.VMEM((128, 128), BF16),
            pltpu.VMEM((128, 256), BF16),
            pltpu.VMEM((256, 128), BF16),
            pltpu.VMEM((256, 2 * NL), BF16),
            pltpu.VMEM((768, 1024), BF16),
            pltpu.VMEM((192, 256), BF16),
            pltpu.VMEM((256, 192), BF16),
            pltpu.VMEM((1024, 768), BF16),
            pltpu.VMEM((2 * NL, 256), BF16),
            pltpu.VMEM((3, 3, 4, 144, 128), BF16),
            pltpu.VMEM((16, 64, 128), BF16),
            pltpu.VMEM((16, 64, 128), BF16),
            pltpu.VMEM((16, 48, NL), BF16),
            pltpu.VMEM((16, 48, NL), BF16),
            pltpu.VMEM((16, 48, NL), BF16),
            pltpu.VMEM((16, 48, NL), BF16),
            pltpu.VMEM((16, 64, 128), BF16),
            pltpu.VMEM((16, 64, 128), BF16),
            pltpu.VMEM((4, 144, NL), BF16),
            pltpu.VMEM((2, 3, 4, 24, NL), F32),
            pltpu.VMEM((2, 16, 128), F32),
            pltpu.VMEM((512, 256), BF16),
            pltpu.VMEM((1024, NL), BF16),
            pltpu.VMEM((512, 2 * NL), BF16),
            pltpu.VMEM((2, 64, 128), BF16),
            pltpu.VMEM((2, 128, 128), F32),
            pltpu.VMEM((128, 1024), BF16),
            pltpu.VMEM((2, 128, 16), F32),
            pltpu.VMEM((2, 128, 128), BF16),
            pltpu.VMEM((2, 128, 16), BF16),
            pltpu.VMEM((16, 512), BF16),
            pltpu.VMEM((9, 2, 128, 384), F32),
            pltpu.VMEM((2, 128, 384), F32),
            pltpu.VMEM((9, 512, 256), BF16),
            pltpu.VMEM((2, 128, 128), F32),
            pltpu.SemaphoreType.DMA((4, 16)),
            pltpu.SemaphoreType.DMA((4, 16)),
            pltpu.SemaphoreType.DMA((3, 2)),
            pltpu.SemaphoreType.DMA((3, 2)),
            pltpu.SemaphoreType.DMA((4,)),
            pltpu.SemaphoreType.DMA((4,)),
            pltpu.SemaphoreType.DMA((15,)),
        ],
        compiler_params=pltpu.CompilerParams(
            collective_id=0, has_side_effects=True, vmem_limit_bytes=63 * 1024 * 1024
        ),
    )(
        features.reshape(2, 128, 128),
        jnp.transpose(frac.reshape(2, 3, 128), (1, 0, 2)),
        jnp.transpose(subpoint.reshape(2, 3, 128), (1, 0, 2)),
        counts.reshape(2),
        rbf_coef,
        mesh_gain.reshape(1, 128),
        w_query,
        w_key,
        w_value,
        w_out,
        w_charge,
        w_up,
        w_down,
        mode_rows,
        *tables(),
    )
    return out.reshape(features.shape)


def solution(mesh):
    return jax.shard_map(
        per_device,
        mesh=mesh,
        in_specs=(
            P("gx", "gy", "gz", None, None),
            P("gx", "gy", "gz", None, None),
            P("gx", "gy", "gz", None, None),
            P("gx", "gy", "gz"),
            P(),
            P(),
            P(),
            P(),
            P(),
            P(),
            P(None, "gx", "gy", "gz"),
            P(),
            P(),
            P(),
        ),
        out_specs=P("gx", "gy", "gz", None, None),
        check_vma=False,
    )
```

```python
import functools
import math

import jax
import jax.numpy as jnp
import numpy as np
from jax import lax
from jax.experimental import pallas as pl
from jax.experimental.pallas import tpu as pltpu
from jax.sharding import PartitionSpec as P

MESH = pl.DeviceIdType.MESH
F32 = jnp.float32
BF16 = jnp.bfloat16

D = 128
R = 6
NRBF = 8
MX, MY, MZ = 24, 96, 48
NL = 256
LOG2E = math.log2(math.e)


def tables():
    gx, ch, px = np.meshgrid(np.arange(4), np.arange(8), np.arange(8), indexing="ij")
    x_pos, x_ch = (6 * gx + px - 1).reshape(-1), ch.reshape(-1)
    fwd_x, inv_x = [], []
    for first in (0, 64):
        lane = np.arange(NL) - first
        l_ch, l_kx, l_ok = lane // MX, lane % MX, (lane >= 0) & (lane < 8 * MX)
        ang = 2 * np.pi / MX * ((x_pos[:, None] * l_kx[None, :]) % MX)
        same = (x_ch[:, None] == l_ch[None, :]) & l_ok[None, :]
        cos_x, sin_x = np.where(same, np.cos(ang), 0.0), np.where(same, np.sin(ang), 0.0)
        fwd_x.append(np.concatenate([cos_x, -sin_x], axis=1))
        inv_x.append(np.concatenate([cos_x.T, -sin_x.T], axis=0))
    fwd_x, inv_x = np.stack(fwd_x), np.stack(inv_x)

    gz, cell, pz = np.meshgrid(np.arange(4), np.arange(2), np.arange(8), indexing="ij")
    z_pos = (12 * gz + 6 * cell + pz - 1).reshape(-1)
    ang = 2 * np.pi / MZ * ((z_pos[None, :] * np.arange(MZ)[:, None]) % MZ)
    c, s = np.cos(ang), np.sin(ang)
    mat = np.stack([np.stack([c, s], 1), np.stack([-s, c], 1)], axis=1)
    eye = np.eye(8)
    fwd_z = np.einsum("kciz,pq->kcpizq", mat, eye).reshape(MZ * 2 * 8, 2 * 64 * 8)
    mat = np.stack([np.stack([c.T, -s.T], -1), np.stack([s.T, c.T], -1)], axis=0)
    inv_z = np.einsum("czki,pq->czpkiq", mat, eye).reshape(2 * 64 * 8, MZ * 2 * 8)

    gy, py = np.meshgrid(np.arange(16), np.arange(8), indexing="ij")
    y_pos = (6 * gy + py - 1)
    ang = 2 * np.pi / MY * ((y_pos[None] * np.arange(MY)[:, None, None]) % MY)
    c, s = np.cos(ang), np.sin(ang)
    fwd_y = np.stack([np.stack([c, s], 2), np.stack([-s, c], 2)], axis=0)
    fwd_y = fwd_y.reshape(2 * MY, 256)
    ct, st = np.moveaxis(c, 0, -1), np.moveaxis(s, 0, -1)
    inv_y = np.stack([np.stack([ct, -st], 2), np.stack([st, ct], 2)], axis=1)
    inv_y = inv_y.reshape(256, 2 * MY)
    return [jnp.asarray(t, dtype=BF16) for t in (fwd_x, fwd_z, fwd_y, inv_y, inv_z, inv_x)]


def dot_nn(a, b):
    return lax.dot_general(a, b, (((1,), (0,)), ((), ())), preferred_element_type=F32)


def dot_nt(a, b):
    return lax.dot_general(a, b, (((1,), (1,)), ((), ())), preferred_element_type=F32)


def dot_tn(a, b):
    return lax.dot_general(a, b, (((0,), (0,)), ((), ())), preferred_element_type=F32)


def swap_halves(first, second):
    low = lax.broadcasted_iota(jnp.int32, first.shape, 1) < 64
    return (
        jnp.where(low, first, pltpu.roll(second, 64, 1)),
        jnp.where(low, pltpu.roll(first, 64, 1), second),
    )


def stencil(point, sub, frac):
    offset = point - 1.0 - sub
    lower_w = 0.5 * (0.5 - frac) * (0.5 - frac)
    centre_w = 0.75 - frac * frac
    upper_w = 0.5 * (0.5 + frac) * (0.5 + frac)
    zero = jnp.zeros_like(offset)
    return jnp.where(
        offset == -1.0,
        lower_w,
        jnp.where(offset == 0.0, centre_w, jnp.where(offset == 1.0, upper_w, zero)),
    )


def split3(value):
    high = value.astype(BF16).astype(F32)
    rest = value - high
    middle = rest.astype(BF16).astype(F32)
    return high, middle, rest - middle


def kernel(
    feat_hbm,
    frac_ref,
    sub_ref,
    counts_ref,
    coef_ref,
    gain_ref,
    wq_hbm,
    wk_hbm,
    wv_hbm,
    wo_hbm,
    wch_hbm,
    wup_hbm,
    wdown_hbm,
    mode_hbm,
    fx_hbm,
    fz_hbm,
    fy_hbm,
    iy_hbm,
    iz_hbm,
    ix_hbm,
    out_ref,
    feat_ref,
    wq_ref,
    wk_ref,
    wv_ref,
    wo_ref,
    wch_ref,
    wup_ref,
    wdown_ref,
    fx_ref,
    fz_ref,
    fy_ref,
    iy_ref,
    iz_ref,
    ix_ref,
    halo,
    s1,
    r1,
    s2,
    r2,
    s3,
    r3,
    s4,
    r4,
    wrecv,
    wf,
    aux,
    x1,
    t2,
    v2,
    wyz,
    wx,
    rep,
    cols,
    qs,
    qaug,
    kaug,
    scores,
    dist,
    vext,
    smax,
    send_sem,
    recv_sem,
    hsend,
    hrecv,
    wsem,
    wrsem,
    lsem,
):
    gx, gy, gz = lax.axis_index("gx"), lax.axis_index("gy"), lax.axis_index("gz")
    me_xz = gz * 4 + gx

    def dev_xz(p):
        return {"gx": lax.rem(p, 4), "gz": lax.div(p, 4)}

    def dev_y(p):
        return {"gy": p}

    def remote(src, dst, ssem, rsem, device):
        return pltpu.make_async_remote_copy(
            src_ref=src, dst_ref=dst, send_sem=ssem, recv_sem=rsem, device_id=device, device_id_type=MESH
        )

    barrier = pltpu.get_barrier_semaphore()
    for off in range(1, 16):
        pl.semaphore_signal(barrier, inc=1, device_id=dev_xz(lax.rem(me_xz + off, 16)), device_id_type=MESH)
        pl.semaphore_signal(barrier, inc=1, device_id=dev_y(lax.rem(gy + off, 16)), device_id_type=MESH)

    loads = {}

    def load(index, name, src, dst):
        loads[name] = pltpu.make_async_copy(src, dst, lsem.at[index])
        loads[name].start()

    def window(p):
        start = 128 * (lax.div(p, 2) * 3 + lax.rem(p, 2))
        return mode_hbm.at[:, pl.ds(pl.multiple_of(start, 128), NL)]

    parity = lax.rem(gx, 2)
    load(0, "feat", feat_hbm, feat_ref)
    load(1, "wch", wch_hbm, wch_ref)
    load(2, "wq", wq_hbm, wq_ref)
    load(3, "fx", fx_hbm.at[parity], fx_ref)
    load(4, "fz", fz_hbm, fz_ref)
    load(5, "wk", wk_hbm, wk_ref)
    load(6, "wv", wv_hbm, wv_ref)
    load(7, "mode", window(gx), wrecv.at[gx])
    load(8, "fy", fy_hbm, fy_ref)
    load(9, "iy", iy_hbm, iy_ref)
    load(10, "iz", iz_hbm, iz_ref)
    load(11, "ix", ix_hbm.at[parity], ix_ref)
    load(12, "wo", wo_hbm, wo_ref)
    load(13, "wup", wup_hbm, wup_ref)
    load(14, "wdown", wdown_hbm, wdown_ref)

    mine = lax.div(gx, 2)
    lane_row = lax.broadcasted_iota(jnp.int32, (1, 128), 1)
    aux[...] = jnp.zeros_like(aux)
    for c in range(2):
        sub = jnp.concatenate([sub_ref[d, c : c + 1, :] for d in range(3)], axis=0).astype(F32)
        frac = jnp.concatenate([frac_ref[d, c : c + 1, :].astype(F32) for d in range(3)], axis=0)
        aux[c, 0:3, :] = ((sub + 0.5 + frac) / R).astype(BF16).astype(F32)
        aux[c, 3:4, :] = (lane_row < counts_ref[c]).astype(F32)
        aux[c, 4:7, :] = frac
        aux[c, 7:10, :] = sub
        halo[1, mine, 1 + c, 128:144, :] = aux[c].astype(BF16)
    loads["feat"].wait()
    for c in range(2):
        halo[1, mine, 1 + c, 0:128, :] = feat_ref[c]

    row_i = lax.broadcasted_iota(jnp.int32, (128, 1024), 0)
    lane_i = lax.broadcasted_iota(jnp.int32, (128, 1024), 1)
    rep[...] = (lax.shift_right_logical(lane_i, 3) == row_i).astype(F32).astype(BF16)
    eye = (
        lax.broadcasted_iota(jnp.int32, (128, 128), 0) == lax.broadcasted_iota(jnp.int32, (128, 128), 1)
    ).astype(F32).astype(BF16)
    loads["wch"].wait()
    wch = dot_nn(wch_ref[...], rep[...]).astype(BF16)
    point_rows = lax.broadcasted_iota(jnp.int32, (8, 128), 0).astype(F32)
    point_lanes = lax.bitwise_and(lax.broadcasted_iota(jnp.int32, (128, 128), 1), 7).astype(F32)
    spread = []
    for c in range(2):
        cols[c] = dot_nt(eye, aux[c].astype(BF16))
        col = cols[c]
        wy = stencil(point_rows, aux[c, 8:9, :], aux[c, 5:6, :])
        wz = stencil(point_rows, aux[c, 9:10, :], aux[c, 6:7, :])
        wyz[c] = jnp.concatenate([wz[p : p + 1, :] * wy for p in range(8)], axis=0).astype(BF16)
        wx[c] = stencil(point_lanes, col[:, 7:8], col[:, 4:5])
        wxv = wx[c] * col[:, 3:4]
        charge = dot_nn(feat_ref[c], wch)
        scaled = jnp.concatenate(
            [charge[:, 128 * t : 128 * t + 128] * wxv for t in range(8)], axis=1
        ).astype(BF16)
        spread.append(dot_nn(wyz[c], scaled))
    for t in range(8):
        even, odd = swap_halves(
            spread[0][:, 128 * t : 128 * t + 128], spread[1][:, 128 * t : 128 * t + 128]
        )
        s1[2 * t] = even.astype(BF16)
        s1[2 * t + 1] = odd.astype(BF16)

    def exchange(phase, src, dst, me, device):
        copies = []
        for off in range(1, 16):
            p = lax.rem(me + off, 16)
            copy = remote(src.at[p], dst.at[me], send_sem.at[phase, off], recv_sem.at[phase, off], device(p))
            copy.start()
            copies.append(copy)
        dst[me] = src[me]
        return copies

    pl.semaphore_wait(barrier, 30)
    phase1 = exchange(0, s1, r1, me_xz, dev_xz)

    halo_copies = []

    def halo_send(index, src, dst, device):
        copy = remote(src, dst, hsend.at[index], hrecv.at[index], device)
        copy.start()
        halo_copies.append(copy)
        return copy

    far = 3 - gx
    own = halo.at[1, mine, pl.ds(1, 2)]
    halo_far = halo_send(0, own, own, {"gx": far})

    loads["wq"].wait()
    for c in range(2):
        qs[c] = dot_nn(feat_ref[c], wq_ref[...]).astype(BF16)
        pos = aux[c, 0:3, :]
        qx, qy, qz = pos[0:1, :], pos[1:2, :], pos[2:3, :] + float(c)
        norm = split3(qx * qx + qy * qy + qz * qz)
        one = jnp.ones((1, 128), F32)
        rows = jnp.concatenate(
            [-2.0 * pos, -2.0 * pos, one, one, one, *norm, -2.0 * c * one, -2.0 * c * one, 0.0 * one, 0.0 * one],
            axis=0,
        )
        qaug[c] = dot_nt(eye, rows.astype(BF16)).astype(BF16)
        smax[c] = jnp.full((128, 128), -jnp.inf, F32)

    halo_far.wait_recv()
    wrap_up, wrap_down = lax.div(gz + 1, 4), lax.div(4 - gz, 4)
    dev_up = {"gx": gx + wrap_up * (far - gx), "gz": lax.rem(gz + 1, 4)}
    dev_down = {"gx": gx + wrap_down * (far - gx), "gz": lax.rem(gz + 3, 4)}
    pair = pl.ds(0, 2)
    halo_z = [
        halo_send(1, halo.at[1, pair, 2], halo.at[1, pair, 0], dev_up),
        halo_send(2, halo.at[1, pair, 1], halo.at[1, pair, 3], dev_down),
    ]

    weights = []
    for off in range(1, 4):
        p = lax.rem(gx + off, 4)
        copy = remote(window(p), wrecv.at[gx], wsem.at[off], wrsem.at[off], {"gx": p})
        copy.start()
        weights.append(copy)

    for copy in phase1:
        copy.wait_recv()
    for g in range(4):
        for t in range(2):
            first, second = swap_halves(r1[4 * g + 2 * t].astype(F32), r1[4 * g + 2 * t + 1].astype(F32))
            x1[128 * g : 128 * g + 64, 128 * t : 128 * t + 128] = first.astype(BF16)
            x1[128 * g + 64 : 128 * g + 128, 128 * t : 128 * t + 128] = second.astype(BF16)
    loads["fx"].wait()
    loads["fz"].wait()
    field = dot_nn(x1[...], fx_ref[...]).astype(BF16)
    t2[0:512, :] = field[:, 0:NL]
    t2[512:1024, :] = field[:, NL : 2 * NL]
    s2[...] = dot_nn(fz_ref[...], t2[...]).astype(BF16).reshape(16, 48, NL)
    phase2 = exchange(1, s2, r2, gy, dev_y)

    for copy in halo_z:
        copy.wait_recv()
    both = halo.at[1, pair]
    halo_y = [
        halo_send(3, both, halo.at[0, pair], dev_y(lax.rem(gy + 1, 16))),
        halo_send(4, both, halo.at[2, pair], dev_y(lax.rem(gy + 15, 16))),
    ]
    odd_core = lax.rem(gx, 2)
    dev_near = {"gx": gx + 1 - 2 * odd_core}
    halo_near = [halo_send(5, halo.at[1, mine], halo.at[1, 2], dev_near)]
    near_step = (1 - 2 * odd_core).astype(F32)

    coef = [coef_ref[k] * LOG2E for k in range(NRBF)]
    scale = LOG2E / math.sqrt(D)

    def score_slab(y, x):
        slab = 3 * y + x
        feats = halo[y, x, :, 0:128, :].reshape(512, 128)
        keys = dot_nn(feats, wk_ref[...]).astype(BF16)
        vext[slab, :, 0:128] = dot_nn(feats, wv_ref[...]).astype(BF16)
        vext[slab, :, 128:256] = jnp.ones((512, 128), BF16)
        off_x = near_step if isinstance(x, int) else jnp.where(x == mine, 0.0, -near_step)
        off_y = float(y - 1)
        one = jnp.ones((1, 128), F32)
        masks = []
        for z in range(4):
            rows = halo[y, x, z, 128:144, :].astype(F32)
            pos = rows[0:3, :]
            kx, ky, kz = pos[0:1, :] + off_x, pos[1:2, :] + off_y, pos[2:3, :] + float(z - 1)
            norm = split3(kx * kx + ky * ky + kz * kz)
            kaug[:, 128 * z : 128 * z + 128] = jnp.concatenate(
                [
                    pos, off_x * one, off_y * one, float(z - 1) * one, *norm, one, one, one,
                    pos[2:3, :], float(z - 1) * one, 0.0 * one, 0.0 * one,
                ],
                axis=0,
            ).astype(BF16)
            masks.append(jnp.where(rows[3:4, :] > 0.5, 0.0, -jnp.inf))
        mask = jnp.concatenate(masks, axis=1)
        for c in range(2):
            scores[slab, c] = dot_nt(qs[c], keys[128 * c : 128 * c + 384, :])
            dist[c] = dot_nn(qaug[c], kaug[:, 128 * c : 128 * c + 384])
            for r in range(0, 128, 16):
                t = jnp.exp2(dist[c, r : r + 16, :] * (-0.08 * LOG2E))
                powers = [t]
                for k in range(NRBF - 2):
                    powers.append(powers[-1] * powers[-1])
                bias = coef[NRBF - 1] * powers[-1] + coef[NRBF - 2]
                for k in range(NRBF - 3, -1, -1):
                    bias = bias * powers[k] + coef[k]
                bias = bias * t
                full = scores[slab, c, r : r + 16, :] * scale + bias + mask[:, 128 * c : 128 * c + 384]
                scores[slab, c, r : r + 16, :] = full
                top = jnp.maximum(jnp.maximum(full[:, 0:128], full[:, 128:256]), full[:, 256:384])
                smax[c, r : r + 16, :] = jnp.maximum(smax[c, r : r + 16, :], top)

    def score_pair(y):
        lax.fori_loop(0, 2, lambda x, carry: (score_slab(y, x), carry)[1], 0)

    loads["wk"].wait()
    loads["wv"].wait()
    score_pair(1)

    for copy in weights:
        copy.wait_recv()
    for name in ("mode", "fy", "iy"):
        loads[name].wait()
    for q in range(4):
        wf[:, :, q] = wrecv[q].astype(F32).reshape(2, 3, 24, NL) * (1.0 / (MX * MY * MZ))
    for copy in phase2:
        copy.wait_recv()
    for j in range(3):
        spectrum = dot_nn(fy_ref[...], r2[:, 16 * j : 16 * j + 16, :].reshape(256, NL))
        real, imag = spectrum[0:MY, :], spectrum[MY : 2 * MY, :]
        w_real, w_imag = wf[0, j].reshape(MY, NL), wf[1, j].reshape(MY, NL)
        mixed = jnp.concatenate(
            [real * w_real - imag * w_imag, real * w_imag + imag * w_real], axis=0
        ).astype(BF16)
        s3[:, 16 * j : 16 * j + 16, :] = dot_nn(iy_ref[...], mixed).astype(BF16).reshape(16, 16, NL)
    phase3 = exchange(2, s3, r3, gy, dev_y)

    for copy in halo_y:
        copy.wait_recv()
    halo_near.append(halo_send(6, halo.at[0, mine], halo.at[0, 2], dev_near))
    halo_near.append(halo_send(7, halo.at[2, mine], halo.at[2, 2], dev_near))
    score_pair(0)
    score_pair(2)

    for copy in phase3:
        copy.wait_recv()
    loads["iz"].wait()
    loads["ix"].wait()
    back = dot_nn(iz_ref[...], r3[...].reshape(768, NL)).astype(BF16)
    v2[:, 0:NL] = back[0:512, :]
    v2[:, NL : 2 * NL] = back[512:1024, :]
    potential = dot_nn(v2[...], ix_ref[...])
    for g in range(4):
        for t in range(2):
            even, odd = swap_halves(
                potential[128 * g : 128 * g + 64, 128 * t : 128 * t + 128],
                potential[128 * g + 64 : 128 * g + 128, 128 * t : 128 * t + 128],
            )
            s4[4 * g + 2 * t] = even.astype(BF16)
            s4[4 * g + 2 * t + 1] = odd.astype(BF16)
    phase4 = exchange(3, s4, r4, me_xz, dev_xz)

    for y, copy in zip((1, 0, 2), halo_near):
        copy.wait_recv()
        score_slab(y, 2)
    after = []
    for name in ("wo", "wup", "wdown"):
        loads[name].wait()
    for c in range(2):
        top = jnp.max(smax[c], axis=1, keepdims=True)

        def mix(slab, acc, c=c, top=top):
            probs = jnp.exp2(scores[slab, c] - top).astype(BF16)
            return acc + dot_nn(probs, vext[slab, 128 * c : 128 * c + 384, :])

        acc = lax.fori_loop(0, 9, mix, jnp.zeros((128, 256), F32))
        attended = (acc[:, 0:128] / acc[:, 128:256]).astype(BF16)
        after.append(feat_ref[c].astype(F32) + dot_nn(attended, wo_ref[...]))

    for copy in phase4:
        copy.wait_recv()
    fields = [[], []]
    for t in range(8):
        first, second = swap_halves(r4[2 * t].astype(F32), r4[2 * t + 1].astype(F32))
        fields[0].append(first.astype(BF16))
        fields[1].append(second.astype(BF16))
    for c in range(2):
        lines = dot_tn(wyz[c], jnp.concatenate(fields[c], axis=1))
        lines = jnp.concatenate(
            [lines[:, 128 * t : 128 * t + 128] * wx[c] for t in range(8)], axis=1
        ).astype(BF16)
        sampled = dot_nt(lines, rep[...])
        norm_scale = lax.rsqrt(jnp.mean(sampled * sampled, axis=1, keepdims=True) + 1e-06)
        joined = after[c] + sampled * norm_scale * gain_ref[...]
        inner = dot_nn(joined.astype(BF16), wup_ref[...])
        inner = (inner * jax.nn.sigmoid(inner)).astype(BF16)
        result = joined + dot_nn(inner, wdown_ref[...])
        out_ref[c] = jnp.where(cols[c][:, 3:4] > 0.5, result, 0.0).astype(BF16)

    for copy in phase1 + phase2 + phase3 + phase4 + weights + halo_copies:
        copy.wait_send()


def per_device(
    features,
    frac,
    subpoint,
    counts,
    w_query,
    w_key,
    w_value,
    rbf_coef,
    w_out,
    w_charge,
    mode_weight,
    mesh_gain,
    w_up,
    w_down,
):
    mode_rows = jnp.transpose(mode_weight, (0, 2, 1, 3)).reshape(144, 768)
    vmem = pl.BlockSpec(memory_space=pltpu.VMEM)
    smem = pl.BlockSpec(memory_space=pltpu.SMEM)
    hbm = pl.BlockSpec(memory_space=pltpu.HBM)
    out = pl.pallas_call(
        kernel,
        out_shape=jax.ShapeDtypeStruct((2, 128, 128), BF16),
        in_specs=[hbm, vmem, vmem, smem, smem, vmem] + [hbm] * 14,
        out_specs=vmem,
        scratch_shapes=[
            pltpu.VMEM((2, 128, 128), BF16),
            pltpu.VMEM((128, 128), BF16),
            pltpu.VMEM((128, 128), BF16),
            pltpu.VMEM((128, 128), BF16),
            pltpu.VMEM((128, 128), BF16),
            pltpu.VMEM((128, 128), BF16),
            pltpu.VMEM((128, 256), BF16),
            pltpu.VMEM((256, 128), BF16),
            pltpu.VMEM((256, 2 * NL), BF16),
            pltpu.VMEM((768, 1024), BF16),
            pltpu.VMEM((192, 256), BF16),
            pltpu.VMEM((256, 192), BF16),
            pltpu.VMEM((1024, 768), BF16),
            pltpu.VMEM((2 * NL, 256), BF16),
            pltpu.VMEM((3, 3, 4, 144, 128), BF16),
            pltpu.VMEM((16, 64, 128), BF16),
            pltpu.VMEM((16, 64, 128), BF16),
            pltpu.VMEM((16, 48, NL), BF16),
            pltpu.VMEM((16, 48, NL), BF16),
            pltpu.VMEM((16, 48, NL), BF16),
            pltpu.VMEM((16, 48, NL), BF16),
            pltpu.VMEM((16, 64, 128), BF16),
            pltpu.VMEM((16, 64, 128), BF16),
            pltpu.VMEM((4, 144, NL), BF16),
            pltpu.VMEM((2, 3, 4, 24, NL), F32),
            pltpu.VMEM((2, 16, 128), F32),
            pltpu.VMEM((512, 256), BF16),
            pltpu.VMEM((1024, NL), BF16),
            pltpu.VMEM((512, 2 * NL), BF16),
            pltpu.VMEM((2, 64, 128), BF16),
            pltpu.VMEM((2, 128, 128), F32),
            pltpu.VMEM((128, 1024), BF16),
            pltpu.VMEM((2, 128, 16), F32),
            pltpu.VMEM((2, 128, 128), BF16),
            pltpu.VMEM((2, 128, 16), BF16),
            pltpu.VMEM((16, 512), BF16),
            pltpu.VMEM((9, 2, 128, 384), F32),
            pltpu.VMEM((2, 128, 384), F32),
            pltpu.VMEM((9, 512, 256), BF16),
            pltpu.VMEM((2, 128, 128), F32),
            pltpu.SemaphoreType.DMA((4, 16)),
            pltpu.SemaphoreType.DMA((4, 16)),
            pltpu.SemaphoreType.DMA((8,)),
            pltpu.SemaphoreType.DMA((8,)),
            pltpu.SemaphoreType.DMA((4,)),
            pltpu.SemaphoreType.DMA((4,)),
            pltpu.SemaphoreType.DMA((15,)),
        ],
        compiler_params=pltpu.CompilerParams(
            collective_id=0, has_side_effects=True, vmem_limit_bytes=63 * 1024 * 1024
        ),
    )(
        features.reshape(2, 128, 128),
        jnp.transpose(frac.reshape(2, 3, 128), (1, 0, 2)),
        jnp.transpose(subpoint.reshape(2, 3, 128), (1, 0, 2)),
        counts.reshape(2),
        rbf_coef,
        mesh_gain.reshape(1, 128),
        w_query,
        w_key,
        w_value,
        w_out,
        w_charge,
        w_up,
        w_down,
        mode_rows,
        *tables(),
    )
    return out.reshape(features.shape)


def solution(mesh):
    return jax.shard_map(
        per_device,
        mesh=mesh,
        in_specs=(
            P("gx", "gy", "gz", None, None),
            P("gx", "gy", "gz", None, None),
            P("gx", "gy", "gz", None, None),
            P("gx", "gy", "gz"),
            P(),
            P(),
            P(),
            P(),
            P(),
            P(),
            P(None, "gx", "gy", "gz"),
            P(),
            P(),
            P(),
        ),
        out_specs=P("gx", "gy", "gz", None, None),
        check_vma=False,
    )
```

```python
import functools
import math

import jax
import jax.numpy as jnp
import numpy as np
from jax import lax
from jax.experimental import pallas as pl
from jax.experimental.pallas import tpu as pltpu
from jax.sharding import PartitionSpec as P

MESH = pl.DeviceIdType.MESH
F32 = jnp.float32
BF16 = jnp.bfloat16

D = 128
R = 6
NRBF = 8
MX, MY, MZ = 24, 96, 48
NL = 256
LOG2E = math.log2(math.e)
NEAR = 2
XZ_STEPS = [(4, 1), (4, 0), (5, 1), (3, 1), (5, 0), (3, 0), (6, 1), (2, 1), (6, 0), (2, 0), (7, 1), (1, 1), (7, 0), (1, 0), (0, 1)]
Y_STEPS = [(0, 1), (0, 3), (1, 0), (3, 0), (1, 1), (3, 3), (1, 3), (3, 1), (0, 2), (2, 0), (1, 2), (2, 1), (3, 2), (2, 3), (2, 2)]


def tables():
    gx, ch, px = np.meshgrid(np.arange(4), np.arange(8), np.arange(8), indexing="ij")
    x_pos, x_ch = (6 * gx + px - 1).reshape(-1), ch.reshape(-1)
    fwd_x, inv_x = [], []
    for first in (0, 64):
        lane = np.arange(NL) - first
        l_ch, l_kx, l_ok = lane // MX, lane % MX, (lane >= 0) & (lane < 8 * MX)
        ang = 2 * np.pi / MX * ((x_pos[:, None] * l_kx[None, :]) % MX)
        same = (x_ch[:, None] == l_ch[None, :]) & l_ok[None, :]
        cos_x, sin_x = np.where(same, np.cos(ang), 0.0), np.where(same, np.sin(ang), 0.0)
        fwd_x.append(np.concatenate([cos_x, -sin_x], axis=1))
        inv_x.append(np.concatenate([cos_x.T, -sin_x.T], axis=0))
    fwd_x, inv_x = np.stack(fwd_x), np.stack(inv_x)

    gz, cell, pz = np.meshgrid(np.arange(4), np.arange(2), np.arange(8), indexing="ij")
    z_pos = (12 * gz + 6 * cell + pz - 1).reshape(-1)
    ang = 2 * np.pi / MZ * ((z_pos[None, :] * np.arange(MZ)[:, None]) % MZ)
    c, s = np.cos(ang), np.sin(ang)
    mat = np.stack([np.stack([c, s], 1), np.stack([-s, c], 1)], axis=1)
    eye = np.eye(8)
    fwd_z = np.einsum("kciz,pq->kcpizq", mat, eye).reshape(MZ * 2 * 8, 2 * 64 * 8)
    mat = np.stack([np.stack([c.T, -s.T], -1), np.stack([s.T, c.T], -1)], axis=0)
    inv_z = np.einsum("czki,pq->czpkiq", mat, eye).reshape(2 * 64 * 8, MZ * 2 * 8)

    gy, py = np.meshgrid(np.arange(16), np.arange(8), indexing="ij")
    y_pos = (6 * gy + py - 1)
    ang = 2 * np.pi / MY * ((y_pos[None] * np.arange(MY)[:, None, None]) % MY)
    c, s = np.cos(ang), np.sin(ang)
    fwd_y = np.stack([np.stack([c, s], 2), np.stack([-s, c], 2)], axis=0)
    fwd_y = fwd_y.reshape(2 * MY, 256)
    ct, st = np.moveaxis(c, 0, -1), np.moveaxis(s, 0, -1)
    inv_y = np.stack([np.stack([ct, -st], 2), np.stack([st, ct], 2)], axis=1)
    inv_y = inv_y.reshape(256, 2 * MY)
    return [jnp.asarray(t, dtype=BF16) for t in (fwd_x, fwd_z, fwd_y, inv_y, inv_z, inv_x)]


def dot_nn(a, b):
    return lax.dot_general(a, b, (((1,), (0,)), ((), ())), preferred_element_type=F32)


def dot_nt(a, b):
    return lax.dot_general(a, b, (((1,), (1,)), ((), ())), preferred_element_type=F32)


def dot_tn(a, b):
    return lax.dot_general(a, b, (((0,), (0,)), ((), ())), preferred_element_type=F32)


def swap_halves(first, second):
    low = lax.broadcasted_iota(jnp.int32, first.shape, 1) < 64
    return (
        jnp.where(low, first, pltpu.roll(second, 64, 1)),
        jnp.where(low, pltpu.roll(first, 64, 1), second),
    )


def stencil(point, sub, frac):
    offset = point - 1.0 - sub
    lower_w = 0.5 * (0.5 - frac) * (0.5 - frac)
    centre_w = 0.75 - frac * frac
    upper_w = 0.5 * (0.5 + frac) * (0.5 + frac)
    zero = jnp.zeros_like(offset)
    return jnp.where(
        offset == -1.0,
        lower_w,
        jnp.where(offset == 0.0, centre_w, jnp.where(offset == 1.0, upper_w, zero)),
    )


def split3(value):
    high = value.astype(BF16).astype(F32)
    rest = value - high
    middle = rest.astype(BF16).astype(F32)
    return high, middle, rest - middle


def kernel(
    feat_hbm,
    frac_ref,
    sub_ref,
    counts_ref,
    coef_ref,
    gain_ref,
    wq_hbm,
    wk_hbm,
    wv_hbm,
    wo_hbm,
    wch_hbm,
    wup_hbm,
    wdown_hbm,
    mode_hbm,
    fx_hbm,
    fz_hbm,
    fy_hbm,
    iy_hbm,
    iz_hbm,
    ix_hbm,
    out_ref,
    feat_ref,
    wq_ref,
    wk_ref,
    wv_ref,
    wo_ref,
    wch_ref,
    wup_ref,
    wdown_ref,
    fx_ref,
    fz_ref,
    fy_ref,
    iy_ref,
    iz_ref,
    ix_ref,
    halo,
    s1,
    r1,
    s2,
    r2,
    s3,
    r3,
    s4,
    r4,
    wrecv,
    wf,
    aux,
    x1,
    t2,
    v2,
    wyz,
    wx,
    rep,
    cols,
    qs,
    qaug,
    kaug,
    scores,
    dist,
    vext,
    smax,
    send_sem,
    recv_sem,
    hsend,
    hrecv,
    wsem,
    wrsem,
    lsem,
):
    gx, gy, gz = lax.axis_index("gx"), lax.axis_index("gy"), lax.axis_index("gz")
    me_xz = gz * 4 + gx

    def dev_xz(p):
        return {"gx": lax.rem(p, 4), "gz": lax.div(p, 4)}

    def dev_y(p):
        return {"gy": p}

    def remote(src, dst, ssem, rsem, device):
        return pltpu.make_async_remote_copy(
            src_ref=src, dst_ref=dst, send_sem=ssem, recv_sem=rsem, device_id=device, device_id_type=MESH
        )

    z_chip, core = lax.div(gx, 2) * 4 + gz, lax.rem(gx, 2)
    far_xz, near_y = [], []
    for step, other in XZ_STEPS:
        z = lax.rem(z_chip + step, 8)
        far_xz.append(lax.rem(z, 4) * 4 + lax.div(z, 4) * 2 + (core if other == 0 else 1 - core))
    for step_x, step_y in Y_STEPS:
        near_y.append(lax.rem(lax.div(gy, 4) + step_x, 4) * 4 + lax.rem(lax.rem(gy, 4) + step_y, 4))
    barrier = pltpu.get_barrier_semaphore()
    for p in far_xz:
        pl.semaphore_signal(barrier, inc=1, device_id=dev_xz(p), device_id_type=MESH)
    for p in near_y[::-1]:
        pl.semaphore_signal(barrier, inc=1, device_id=dev_y(p), device_id_type=MESH)

    loads = {}

    def load(index, name, src, dst):
        loads[name] = pltpu.make_async_copy(src, dst, lsem.at[index])
        loads[name].start()

    def window(p):
        start = 128 * (lax.div(p, 2) * 3 + lax.rem(p, 2))
        return mode_hbm.at[:, pl.ds(pl.multiple_of(start, 128), NL)]

    parity = lax.rem(gx, 2)
    load(0, "feat", feat_hbm, feat_ref)
    load(1, "wch", wch_hbm, wch_ref)
    load(2, "wq", wq_hbm, wq_ref)
    load(3, "fx", fx_hbm.at[parity], fx_ref)
    load(4, "fz", fz_hbm, fz_ref)
    load(5, "wk", wk_hbm, wk_ref)
    load(6, "wv", wv_hbm, wv_ref)
    load(7, "mode", window(gx), wrecv.at[gx])
    load(8, "fy", fy_hbm, fy_ref)
    load(9, "iy", iy_hbm, iy_ref)
    load(10, "iz", iz_hbm, iz_ref)
    load(11, "ix", ix_hbm.at[parity], ix_ref)
    load(12, "wo", wo_hbm, wo_ref)
    load(13, "wup", wup_hbm, wup_ref)
    load(14, "wdown", wdown_hbm, wdown_ref)

    mine = lax.div(gx, 2)
    lane_row = lax.broadcasted_iota(jnp.int32, (1, 128), 1)
    aux[...] = jnp.zeros_like(aux)
    for c in range(2):
        sub = jnp.concatenate([sub_ref[d, c : c + 1, :] for d in range(3)], axis=0).astype(F32)
        frac = jnp.concatenate([frac_ref[d, c : c + 1, :].astype(F32) for d in range(3)], axis=0)
        aux[c, 0:3, :] = ((sub + 0.5 + frac) / R).astype(BF16).astype(F32)
        aux[c, 3:4, :] = (lane_row < counts_ref[c]).astype(F32)
        aux[c, 4:7, :] = frac
        aux[c, 7:10, :] = sub
        halo[1, mine, 1 + c, 128:144, :] = aux[c].astype(BF16)
    loads["feat"].wait()
    for c in range(2):
        halo[1, mine, 1 + c, 0:128, :] = feat_ref[c]

    row_i = lax.broadcasted_iota(jnp.int32, (128, 1024), 0)
    lane_i = lax.broadcasted_iota(jnp.int32, (128, 1024), 1)
    rep[...] = (lax.shift_right_logical(lane_i, 3) == row_i).astype(F32).astype(BF16)
    eye = (
        lax.broadcasted_iota(jnp.int32, (128, 128), 0) == lax.broadcasted_iota(jnp.int32, (128, 128), 1)
    ).astype(F32).astype(BF16)
    loads["wch"].wait()
    wch = dot_nn(wch_ref[...], rep[...]).astype(BF16)
    point_rows = lax.broadcasted_iota(jnp.int32, (8, 128), 0).astype(F32)
    point_lanes = lax.bitwise_and(lax.broadcasted_iota(jnp.int32, (128, 128), 1), 7).astype(F32)
    spread = []
    for c in range(2):
        cols[c] = dot_nt(eye, aux[c].astype(BF16))
        col = cols[c]
        wy = stencil(point_rows, aux[c, 8:9, :], aux[c, 5:6, :])
        wz = stencil(point_rows, aux[c, 9:10, :], aux[c, 6:7, :])
        wyz[c] = jnp.concatenate([wz[p : p + 1, :] * wy for p in range(8)], axis=0).astype(BF16)
        wx[c] = stencil(point_lanes, col[:, 7:8], col[:, 4:5])
        wxv = wx[c] * col[:, 3:4]
        charge = dot_nn(feat_ref[c], wch)
        scaled = jnp.concatenate(
            [charge[:, 128 * t : 128 * t + 128] * wxv for t in range(8)], axis=1
        ).astype(BF16)
        spread.append(dot_nn(wyz[c], scaled))
    for t in range(8):
        even, odd = swap_halves(
            spread[0][:, 128 * t : 128 * t + 128], spread[1][:, 128 * t : 128 * t + 128]
        )
        s1[2 * t] = even.astype(BF16)
        s1[2 * t + 1] = odd.astype(BF16)

    def exchange(phase, src, dst, me, device, partners):
        copies = []
        for k, p in enumerate(partners):
            copy = remote(src.at[p], dst.at[me], send_sem.at[phase, k], recv_sem.at[phase, k], device(p))
            copy.start()
            copies.append(copy)
        dst[me] = src[me]
        return copies

    pl.semaphore_wait(barrier, 30)
    phase1 = exchange(0, s1, r1, me_xz, dev_xz, far_xz)

    halo_copies = []

    def halo_send(index, src, dst, device):
        copy = remote(src, dst, hsend.at[index], hrecv.at[index], device)
        copy.start()
        halo_copies.append(copy)
        return copy

    own_slot, far_slot = mine, 1 - mine
    inner = pl.ds(1, 2)
    own = halo.at[1, own_slot, inner]
    up_y, down_y = dev_y(lax.rem(gy + 1, 16)), dev_y(lax.rem(gy + 15, 16))
    up_z, down_z = {"gz": lax.rem(gz + 1, 4)}, {"gz": lax.rem(gz + 3, 4)}

    def send_z(index, slot):
        return [
            halo_send(index, halo.at[1, slot, 2], halo.at[1, slot, 0], up_z),
            halo_send(index + 1, halo.at[1, slot, 1], halo.at[1, slot, 3], down_z),
        ]

    def send_y(index, slot, cells):
        return [
            halo_send(index, halo.at[1, slot, cells], halo.at[0, slot, cells], up_y),
            halo_send(index + 1, halo.at[1, slot, cells], halo.at[2, slot, cells], down_y),
        ]

    own_y = send_y(2, own_slot, inner)

    loads["wq"].wait()
    for c in range(2):
        qs[c] = dot_nn(feat_ref[c], wq_ref[...]).astype(BF16)
        pos = aux[c, 0:3, :]
        qx, qy, qz = pos[0:1, :], pos[1:2, :], pos[2:3, :] + float(c)
        norm = split3(qx * qx + qy * qy + qz * qz)
        one = jnp.ones((1, 128), F32)
        rows = jnp.concatenate(
            [-2.0 * pos, -2.0 * pos, one, one, one, *norm, -2.0 * c * one, -2.0 * c * one, 0.0 * one, 0.0 * one],
            axis=0,
        )
        qaug[c] = dot_nt(eye, rows.astype(BF16)).astype(BF16)
        smax[c] = jnp.full((128, 128), -jnp.inf, F32)

    for copy in phase1:
        copy.wait_send()
    weights = []
    for off in (2, 1, 3):
        p = lax.rem(gx + off, 4)
        copy = remote(window(p), wrecv.at[gx], wsem.at[off], wrsem.at[off], {"gx": p})
        copy.start()
        weights.append(copy)

    own_z = send_z(0, own_slot)
    far_copy = halo_send(4, own, own, {"gx": 3 - gx})
    for copy in phase1:
        copy.wait_recv()
    for g in range(4):
        for t in range(2):
            first, second = swap_halves(r1[4 * g + 2 * t].astype(F32), r1[4 * g + 2 * t + 1].astype(F32))
            x1[128 * g : 128 * g + 64, 128 * t : 128 * t + 128] = first.astype(BF16)
            x1[128 * g + 64 : 128 * g + 128, 128 * t : 128 * t + 128] = second.astype(BF16)
    loads["fx"].wait()
    loads["fz"].wait()
    field = dot_nn(x1[...], fx_ref[...]).astype(BF16)
    t2[0:512, :] = field[:, 0:NL]
    t2[512:1024, :] = field[:, NL : 2 * NL]
    s2[...] = dot_nn(fz_ref[...], t2[...]).astype(BF16).reshape(16, 48, NL)
    phase2 = exchange(1, s2, r2, gy, dev_y, near_y)

    for copy in own_z:
        copy.wait_recv()
    own_y += send_y(5, own_slot, 0) + send_y(7, own_slot, 3)
    odd_core = lax.rem(gx, 2)
    near_step = (1 - 2 * odd_core).astype(F32)

    coef = [coef_ref[k] * LOG2E for k in range(NRBF)]
    scale = LOG2E / math.sqrt(D)

    def score_slab(y, x):
        slab = 3 * y + x
        feats = halo[y, x, :, 0:128, :].reshape(512, 128)
        keys = dot_nn(feats, wk_ref[...]).astype(BF16)
        vext[slab, :, 0:128] = dot_nn(feats, wv_ref[...]).astype(BF16)
        vext[slab, :, 128:256] = jnp.ones((512, 128), BF16)
        off_x = 0.0 if x is own_slot else (near_step if x is NEAR else -near_step)
        off_y = float(y - 1)
        one = jnp.ones((1, 128), F32)
        masks = []
        for z in range(4):
            rows = halo[y, x, z, 128:144, :].astype(F32)
            pos = rows[0:3, :]
            kx, ky, kz = pos[0:1, :] + off_x, pos[1:2, :] + off_y, pos[2:3, :] + float(z - 1)
            norm = split3(kx * kx + ky * ky + kz * kz)
            kaug[:, 128 * z : 128 * z + 128] = jnp.concatenate(
                [
                    pos, off_x * one, off_y * one, float(z - 1) * one, *norm, one, one, one,
                    pos[2:3, :], float(z - 1) * one, 0.0 * one, 0.0 * one,
                ],
                axis=0,
            ).astype(BF16)
            masks.append(jnp.where(rows[3:4, :] > 0.5, 0.0, -jnp.inf))
        mask = jnp.concatenate(masks, axis=1)
        for c in range(2):
            scores[slab, c] = dot_nt(qs[c], keys[128 * c : 128 * c + 384, :])
            dist[c] = dot_nn(qaug[c], kaug[:, 128 * c : 128 * c + 384])
            for r in range(0, 128, 16):
                t = jnp.exp2(dist[c, r : r + 16, :] * (-0.08 * LOG2E))
                powers = [t]
                for k in range(NRBF - 2):
                    powers.append(powers[-1] * powers[-1])
                bias = coef[NRBF - 1] * powers[-1] + coef[NRBF - 2]
                for k in range(NRBF - 3, -1, -1):
                    bias = bias * powers[k] + coef[k]
                bias = bias * t
                full = scores[slab, c, r : r + 16, :] * scale + bias + mask[:, 128 * c : 128 * c + 384]
                scores[slab, c, r : r + 16, :] = full
                top = jnp.maximum(jnp.maximum(full[:, 0:128], full[:, 128:256]), full[:, 256:384])
                smax[c, r : r + 16, :] = jnp.maximum(smax[c, r : r + 16, :], top)

    loads["wk"].wait()
    loads["wv"].wait()
    score_slab(1, own_slot)
    far_copy.wait_recv()
    far_z = send_z(9, far_slot)

    for copy in weights:
        copy.wait_recv()
    for name in ("mode", "fy", "iy"):
        loads[name].wait()
    for q in range(4):
        wf[:, :, q] = wrecv[q].astype(F32).reshape(2, 3, 24, NL) * (1.0 / (MX * MY * MZ))
    for copy in phase2:
        copy.wait_recv()
    for j in range(3):
        spectrum = dot_nn(fy_ref[...], r2[:, 16 * j : 16 * j + 16, :].reshape(256, NL))
        real, imag = spectrum[0:MY, :], spectrum[MY : 2 * MY, :]
        w_real, w_imag = wf[0, j].reshape(MY, NL), wf[1, j].reshape(MY, NL)
        mixed = jnp.concatenate(
            [real * w_real - imag * w_imag, real * w_imag + imag * w_real], axis=0
        ).astype(BF16)
        s3[:, 16 * j : 16 * j + 16, :] = dot_nn(iy_ref[...], mixed).astype(BF16).reshape(16, 16, NL)
    phase3 = exchange(2, s3, r3, gy, dev_y, near_y)

    for copy in far_z:
        copy.wait_recv()
    far_y = send_y(11, far_slot, pl.ds(0, 4))
    for copy in own_y:
        copy.wait_recv()
    near = halo_send(13, halo.at[:, own_slot], halo.at[:, NEAR], {"gx": gx + 1 - 2 * odd_core})
    score_slab(0, own_slot)
    score_slab(2, own_slot)
    near.wait_recv()
    for y in range(3):
        score_slab(y, NEAR)

    for copy in phase3:
        copy.wait_recv()
    loads["iz"].wait()
    loads["ix"].wait()
    back = dot_nn(iz_ref[...], r3[...].reshape(768, NL)).astype(BF16)
    v2[:, 0:NL] = back[0:512, :]
    v2[:, NL : 2 * NL] = back[512:1024, :]
    potential = dot_nn(v2[...], ix_ref[...])
    for g in range(4):
        for t in range(2):
            even, odd = swap_halves(
                potential[128 * g : 128 * g + 64, 128 * t : 128 * t + 128],
                potential[128 * g + 64 : 128 * g + 128, 128 * t : 128 * t + 128],
            )
            s4[4 * g + 2 * t] = even.astype(BF16)
            s4[4 * g + 2 * t + 1] = odd.astype(BF16)
    phase4 = exchange(3, s4, r4, me_xz, dev_xz, far_xz)

    score_slab(1, far_slot)
    for copy in far_y:
        copy.wait_recv()
    score_slab(0, far_slot)
    score_slab(2, far_slot)
    after = []
    for name in ("wo", "wup", "wdown"):
        loads[name].wait()
    for c in range(2):
        top = jnp.max(smax[c], axis=1, keepdims=True)

        def mix(slab, acc, c=c, top=top):
            probs = jnp.exp2(scores[slab, c] - top).astype(BF16)
            return acc + dot_nn(probs, vext[slab, 128 * c : 128 * c + 384, :])

        acc = lax.fori_loop(0, 9, mix, jnp.zeros((128, 256), F32))
        attended = (acc[:, 0:128] / acc[:, 128:256]).astype(BF16)
        after.append(feat_ref[c].astype(F32) + dot_nn(attended, wo_ref[...]))

    for copy in phase4:
        copy.wait_recv()
    fields = [[], []]
    for t in range(8):
        first, second = swap_halves(r4[2 * t].astype(F32), r4[2 * t + 1].astype(F32))
        fields[0].append(first.astype(BF16))
        fields[1].append(second.astype(BF16))
    for c in range(2):
        lines = dot_tn(wyz[c], jnp.concatenate(fields[c], axis=1))
        lines = jnp.concatenate(
            [lines[:, 128 * t : 128 * t + 128] * wx[c] for t in range(8)], axis=1
        ).astype(BF16)
        sampled = dot_nt(lines, rep[...])
        norm_scale = lax.rsqrt(jnp.mean(sampled * sampled, axis=1, keepdims=True) + 1e-06)
        joined = after[c] + sampled * norm_scale * gain_ref[...]
        inner = dot_nn(joined.astype(BF16), wup_ref[...])
        inner = (inner * jax.nn.sigmoid(inner)).astype(BF16)
        result = joined + dot_nn(inner, wdown_ref[...])
        out_ref[c] = jnp.where(cols[c][:, 3:4] > 0.5, result, 0.0).astype(BF16)

    for copy in phase2 + phase3 + phase4 + weights + halo_copies:
        copy.wait_send()


def per_device(
    features,
    frac,
    subpoint,
    counts,
    w_query,
    w_key,
    w_value,
    rbf_coef,
    w_out,
    w_charge,
    mode_weight,
    mesh_gain,
    w_up,
    w_down,
):
    mode_rows = jnp.transpose(mode_weight, (0, 2, 1, 3)).reshape(144, 768)
    vmem = pl.BlockSpec(memory_space=pltpu.VMEM)
    smem = pl.BlockSpec(memory_space=pltpu.SMEM)
    hbm = pl.BlockSpec(memory_space=pltpu.HBM)
    out = pl.pallas_call(
        kernel,
        out_shape=jax.ShapeDtypeStruct((2, 128, 128), BF16),
        in_specs=[hbm, vmem, vmem, smem, smem, vmem] + [hbm] * 14,
        out_specs=vmem,
        scratch_shapes=[
            pltpu.VMEM((2, 128, 128), BF16),
            pltpu.VMEM((128, 128), BF16),
            pltpu.VMEM((128, 128), BF16),
            pltpu.VMEM((128, 128), BF16),
            pltpu.VMEM((128, 128), BF16),
            pltpu.VMEM((128, 128), BF16),
            pltpu.VMEM((128, 256), BF16),
            pltpu.VMEM((256, 128), BF16),
            pltpu.VMEM((256, 2 * NL), BF16),
            pltpu.VMEM((768, 1024), BF16),
            pltpu.VMEM((192, 256), BF16),
            pltpu.VMEM((256, 192), BF16),
            pltpu.VMEM((1024, 768), BF16),
            pltpu.VMEM((2 * NL, 256), BF16),
            pltpu.VMEM((3, 3, 4, 144, 128), BF16),
            pltpu.VMEM((16, 64, 128), BF16),
            pltpu.VMEM((16, 64, 128), BF16),
            pltpu.VMEM((16, 48, NL), BF16),
            pltpu.VMEM((16, 48, NL), BF16),
            pltpu.VMEM((16, 48, NL), BF16),
            pltpu.VMEM((16, 48, NL), BF16),
            pltpu.VMEM((16, 64, 128), BF16),
            pltpu.VMEM((16, 64, 128), BF16),
            pltpu.VMEM((4, 144, NL), BF16),
            pltpu.VMEM((2, 3, 4, 24, NL), F32),
            pltpu.VMEM((2, 16, 128), F32),
            pltpu.VMEM((512, 256), BF16),
            pltpu.VMEM((1024, NL), BF16),
            pltpu.VMEM((512, 2 * NL), BF16),
            pltpu.VMEM((2, 64, 128), BF16),
            pltpu.VMEM((2, 128, 128), F32),
            pltpu.VMEM((128, 1024), BF16),
            pltpu.VMEM((2, 128, 16), F32),
            pltpu.VMEM((2, 128, 128), BF16),
            pltpu.VMEM((2, 128, 16), BF16),
            pltpu.VMEM((16, 512), BF16),
            pltpu.VMEM((9, 2, 128, 384), F32),
            pltpu.VMEM((2, 128, 384), F32),
            pltpu.VMEM((9, 512, 256), BF16),
            pltpu.VMEM((2, 128, 128), F32),
            pltpu.SemaphoreType.DMA((4, 16)),
            pltpu.SemaphoreType.DMA((4, 16)),
            pltpu.SemaphoreType.DMA((14,)),
            pltpu.SemaphoreType.DMA((14,)),
            pltpu.SemaphoreType.DMA((4,)),
            pltpu.SemaphoreType.DMA((4,)),
            pltpu.SemaphoreType.DMA((15,)),
        ],
        compiler_params=pltpu.CompilerParams(
            collective_id=0, has_side_effects=True, vmem_limit_bytes=63 * 1024 * 1024
        ),
    )(
        features.reshape(2, 128, 128),
        jnp.transpose(frac.reshape(2, 3, 128), (1, 0, 2)),
        jnp.transpose(subpoint.reshape(2, 3, 128), (1, 0, 2)),
        counts.reshape(2),
        rbf_coef,
        mesh_gain.reshape(1, 128),
        w_query,
        w_key,
        w_value,
        w_out,
        w_charge,
        w_up,
        w_down,
        mode_rows,
        *tables(),
    )
    return out.reshape(features.shape)


def solution(mesh):
    return jax.shard_map(
        per_device,
        mesh=mesh,
        in_specs=(
            P("gx", "gy", "gz", None, None),
            P("gx", "gy", "gz", None, None),
            P("gx", "gy", "gz", None, None),
            P("gx", "gy", "gz"),
            P(),
            P(),
            P(),
            P(),
            P(),
            P(),
            P(None, "gx", "gy", "gz"),
            P(),
            P(),
            P(),
        ),
        out_specs=P("gx", "gy", "gz", None, None),
        check_vma=False,
    )
```

```python
import functools
import math

import jax
import jax.numpy as jnp
import numpy as np
from jax import lax
from jax.experimental import pallas as pl
from jax.experimental.pallas import tpu as pltpu
from jax.sharding import PartitionSpec as P

MESH = pl.DeviceIdType.MESH
F32 = jnp.float32
BF16 = jnp.bfloat16

D = 128
R = 6
NRBF = 8
MX, MY, MZ = 24, 96, 48
NL = 128
LOG2E = math.log2(math.e)
NEAR = 2
XZ_STEPS = [(4, 1), (4, 0), (5, 1), (3, 1), (5, 0), (3, 0), (6, 1), (2, 1), (6, 0), (2, 0), (7, 1), (1, 1), (7, 0), (1, 0), (0, 1)]
Y_STEPS = [(0, 1), (0, 3), (1, 0), (3, 0), (1, 1), (3, 3), (1, 3), (3, 1), (0, 2), (2, 0), (1, 2), (2, 1), (3, 2), (2, 3), (2, 2)]


def tables():
    gx, ch, px = np.meshgrid(np.arange(4), np.arange(8), np.arange(8), indexing="ij")
    x_pos, x_ch = (6 * gx + px - 1).reshape(-1), ch.reshape(-1)
    lane = np.arange(NL)
    l_ch, l_kx, l_ok = lane // 16, lane % 16, lane % 16 <= MX // 2
    ang = 2 * np.pi / MX * ((x_pos[:, None] * l_kx[None, :]) % MX)
    same = (x_ch[:, None] == l_ch[None, :]) & l_ok[None, :]
    cos_x, sin_x = np.where(same, np.cos(ang), 0.0), np.where(same, np.sin(ang), 0.0)
    fwd_x = np.concatenate([cos_x, -sin_x], axis=1)
    inv_x = np.concatenate([cos_x.T, -sin_x.T], axis=0)

    row = np.arange(384)
    pair_lane = np.arange(2 * NL)
    l_ch, l_kx = pair_lane // 16, pair_lane % 16
    share = np.where(l_kx % (MX // 2) == 0, 0.5, 1.0) * (l_kx <= MX // 2)
    picks = [
        (row[:, None] == (l_ch * MX + kx)[None, :]) * share[None, :] for kx in (l_kx, (MX - l_kx) % MX)
    ]
    pick = np.concatenate(picks, axis=1)

    gz, cell, pz = np.meshgrid(np.arange(4), np.arange(2), np.arange(8), indexing="ij")
    z_pos = (12 * gz + 6 * cell + pz - 1).reshape(-1)
    ang = 2 * np.pi / MZ * ((z_pos[None, :] * np.arange(MZ)[:, None]) % MZ)
    c, s = np.cos(ang), np.sin(ang)
    mat = np.stack([np.stack([c, s], 1), np.stack([-s, c], 1)], axis=1)
    eye = np.eye(8)
    fwd_z = np.einsum("kciz,pq->kcpizq", mat, eye).reshape(MZ * 2 * 8, 2 * 64 * 8)
    mat = np.stack([np.stack([c.T, -s.T], -1), np.stack([s.T, c.T], -1)], axis=0)
    inv_z = np.einsum("czki,pq->czpkiq", mat, eye).reshape(2 * 64 * 8, MZ * 2 * 8)

    gy, py = np.meshgrid(np.arange(16), np.arange(8), indexing="ij")
    y_pos = (6 * gy + py - 1)
    ang = 2 * np.pi / MY * ((y_pos[None] * np.arange(MY)[:, None, None]) % MY)
    c, s = np.cos(ang), np.sin(ang)
    fwd_y = np.stack([np.stack([c, s], 2), np.stack([-s, c], 2)], axis=0)
    fwd_y = fwd_y.reshape(2 * MY, 256)
    ct, st = np.moveaxis(c, 0, -1), np.moveaxis(s, 0, -1)
    inv_y = np.stack([np.stack([ct, -st], 2), np.stack([st, ct], 2)], axis=1)
    inv_y = inv_y.reshape(256, 2 * MY)
    return [jnp.asarray(t, dtype=BF16) for t in (fwd_x, fwd_z, fwd_y, inv_y, inv_z, inv_x, pick)]


def dot_nn(a, b):
    return lax.dot_general(a, b, (((1,), (0,)), ((), ())), preferred_element_type=F32)


def dot_nt(a, b):
    return lax.dot_general(a, b, (((1,), (1,)), ((), ())), preferred_element_type=F32)


def dot_tn(a, b):
    return lax.dot_general(a, b, (((0,), (0,)), ((), ())), preferred_element_type=F32)


def swap_halves(first, second):
    low = lax.broadcasted_iota(jnp.int32, first.shape, 1) < 64
    return (
        jnp.where(low, first, pltpu.roll(second, 64, 1)),
        jnp.where(low, pltpu.roll(first, 64, 1), second),
    )


def stencil(point, sub, frac):
    offset = point - 1.0 - sub
    lower_w = 0.5 * (0.5 - frac) * (0.5 - frac)
    centre_w = 0.75 - frac * frac
    upper_w = 0.5 * (0.5 + frac) * (0.5 + frac)
    zero = jnp.zeros_like(offset)
    return jnp.where(
        offset == -1.0,
        lower_w,
        jnp.where(offset == 0.0, centre_w, jnp.where(offset == 1.0, upper_w, zero)),
    )


def split3(value):
    high = value.astype(BF16).astype(F32)
    rest = value - high
    middle = rest.astype(BF16).astype(F32)
    return high, middle, rest - middle


def kernel(
    feat_hbm,
    frac_ref,
    sub_ref,
    counts_ref,
    coef_ref,
    gain_ref,
    wq_hbm,
    wk_hbm,
    wv_hbm,
    wo_hbm,
    wch_hbm,
    wup_hbm,
    wdown_hbm,
    mode_hbm,
    fx_hbm,
    fz_hbm,
    fy_hbm,
    iy_hbm,
    iz_hbm,
    ix_hbm,
    pick_hbm,
    out_ref,
    feat_ref,
    wq_ref,
    wk_ref,
    wv_ref,
    wo_ref,
    wch_ref,
    wup_ref,
    wdown_ref,
    fx_ref,
    fz_ref,
    fy_ref,
    iy_ref,
    iz_ref,
    ix_ref,
    pick_ref,
    mode_own,
    mode_first,
    mode_rest,
    wsend,
    halo,
    s1,
    r1,
    s2,
    r2,
    s3,
    r3,
    s4,
    r4,
    wrecv,
    wf,
    aux,
    x1,
    t2,
    v2,
    wyz,
    wx,
    rep,
    cols,
    qs,
    qaug,
    kaug,
    scores,
    dist,
    vext,
    smax,
    send_sem,
    recv_sem,
    hsend,
    hrecv,
    wsem,
    wrsem,
    lsem,
    psend,
    precv,
):
    gx, gy, gz = lax.axis_index("gx"), lax.axis_index("gy"), lax.axis_index("gz")
    me_xz = gz * 4 + gx

    def dev_xz(p):
        return {"gx": lax.rem(p, 4), "gz": lax.div(p, 4)}

    def dev_y(p):
        return {"gy": p}

    def remote(src, dst, ssem, rsem, device):
        return pltpu.make_async_remote_copy(
            src_ref=src, dst_ref=dst, send_sem=ssem, recv_sem=rsem, device_id=device, device_id_type=MESH
        )

    z_chip, core = lax.div(gx, 2) * 4 + gz, lax.rem(gx, 2)
    far_xz, near_y = [], []
    for step, other in XZ_STEPS:
        z = lax.rem(z_chip + step, 8)
        far_xz.append(lax.rem(z, 4) * 4 + lax.div(z, 4) * 2 + (core if other == 0 else 1 - core))
    for step_x, step_y in Y_STEPS:
        near_y.append(lax.rem(lax.div(gy, 4) + step_x, 4) * 4 + lax.rem(lax.rem(gy, 4) + step_y, 4))
    barrier = pltpu.get_barrier_semaphore()
    for p in far_xz:
        pl.semaphore_signal(barrier, inc=1, device_id=dev_xz(p), device_id_type=MESH)
    for p in near_y[::-1]:
        pl.semaphore_signal(barrier, inc=1, device_id=dev_y(p), device_id_type=MESH)

    loads = {}

    def load(index, name, src, dst):
        loads[name] = pltpu.make_async_copy(src, dst, lsem.at[index])
        loads[name].start()

    load(0, "feat", feat_hbm, feat_ref)
    load(1, "wch", wch_hbm, wch_ref)
    load(2, "wq", wq_hbm, wq_ref)
    load(3, "fx", fx_hbm, fx_ref)
    load(4, "fz", fz_hbm, fz_ref)
    load(5, "wk", wk_hbm, wk_ref)
    load(6, "wv", wv_hbm, wv_ref)
    load(7, "mode", mode_hbm, mode_own)
    load(15, "pick", pick_hbm, pick_ref)
    load(8, "fy", fy_hbm, fy_ref)
    load(9, "iy", iy_hbm, iy_ref)
    load(10, "iz", iz_hbm, iz_ref)
    load(11, "ix", ix_hbm, ix_ref)
    load(12, "wo", wo_hbm, wo_ref)
    load(13, "wup", wup_hbm, wup_ref)
    load(14, "wdown", wdown_hbm, wdown_ref)

    mine = lax.div(gx, 2)
    lane_row = lax.broadcasted_iota(jnp.int32, (1, 128), 1)
    aux[...] = jnp.zeros_like(aux)
    for c in range(2):
        sub = jnp.concatenate([sub_ref[d, c : c + 1, :] for d in range(3)], axis=0).astype(F32)
        frac = jnp.concatenate([frac_ref[d, c : c + 1, :].astype(F32) for d in range(3)], axis=0)
        aux[c, 0:3, :] = ((sub + 0.5 + frac) / R).astype(BF16).astype(F32)
        aux[c, 3:4, :] = (lane_row < counts_ref[c]).astype(F32)
        aux[c, 4:7, :] = frac
        aux[c, 7:10, :] = sub
        halo[1, mine, 1 + c, 128:144, :] = aux[c].astype(BF16)
    loads["feat"].wait()
    for c in range(2):
        halo[1, mine, 1 + c, 0:128, :] = feat_ref[c]

    row_i = lax.broadcasted_iota(jnp.int32, (128, 1024), 0)
    lane_i = lax.broadcasted_iota(jnp.int32, (128, 1024), 1)
    rep[...] = (lax.shift_right_logical(lane_i, 3) == row_i).astype(F32).astype(BF16)
    eye = (
        lax.broadcasted_iota(jnp.int32, (128, 128), 0) == lax.broadcasted_iota(jnp.int32, (128, 128), 1)
    ).astype(F32).astype(BF16)
    loads["wch"].wait()
    wch = dot_nn(wch_ref[...], rep[...]).astype(BF16)
    point_rows = lax.broadcasted_iota(jnp.int32, (8, 128), 0).astype(F32)
    point_lanes = lax.bitwise_and(lax.broadcasted_iota(jnp.int32, (128, 128), 1), 7).astype(F32)
    spread = []
    for c in range(2):
        cols[c] = dot_nt(eye, aux[c].astype(BF16))
        col = cols[c]
        wy = stencil(point_rows, aux[c, 8:9, :], aux[c, 5:6, :])
        wz = stencil(point_rows, aux[c, 9:10, :], aux[c, 6:7, :])
        wyz[c] = jnp.concatenate([wz[p : p + 1, :] * wy for p in range(8)], axis=0).astype(BF16)
        wx[c] = stencil(point_lanes, col[:, 7:8], col[:, 4:5])
        wxv = wx[c] * col[:, 3:4]
        charge = dot_nn(feat_ref[c], wch)
        scaled = jnp.concatenate(
            [charge[:, 128 * t : 128 * t + 128] * wxv for t in range(8)], axis=1
        ).astype(BF16)
        spread.append(dot_nn(wyz[c], scaled))
    for t in range(8):
        even, odd = swap_halves(
            spread[0][:, 128 * t : 128 * t + 128], spread[1][:, 128 * t : 128 * t + 128]
        )
        s1[2 * t] = even.astype(BF16)
        s1[2 * t + 1] = odd.astype(BF16)

    def exchange(phase, src, dst, me, device, partners):
        copies = []
        for k, p in enumerate(partners):
            copy = remote(src.at[p], dst.at[me], send_sem.at[phase, k], recv_sem.at[phase, k], device(p))
            copy.start()
            copies.append(copy)
        dst[me] = src[me]
        return copies

    pl.semaphore_wait(barrier, 30)
    phase1 = exchange(0, s1, r1, me_xz, dev_xz, far_xz)

    mirror, is_own = lax.rem(16 - gy, 16), lax.rem(gy, 8) == 0
    first_local = pltpu.make_async_copy(mode_hbm.at[:, 0], mode_first, lsem.at[16])
    first_copy = remote(mode_hbm.at[:, 0], mode_first, psend.at[0], precv.at[0], dev_y(mirror))
    rest_copy = remote(mode_hbm.at[:, pl.ds(1, 2)], mode_rest, psend.at[1], precv.at[1], dev_y(15 - gy))

    @pl.when(is_own)
    def _():
        first_local.start()

    @pl.when(jnp.logical_not(is_own))
    def _():
        first_copy.start()

    rest_copy.start()

    halo_copies = []

    def halo_send(index, src, dst, device):
        copy = remote(src, dst, hsend.at[index], hrecv.at[index], device)
        copy.start()
        halo_copies.append(copy)
        return copy

    own_slot, far_slot = mine, 1 - mine
    inner = pl.ds(1, 2)
    own = halo.at[1, own_slot, inner]
    up_y, down_y = dev_y(lax.rem(gy + 1, 16)), dev_y(lax.rem(gy + 15, 16))
    up_z, down_z = {"gz": lax.rem(gz + 1, 4)}, {"gz": lax.rem(gz + 3, 4)}

    def send_z(index, slot):
        return [
            halo_send(index, halo.at[1, slot, 2], halo.at[1, slot, 0], up_z),
            halo_send(index + 1, halo.at[1, slot, 1], halo.at[1, slot, 3], down_z),
        ]

    def send_y(index, slot, cells):
        return [
            halo_send(index, halo.at[1, slot, cells], halo.at[0, slot, cells], up_y),
            halo_send(index + 1, halo.at[1, slot, cells], halo.at[2, slot, cells], down_y),
        ]

    own_y = send_y(2, own_slot, inner)

    loads["wq"].wait()
    for c in range(2):
        qs[c] = dot_nn(feat_ref[c], wq_ref[...]).astype(BF16)
        pos = aux[c, 0:3, :]
        qx, qy, qz = pos[0:1, :], pos[1:2, :], pos[2:3, :] + float(c)
        norm = split3(qx * qx + qy * qy + qz * qz)
        one = jnp.ones((1, 128), F32)
        rows = jnp.concatenate(
            [-2.0 * pos, -2.0 * pos, one, one, one, *norm, -2.0 * c * one, -2.0 * c * one, 0.0 * one, 0.0 * one],
            axis=0,
        )
        qaug[c] = dot_nt(eye, rows.astype(BF16)).astype(BF16)
        smax[c] = jnp.full((128, 128), -jnp.inf, F32)

    for copy in phase1:
        copy.wait_send()
    loads["mode"].wait()
    loads["pick"].wait()
    at_k = mode_own[...].astype(F32).reshape(144, 768).astype(BF16)
    for t in range(2):
        picked = dot_nn(at_k[:, 384 * t : 384 * t + 384], pick_ref[:, 0 : 2 * NL]).astype(BF16)
        for e in range(2):
            wsend[2 * t + e, :, 0:NL] = picked[:, NL * e : NL * e + NL]

    @pl.when(is_own)
    def _():
        first_local.wait()

    @pl.when(jnp.logical_not(is_own))
    def _():
        first_copy.wait()

    rest_copy.wait()
    first = mode_first[...].astype(F32).reshape(2, 1, 24, 768)
    rest = mode_rest[...].astype(F32)
    at_minus_k = jnp.concatenate([first, rest[:, 1:2], rest[:, 0:1]], axis=1).reshape(144, 768).astype(BF16)
    for t in range(2):
        picked = dot_nn(at_minus_k[:, 384 * t : 384 * t + 384], pick_ref[:, 2 * NL : 4 * NL]).astype(BF16)
        for e in range(2):
            wsend[2 * t + e, :, NL : 2 * NL] = picked[:, NL * e : NL * e + NL]
    weights = []
    for off in (2, 1, 3):
        p = lax.rem(gx + off, 4)
        copy = remote(wsend.at[p], wrecv.at[gx], wsem.at[off], wrsem.at[off], {"gx": p})
        copy.start()
        weights.append(copy)
    wrecv[gx] = wsend[gx]

    own_z = send_z(0, own_slot)
    far_copy = halo_send(4, own, own, {"gx": 3 - gx})
    for copy in phase1:
        copy.wait_recv()
    for g in range(4):
        for t in range(2):
            first, second = swap_halves(r1[4 * g + 2 * t].astype(F32), r1[4 * g + 2 * t + 1].astype(F32))
            x1[128 * g : 128 * g + 64, 128 * t : 128 * t + 128] = first.astype(BF16)
            x1[128 * g + 64 : 128 * g + 128, 128 * t : 128 * t + 128] = second.astype(BF16)
    loads["fx"].wait()
    loads["fz"].wait()
    field = dot_nn(x1[...], fx_ref[...]).astype(BF16)
    t2[0:512, :] = field[:, 0:NL]
    t2[512:1024, :] = field[:, NL : 2 * NL]
    s2[...] = dot_nn(fz_ref[...], t2[...]).astype(BF16).reshape(16, 48, NL)
    phase2 = exchange(1, s2, r2, gy, dev_y, near_y)

    for copy in own_z:
        copy.wait_recv()
    own_y += send_y(5, own_slot, 0) + send_y(7, own_slot, 3)
    odd_core = lax.rem(gx, 2)
    near_step = (1 - 2 * odd_core).astype(F32)

    coef = [coef_ref[k] * LOG2E for k in range(NRBF)]
    scale = LOG2E / math.sqrt(D)

    def score_slab(y, x):
        slab = 3 * y + x
        feats = halo[y, x, :, 0:128, :].reshape(512, 128)
        keys = dot_nn(feats, wk_ref[...]).astype(BF16)
        vext[slab, :, 0:128] = dot_nn(feats, wv_ref[...]).astype(BF16)
        vext[slab, :, 128:256] = jnp.ones((512, 128), BF16)
        off_x = 0.0 if x is own_slot else (near_step if x is NEAR else -near_step)
        off_y = float(y - 1)
        one = jnp.ones((1, 128), F32)
        masks = []
        for z in range(4):
            rows = halo[y, x, z, 128:144, :].astype(F32)
            pos = rows[0:3, :]
            kx, ky, kz = pos[0:1, :] + off_x, pos[1:2, :] + off_y, pos[2:3, :] + float(z - 1)
            norm = split3(kx * kx + ky * ky + kz * kz)
            kaug[:, 128 * z : 128 * z + 128] = jnp.concatenate(
                [
                    pos, off_x * one, off_y * one, float(z - 1) * one, *norm, one, one, one,
                    pos[2:3, :], float(z - 1) * one, 0.0 * one, 0.0 * one,
                ],
                axis=0,
            ).astype(BF16)
            masks.append(jnp.where(rows[3:4, :] > 0.5, 0.0, -jnp.inf))
        mask = jnp.concatenate(masks, axis=1)
        for c in range(2):
            scores[slab, c] = dot_nt(qs[c], keys[128 * c : 128 * c + 384, :])
            dist[c] = dot_nn(qaug[c], kaug[:, 128 * c : 128 * c + 384])
            for r in range(0, 128, 16):
                t = jnp.exp2(dist[c, r : r + 16, :] * (-0.08 * LOG2E))
                powers = [t]
                for k in range(NRBF - 2):
                    powers.append(powers[-1] * powers[-1])
                bias = coef[NRBF - 1] * powers[-1] + coef[NRBF - 2]
                for k in range(NRBF - 3, -1, -1):
                    bias = bias * powers[k] + coef[k]
                bias = bias * t
                full = scores[slab, c, r : r + 16, :] * scale + bias + mask[:, 128 * c : 128 * c + 384]
                scores[slab, c, r : r + 16, :] = full
                top = jnp.maximum(jnp.maximum(full[:, 0:128], full[:, 128:256]), full[:, 256:384])
                smax[c, r : r + 16, :] = jnp.maximum(smax[c, r : r + 16, :], top)

    loads["wk"].wait()
    loads["wv"].wait()
    score_slab(1, own_slot)
    far_copy.wait_recv()
    far_z = send_z(9, far_slot)

    for copy in weights:
        copy.wait_recv()
    for name in ("fy", "iy"):
        loads[name].wait()
    for q in range(4):
        wf[:, :, q] = wrecv[q].astype(F32).reshape(2, 3, 24, 2 * NL) * (1.0 / (MX * MY * MZ))
    place = lax.broadcasted_iota(jnp.int32, (MY, MY), 0) + lax.broadcasted_iota(jnp.int32, (MY, MY), 1)
    flip = jnp.logical_or(place == 0, place == MY).astype(F32).astype(BF16)
    minus = jnp.concatenate(
        [
            jnp.concatenate([wrecv[q, 24 * i : 24 * i + 24, NL : 2 * NL].astype(F32) for q in range(4)], axis=0)
            for i in range(6)
        ],
        axis=1,
    ).astype(BF16)
    minus = dot_nn(flip, minus) * (1.0 / (MX * MY * MZ))
    w_real = jnp.concatenate([wf[0, j].reshape(MY, 2 * NL)[:, 0:NL] for j in range(3)], axis=1)
    w_imag = jnp.concatenate([wf[1, j].reshape(MY, 2 * NL)[:, 0:NL] for j in range(3)], axis=1)
    w_real = w_real + minus[:, 0 : 3 * NL]
    w_imag = w_imag - minus[:, 3 * NL : 6 * NL]
    for copy in phase2:
        copy.wait_recv()
    lines = jnp.concatenate([r2[:, 16 * j : 16 * j + 16, :].reshape(256, NL) for j in range(3)], axis=1)
    spectrum = dot_nn(fy_ref[...], lines)
    real, imag = spectrum[0:MY, :], spectrum[MY : 2 * MY, :]
    mixed = jnp.concatenate(
        [real * w_real - imag * w_imag, real * w_imag + imag * w_real], axis=0
    ).astype(BF16)
    lines = dot_nn(iy_ref[...], mixed).astype(BF16)
    for j in range(3):
        s3[:, 16 * j : 16 * j + 16, :] = lines[:, NL * j : NL * j + NL].reshape(16, 16, NL)
    phase3 = exchange(2, s3, r3, gy, dev_y, near_y)

    for copy in far_z:
        copy.wait_recv()
    far_y = send_y(11, far_slot, pl.ds(0, 4))
    for copy in own_y:
        copy.wait_recv()
    near = halo_send(13, halo.at[:, own_slot], halo.at[:, NEAR], {"gx": gx + 1 - 2 * odd_core})
    score_slab(0, own_slot)
    score_slab(2, own_slot)
    near.wait_recv()
    for y in range(3):
        score_slab(y, NEAR)

    for copy in phase3:
        copy.wait_recv()
    loads["iz"].wait()
    loads["ix"].wait()
    back = dot_nn(iz_ref[...], r3[...].reshape(768, NL)).astype(BF16)
    v2[:, 0:NL] = back[0:512, :]
    v2[:, NL : 2 * NL] = back[512:1024, :]
    potential = dot_nn(v2[...], ix_ref[...])
    for g in range(4):
        for t in range(2):
            even, odd = swap_halves(
                potential[128 * g : 128 * g + 64, 128 * t : 128 * t + 128],
                potential[128 * g + 64 : 128 * g + 128, 128 * t : 128 * t + 128],
            )
            s4[4 * g + 2 * t] = even.astype(BF16)
            s4[4 * g + 2 * t + 1] = odd.astype(BF16)
    phase4 = exchange(3, s4, r4, me_xz, dev_xz, far_xz)

    score_slab(1, far_slot)
    for copy in far_y:
        copy.wait_recv()
    score_slab(0, far_slot)
    score_slab(2, far_slot)
    after = []
    for name in ("wo", "wup", "wdown"):
        loads[name].wait()
    for c in range(2):
        top = jnp.max(smax[c], axis=1, keepdims=True)

        def mix(slab, acc, c=c, top=top):
            probs = jnp.exp2(scores[slab, c] - top).astype(BF16)
            return acc + dot_nn(probs, vext[slab, 128 * c : 128 * c + 384, :])

        acc = lax.fori_loop(0, 9, mix, jnp.zeros((128, 256), F32))
        attended = (acc[:, 0:128] / acc[:, 128:256]).astype(BF16)
        after.append(feat_ref[c].astype(F32) + dot_nn(attended, wo_ref[...]))

    for copy in phase4:
        copy.wait_recv()
    fields = [[], []]
    for t in range(8):
        first, second = swap_halves(r4[2 * t].astype(F32), r4[2 * t + 1].astype(F32))
        fields[0].append(first.astype(BF16))
        fields[1].append(second.astype(BF16))
    for c in range(2):
        lines = dot_tn(wyz[c], jnp.concatenate(fields[c], axis=1))
        lines = jnp.concatenate(
            [lines[:, 128 * t : 128 * t + 128] * wx[c] for t in range(8)], axis=1
        ).astype(BF16)
        sampled = dot_nt(lines, rep[...])
        norm_scale = lax.rsqrt(jnp.mean(sampled * sampled, axis=1, keepdims=True) + 1e-06)
        joined = after[c] + sampled * norm_scale * gain_ref[...]
        inner = dot_nn(joined.astype(BF16), wup_ref[...])
        inner = (inner * jax.nn.sigmoid(inner)).astype(BF16)
        result = joined + dot_nn(inner, wdown_ref[...])
        out_ref[c] = jnp.where(cols[c][:, 3:4] > 0.5, result, 0.0).astype(BF16)

    for copy in phase2 + phase3 + phase4 + weights + halo_copies:
        copy.wait_send()


def per_device(
    features,
    frac,
    subpoint,
    counts,
    w_query,
    w_key,
    w_value,
    rbf_coef,
    w_out,
    w_charge,
    mode_weight,
    mesh_gain,
    w_up,
    w_down,
):
    mode_rows = jnp.transpose(mode_weight, (0, 2, 1, 3))
    vmem = pl.BlockSpec(memory_space=pltpu.VMEM)
    smem = pl.BlockSpec(memory_space=pltpu.SMEM)
    hbm = pl.BlockSpec(memory_space=pltpu.HBM)
    out = pl.pallas_call(
        kernel,
        out_shape=jax.ShapeDtypeStruct((2, 128, 128), BF16),
        in_specs=[hbm, vmem, vmem, smem, smem, vmem] + [hbm] * 15,
        out_specs=vmem,
        scratch_shapes=[
            pltpu.VMEM((2, 128, 128), BF16),
            pltpu.VMEM((128, 128), BF16),
            pltpu.VMEM((128, 128), BF16),
            pltpu.VMEM((128, 128), BF16),
            pltpu.VMEM((128, 128), BF16),
            pltpu.VMEM((128, 128), BF16),
            pltpu.VMEM((128, 256), BF16),
            pltpu.VMEM((256, 128), BF16),
            pltpu.VMEM((256, 2 * NL), BF16),
            pltpu.VMEM((768, 1024), BF16),
            pltpu.VMEM((192, 256), BF16),
            pltpu.VMEM((256, 192), BF16),
            pltpu.VMEM((1024, 768), BF16),
            pltpu.VMEM((2 * NL, 256), BF16),
            pltpu.VMEM((384, 4 * NL), BF16),
            pltpu.VMEM((2, 3, 24, 768), BF16),
            pltpu.VMEM((2, 24, 768), BF16),
            pltpu.VMEM((2, 2, 24, 768), BF16),
            pltpu.VMEM((4, 144, 2 * NL), BF16),
            pltpu.VMEM((3, 3, 4, 144, 128), BF16),
            pltpu.VMEM((16, 64, 128), BF16),
            pltpu.VMEM((16, 64, 128), BF16),
            pltpu.VMEM((16, 48, NL), BF16),
            pltpu.VMEM((16, 48, NL), BF16),
            pltpu.VMEM((16, 48, NL), BF16),
            pltpu.VMEM((16, 48, NL), BF16),
            pltpu.VMEM((16, 64, 128), BF16),
            pltpu.VMEM((16, 64, 128), BF16),
            pltpu.VMEM((4, 144, 2 * NL), BF16),
            pltpu.VMEM((2, 3, 4, 24, 2 * NL), F32),
            pltpu.VMEM((2, 16, 128), F32),
            pltpu.VMEM((512, 256), BF16),
            pltpu.VMEM((1024, NL), BF16),
            pltpu.VMEM((512, 2 * NL), BF16),
            pltpu.VMEM((2, 64, 128), BF16),
            pltpu.VMEM((2, 128, 128), F32),
            pltpu.VMEM((128, 1024), BF16),
            pltpu.VMEM((2, 128, 16), F32),
            pltpu.VMEM((2, 128, 128), BF16),
            pltpu.VMEM((2, 128, 16), BF16),
            pltpu.VMEM((16, 512), BF16),
            pltpu.VMEM((9, 2, 128, 384), F32),
            pltpu.VMEM((2, 128, 384), F32),
            pltpu.VMEM((9, 512, 256), BF16),
            pltpu.VMEM((2, 128, 128), F32),
            pltpu.SemaphoreType.DMA((4, 16)),
            pltpu.SemaphoreType.DMA((4, 16)),
            pltpu.SemaphoreType.DMA((14,)),
            pltpu.SemaphoreType.DMA((14,)),
            pltpu.SemaphoreType.DMA((4,)),
            pltpu.SemaphoreType.DMA((4,)),
            pltpu.SemaphoreType.DMA((17,)),
            pltpu.SemaphoreType.DMA((2,)),
            pltpu.SemaphoreType.DMA((2,)),
        ],
        compiler_params=pltpu.CompilerParams(
            collective_id=0, has_side_effects=True, vmem_limit_bytes=63 * 1024 * 1024
        ),
    )(
        features.reshape(2, 128, 128),
        jnp.transpose(frac.reshape(2, 3, 128), (1, 0, 2)),
        jnp.transpose(subpoint.reshape(2, 3, 128), (1, 0, 2)),
        counts.reshape(2),
        rbf_coef,
        mesh_gain.reshape(1, 128),
        w_query,
        w_key,
        w_value,
        w_out,
        w_charge,
        w_up,
        w_down,
        mode_rows,
        *tables(),
    )
    return out.reshape(features.shape)


def solution(mesh):
    return jax.shard_map(
        per_device,
        mesh=mesh,
        in_specs=(
            P("gx", "gy", "gz", None, None),
            P("gx", "gy", "gz", None, None),
            P("gx", "gy", "gz", None, None),
            P("gx", "gy", "gz"),
            P(),
            P(),
            P(),
            P(),
            P(),
            P(),
            P(None, "gx", "gy", "gz"),
            P(),
            P(),
            P(),
        ),
        out_specs=P("gx", "gy", "gz", None, None),
        check_vma=False,
    )
```

```python
import functools
import math

import jax
import jax.numpy as jnp
import numpy as np
from jax import lax
from jax.experimental import pallas as pl
from jax.experimental.pallas import tpu as pltpu
from jax.sharding import PartitionSpec as P

MESH = pl.DeviceIdType.MESH
F32 = jnp.float32
BF16 = jnp.bfloat16

D = 128
R = 6
NRBF = 8
MX, MY, MZ = 24, 96, 48
NL = 128
LOG2E = math.log2(math.e)
NEAR = 2
XZ_STEPS = [(4, 1), (4, 0), (5, 1), (3, 1), (5, 0), (3, 0), (6, 1), (2, 1), (6, 0), (2, 0), (7, 1), (1, 1), (7, 0), (1, 0), (0, 1)]
Y_STEPS = [(0, 1), (0, 3), (1, 0), (3, 0), (1, 1), (3, 3), (1, 3), (3, 1), (0, 2), (2, 0), (1, 2), (2, 1), (3, 2), (2, 3), (2, 2)]


def tables():
    gx, ch, px = np.meshgrid(np.arange(4), np.arange(8), np.arange(8), indexing="ij")
    x_pos, x_ch = (6 * gx + px - 1).reshape(-1), ch.reshape(-1)
    lane = np.arange(NL)
    l_ch, l_kx, l_ok = lane // 16, lane % 16, lane % 16 <= MX // 2
    ang = 2 * np.pi / MX * ((x_pos[:, None] * l_kx[None, :]) % MX)
    same = (x_ch[:, None] == l_ch[None, :]) & l_ok[None, :]
    cos_x, sin_x = np.where(same, np.cos(ang), 0.0), np.where(same, np.sin(ang), 0.0)
    fwd_x = np.concatenate([cos_x, -sin_x], axis=1)
    inv_x = np.concatenate([cos_x.T, -sin_x.T], axis=0)

    row = np.arange(384)
    pair_lane = np.arange(2 * NL)
    l_ch, l_kx = pair_lane // 16, pair_lane % 16
    share = np.where(l_kx % (MX // 2) == 0, 0.5, 1.0) * (l_kx <= MX // 2)
    picks = [
        (row[:, None] == (l_ch * MX + kx)[None, :]) * share[None, :] for kx in (l_kx, (MX - l_kx) % MX)
    ]
    pick = np.concatenate(picks, axis=1)

    gz, cell, pz = np.meshgrid(np.arange(4), np.arange(2), np.arange(8), indexing="ij")
    z_pos = (12 * gz + 6 * cell + pz - 1).reshape(-1)
    ang = 2 * np.pi / MZ * ((z_pos[None, :] * np.arange(MZ)[:, None]) % MZ)
    c, s = np.cos(ang), np.sin(ang)
    mat = np.stack([np.stack([c, s], 1), np.stack([-s, c], 1)], axis=1)
    eye = np.eye(8)
    fwd_z = np.einsum("kciz,pq->kcpizq", mat, eye).reshape(MZ * 2 * 8, 2 * 64 * 8)
    mat = np.stack([np.stack([c.T, -s.T], -1), np.stack([s.T, c.T], -1)], axis=0)
    inv_z = np.einsum("czki,pq->czpkiq", mat, eye).reshape(2 * 64 * 8, MZ * 2 * 8)

    gy, py = np.meshgrid(np.arange(16), np.arange(8), indexing="ij")
    y_pos = (6 * gy + py - 1)
    ang = 2 * np.pi / MY * ((y_pos[None] * np.arange(MY)[:, None, None]) % MY)
    c, s = np.cos(ang), np.sin(ang)
    fwd_y = np.stack([np.stack([c, s], 2), np.stack([-s, c], 2)], axis=0)
    fwd_y = fwd_y.reshape(2 * MY, 256)
    ct, st = np.moveaxis(c, 0, -1), np.moveaxis(s, 0, -1)
    inv_y = np.stack([np.stack([ct, -st], 2), np.stack([st, ct], 2)], axis=1)
    inv_y = inv_y.reshape(256, 2 * MY)
    return [jnp.asarray(t, dtype=BF16) for t in (fwd_x, fwd_z, fwd_y, inv_y, inv_z, inv_x, pick)]


def dot_nn(a, b):
    return lax.dot_general(a, b, (((1,), (0,)), ((), ())), preferred_element_type=F32)


def dot_nt(a, b):
    return lax.dot_general(a, b, (((1,), (1,)), ((), ())), preferred_element_type=F32)


def dot_tn(a, b):
    return lax.dot_general(a, b, (((0,), (0,)), ((), ())), preferred_element_type=F32)


def swap_halves(first, second):
    low = lax.broadcasted_iota(jnp.int32, first.shape, 1) < 64
    return (
        jnp.where(low, first, pltpu.roll(second, 64, 1)),
        jnp.where(low, pltpu.roll(first, 64, 1), second),
    )


def stencil(point, sub, frac):
    offset = point - 1.0 - sub
    lower_w = 0.5 * (0.5 - frac) * (0.5 - frac)
    centre_w = 0.75 - frac * frac
    upper_w = 0.5 * (0.5 + frac) * (0.5 + frac)
    zero = jnp.zeros_like(offset)
    return jnp.where(
        offset == -1.0,
        lower_w,
        jnp.where(offset == 0.0, centre_w, jnp.where(offset == 1.0, upper_w, zero)),
    )


def split3(value):
    high = value.astype(BF16).astype(F32)
    rest = value - high
    middle = rest.astype(BF16).astype(F32)
    return high, middle, rest - middle


def kernel(
    feat_hbm,
    frac_ref,
    sub_ref,
    counts_ref,
    coef_ref,
    gain_ref,
    wq_hbm,
    wk_hbm,
    wv_hbm,
    wo_hbm,
    wch_hbm,
    wup_hbm,
    wdown_hbm,
    mode_hbm,
    fx_hbm,
    fz_hbm,
    fy_hbm,
    iy_hbm,
    iz_hbm,
    ix_hbm,
    pick_hbm,
    out_ref,
    feat_ref,
    wq_ref,
    wk_ref,
    wv_ref,
    wo_ref,
    wch_ref,
    wup_ref,
    wdown_ref,
    fx_ref,
    fz_ref,
    fy_ref,
    iy_ref,
    iz_ref,
    ix_ref,
    pick_ref,
    mode_own,
    mode_first,
    mode_rest,
    wsend,
    halo,
    s1,
    r1,
    s2,
    r2,
    s3,
    r3,
    s4,
    r4,
    wrecv,
    aux,
    x1,
    t2,
    v2,
    wyz,
    wx,
    rep,
    cols,
    qs,
    qaug,
    kaug,
    scores,
    dist,
    vext,
    smax,
    send_sem,
    recv_sem,
    hsend,
    hrecv,
    wsem,
    wrsem,
    lsem,
    psend,
    precv,
):
    gx, gy, gz = lax.axis_index("gx"), lax.axis_index("gy"), lax.axis_index("gz")
    me_xz = gz * 4 + gx

    def dev_xz(p):
        return {"gx": lax.rem(p, 4), "gz": lax.div(p, 4)}

    def dev_y(p):
        return {"gy": p}

    def remote(src, dst, ssem, rsem, device):
        return pltpu.make_async_remote_copy(
            src_ref=src, dst_ref=dst, send_sem=ssem, recv_sem=rsem, device_id=device, device_id_type=MESH
        )

    z_chip, core = lax.div(gx, 2) * 4 + gz, lax.rem(gx, 2)
    far_xz, near_y = [], []
    for step, other in XZ_STEPS:
        z = lax.rem(z_chip + step, 8)
        far_xz.append(lax.rem(z, 4) * 4 + lax.div(z, 4) * 2 + (core if other == 0 else 1 - core))
    for step_x, step_y in Y_STEPS:
        near_y.append(lax.rem(lax.div(gy, 4) + step_x, 4) * 4 + lax.rem(lax.rem(gy, 4) + step_y, 4))
    barrier = pltpu.get_barrier_semaphore()
    for p in far_xz:
        pl.semaphore_signal(barrier, inc=1, device_id=dev_xz(p), device_id_type=MESH)
    for p in near_y[::-1]:
        pl.semaphore_signal(barrier, inc=1, device_id=dev_y(p), device_id_type=MESH)

    loads = {}

    def load(index, name, src, dst):
        loads[name] = pltpu.make_async_copy(src, dst, lsem.at[index])
        loads[name].start()

    load(0, "feat", feat_hbm, feat_ref)
    load(1, "wch", wch_hbm, wch_ref)
    load(2, "wq", wq_hbm, wq_ref)
    load(3, "fx", fx_hbm, fx_ref)
    load(4, "fz", fz_hbm, fz_ref)
    load(5, "wk", wk_hbm, wk_ref)
    load(6, "wv", wv_hbm, wv_ref)
    load(7, "mode", mode_hbm, mode_own)
    load(15, "pick", pick_hbm, pick_ref)
    load(8, "fy", fy_hbm, fy_ref)
    load(9, "iy", iy_hbm, iy_ref)
    load(10, "iz", iz_hbm, iz_ref)
    load(11, "ix", ix_hbm, ix_ref)
    load(12, "wo", wo_hbm, wo_ref)
    load(13, "wup", wup_hbm, wup_ref)
    load(14, "wdown", wdown_hbm, wdown_ref)

    mine = lax.div(gx, 2)
    lane_row = lax.broadcasted_iota(jnp.int32, (1, 128), 1)
    aux[...] = jnp.zeros_like(aux)
    for c in range(2):
        sub = jnp.concatenate([sub_ref[d, c : c + 1, :] for d in range(3)], axis=0).astype(F32)
        frac = jnp.concatenate([frac_ref[d, c : c + 1, :].astype(F32) for d in range(3)], axis=0)
        aux[c, 0:3, :] = ((sub + 0.5 + frac) / R).astype(BF16).astype(F32)
        aux[c, 3:4, :] = (lane_row < counts_ref[c]).astype(F32)
        aux[c, 4:7, :] = frac
        aux[c, 7:10, :] = sub
        halo[1, mine, 1 + c, 128:144, :] = aux[c].astype(BF16)
    loads["feat"].wait()
    for c in range(2):
        halo[1, mine, 1 + c, 0:128, :] = feat_ref[c]

    row_i = lax.broadcasted_iota(jnp.int32, (128, 1024), 0)
    lane_i = lax.broadcasted_iota(jnp.int32, (128, 1024), 1)
    rep[...] = (lax.shift_right_logical(lane_i, 3) == row_i).astype(F32).astype(BF16)
    eye = (
        lax.broadcasted_iota(jnp.int32, (128, 128), 0) == lax.broadcasted_iota(jnp.int32, (128, 128), 1)
    ).astype(F32).astype(BF16)
    loads["wch"].wait()
    wch = dot_nn(wch_ref[...], rep[...]).astype(BF16)
    point_rows = lax.broadcasted_iota(jnp.int32, (8, 128), 0).astype(F32)
    point_lanes = lax.bitwise_and(lax.broadcasted_iota(jnp.int32, (128, 128), 1), 7).astype(F32)
    spread = []
    for c in range(2):
        cols[c] = dot_nt(eye, aux[c].astype(BF16))
        col = cols[c]
        wy = stencil(point_rows, aux[c, 8:9, :], aux[c, 5:6, :])
        wz = stencil(point_rows, aux[c, 9:10, :], aux[c, 6:7, :])
        wyz[c] = jnp.concatenate([wz[p : p + 1, :] * wy for p in range(8)], axis=0).astype(BF16)
        wx[c] = stencil(point_lanes, col[:, 7:8], col[:, 4:5])
        wxv = wx[c] * col[:, 3:4]
        charge = dot_nn(feat_ref[c], wch)
        scaled = jnp.concatenate(
            [charge[:, 128 * t : 128 * t + 128] * wxv for t in range(8)], axis=1
        ).astype(BF16)
        spread.append(dot_nn(wyz[c], scaled))
    for t in range(8):
        even, odd = swap_halves(
            spread[0][:, 128 * t : 128 * t + 128], spread[1][:, 128 * t : 128 * t + 128]
        )
        s1[2 * t] = even.astype(BF16)
        s1[2 * t + 1] = odd.astype(BF16)

    def exchange(phase, src, dst, me, device, partners):
        copies = []
        for k, p in enumerate(partners):
            copy = remote(src.at[p], dst.at[me], send_sem.at[phase, k], recv_sem.at[phase, k], device(p))
            copy.start()
            copies.append(copy)
        dst[me] = src[me]
        return copies

    pl.semaphore_wait(barrier, 30)
    phase1 = exchange(0, s1, r1, me_xz, dev_xz, far_xz)

    mirror, is_own = lax.rem(16 - gy, 16), lax.rem(gy, 8) == 0
    first_local = pltpu.make_async_copy(mode_hbm.at[:, 0], mode_first, lsem.at[16])
    first_copy = remote(mode_hbm.at[:, 0], mode_first, psend.at[0], precv.at[0], dev_y(mirror))
    rest_copy = remote(mode_hbm.at[:, pl.ds(1, 2)], mode_rest, psend.at[1], precv.at[1], dev_y(15 - gy))

    @pl.when(is_own)
    def _():
        first_local.start()

    @pl.when(jnp.logical_not(is_own))
    def _():
        first_copy.start()

    rest_copy.start()

    halo_copies = []

    def halo_send(index, src, dst, device):
        copy = remote(src, dst, hsend.at[index], hrecv.at[index], device)
        copy.start()
        halo_copies.append(copy)
        return copy

    own_slot, far_slot = mine, 1 - mine
    inner = pl.ds(1, 2)
    own = halo.at[1, own_slot, inner]
    up_y, down_y = dev_y(lax.rem(gy + 1, 16)), dev_y(lax.rem(gy + 15, 16))
    up_z, down_z = {"gz": lax.rem(gz + 1, 4)}, {"gz": lax.rem(gz + 3, 4)}

    def send_z(index, slot):
        return [
            halo_send(index, halo.at[1, slot, 2], halo.at[1, slot, 0], up_z),
            halo_send(index + 1, halo.at[1, slot, 1], halo.at[1, slot, 3], down_z),
        ]

    def send_y(index, slot, cells):
        return [
            halo_send(index, halo.at[1, slot, cells], halo.at[0, slot, cells], up_y),
            halo_send(index + 1, halo.at[1, slot, cells], halo.at[2, slot, cells], down_y),
        ]

    own_y = send_y(2, own_slot, inner)

    loads["wq"].wait()
    for c in range(2):
        qs[c] = dot_nn(feat_ref[c], wq_ref[...]).astype(BF16)
        pos = aux[c, 0:3, :]
        qx, qy, qz = pos[0:1, :], pos[1:2, :], pos[2:3, :] + float(c)
        norm = split3(qx * qx + qy * qy + qz * qz)
        one = jnp.ones((1, 128), F32)
        rows = jnp.concatenate(
            [-2.0 * pos, -2.0 * pos, one, one, one, *norm, -2.0 * c * one, -2.0 * c * one, 0.0 * one, 0.0 * one],
            axis=0,
        )
        qaug[c] = dot_nt(eye, rows.astype(BF16)).astype(BF16)
        smax[c] = jnp.full((128, 128), -jnp.inf, F32)

    for copy in phase1:
        copy.wait_send()
    own_z = send_z(0, own_slot)
    far_copy = halo_send(4, own, own, {"gx": 3 - gx})
    loads["mode"].wait()
    loads["pick"].wait()
    at_k = mode_own[...].astype(F32).reshape(144, 768).astype(BF16)
    for t in range(2):
        picked = dot_nn(at_k[:, 384 * t : 384 * t + 384], pick_ref[:, 0 : 2 * NL]).astype(BF16)
        for e in range(2):
            wsend[2 * t + e, :, 0:NL] = picked[:, NL * e : NL * e + NL]

    @pl.when(is_own)
    def _():
        first_local.wait()

    @pl.when(jnp.logical_not(is_own))
    def _():
        first_copy.wait()

    rest_copy.wait()
    first = mode_first[...].astype(F32).reshape(2, 1, 24, 768)
    rest = mode_rest[...].astype(F32)
    at_minus_k = jnp.concatenate([first, rest[:, 1:2], rest[:, 0:1]], axis=1).reshape(144, 768).astype(BF16)
    for t in range(2):
        picked = dot_nn(at_minus_k[:, 384 * t : 384 * t + 384], pick_ref[:, 2 * NL : 4 * NL]).astype(BF16)
        for e in range(2):
            wsend[2 * t + e, :, NL : 2 * NL] = picked[:, NL * e : NL * e + NL]
    weights = []
    for off in (2, 1, 3):
        p = lax.rem(gx + off, 4)
        copy = remote(wsend.at[p], wrecv.at[gx], wsem.at[off], wrsem.at[off], {"gx": p})
        copy.start()
        weights.append(copy)
    wrecv[gx] = wsend[gx]

    for copy in phase1:
        copy.wait_recv()
    for g in range(4):
        for t in range(2):
            first, second = swap_halves(r1[4 * g + 2 * t].astype(F32), r1[4 * g + 2 * t + 1].astype(F32))
            x1[128 * g : 128 * g + 64, 128 * t : 128 * t + 128] = first.astype(BF16)
            x1[128 * g + 64 : 128 * g + 128, 128 * t : 128 * t + 128] = second.astype(BF16)
    loads["fx"].wait()
    loads["fz"].wait()
    field = dot_nn(x1[...], fx_ref[...]).astype(BF16)
    t2[0:512, :] = field[:, 0:NL]
    t2[512:1024, :] = field[:, NL : 2 * NL]
    s2[...] = dot_nn(fz_ref[...], t2[...]).astype(BF16).reshape(16, 48, NL)
    phase2 = exchange(1, s2, r2, gy, dev_y, near_y)

    for copy in own_z:
        copy.wait_recv()
    own_y += send_y(5, own_slot, 0) + send_y(7, own_slot, 3)
    odd_core = lax.rem(gx, 2)
    near_step = (1 - 2 * odd_core).astype(F32)

    coef = [coef_ref[k] * LOG2E for k in range(NRBF)]
    scale = LOG2E / math.sqrt(D)

    def score_slab(y, x):
        slab = 3 * y + x
        feats = halo[y, x, :, 0:128, :].reshape(512, 128)
        keys = dot_nn(feats, wk_ref[...]).astype(BF16)
        vext[slab, :, 0:128] = dot_nn(feats, wv_ref[...]).astype(BF16)
        vext[slab, :, 128:256] = jnp.ones((512, 128), BF16)
        off_x = 0.0 if x is own_slot else (near_step if x is NEAR else -near_step)
        off_y = float(y - 1)
        one = jnp.ones((1, 128), F32)
        masks = []
        for z in range(4):
            rows = halo[y, x, z, 128:144, :].astype(F32)
            pos = rows[0:3, :]
            kx, ky, kz = pos[0:1, :] + off_x, pos[1:2, :] + off_y, pos[2:3, :] + float(z - 1)
            norm = split3(kx * kx + ky * ky + kz * kz)
            kaug[:, 128 * z : 128 * z + 128] = jnp.concatenate(
                [
                    pos, off_x * one, off_y * one, float(z - 1) * one, *norm, one, one, one,
                    pos[2:3, :], float(z - 1) * one, 0.0 * one, 0.0 * one,
                ],
                axis=0,
            ).astype(BF16)
            masks.append(jnp.where(rows[3:4, :] > 0.5, 0.0, -jnp.inf))
        mask = jnp.concatenate(masks, axis=1)
        for c in range(2):
            scores[slab, c] = dot_nt(qs[c], keys[128 * c : 128 * c + 384, :])
            dist[c] = dot_nn(qaug[c], kaug[:, 128 * c : 128 * c + 384])
            for r in range(0, 128, 16):
                t = jnp.exp2(dist[c, r : r + 16, :] * (-0.08 * LOG2E))
                powers = [t]
                for k in range(NRBF - 2):
                    powers.append(powers[-1] * powers[-1])
                bias = coef[NRBF - 1] * powers[-1] + coef[NRBF - 2]
                for k in range(NRBF - 3, -1, -1):
                    bias = bias * powers[k] + coef[k]
                bias = bias * t
                full = scores[slab, c, r : r + 16, :] * scale + bias + mask[:, 128 * c : 128 * c + 384]
                scores[slab, c, r : r + 16, :] = full
                top = jnp.maximum(jnp.maximum(full[:, 0:128], full[:, 128:256]), full[:, 256:384])
                smax[c, r : r + 16, :] = jnp.maximum(smax[c, r : r + 16, :], top)

    loads["wk"].wait()
    loads["wv"].wait()
    score_slab(1, own_slot)

    for copy in weights:
        copy.wait_recv()
    for name in ("fy", "iy"):
        loads[name].wait()
    received = [wrecv[q].astype(F32) for q in range(4)]

    def lines_of(first_lane):
        return [
            jnp.concatenate(
                [received[q][24 * i : 24 * i + 24, first_lane : first_lane + NL] for q in range(4)], axis=0
            )
            for i in range(6)
        ]

    place = lax.broadcasted_iota(jnp.int32, (MY, MY), 0) + lax.broadcasted_iota(jnp.int32, (MY, MY), 1)
    flip = jnp.logical_or(place == 0, place == MY).astype(F32).astype(BF16)
    minus = dot_nn(flip, jnp.concatenate(lines_of(NL), axis=1).astype(BF16))
    plus = jnp.concatenate(lines_of(0), axis=1)
    norm = 1.0 / (MX * MY * MZ)
    w_real = (plus[:, 0 : 3 * NL] + minus[:, 0 : 3 * NL]) * norm
    w_imag = (plus[:, 3 * NL : 6 * NL] - minus[:, 3 * NL : 6 * NL]) * norm
    for copy in phase2:
        copy.wait_recv()
    lines = jnp.concatenate([r2[:, 16 * j : 16 * j + 16, :].reshape(256, NL) for j in range(3)], axis=1)
    spectrum = dot_nn(fy_ref[...], lines)
    real, imag = spectrum[0:MY, :], spectrum[MY : 2 * MY, :]
    mixed = jnp.concatenate(
        [real * w_real - imag * w_imag, real * w_imag + imag * w_real], axis=0
    ).astype(BF16)
    lines = dot_nn(iy_ref[...], mixed).astype(BF16)
    for j in range(3):
        s3[:, 16 * j : 16 * j + 16, :] = lines[:, NL * j : NL * j + NL].reshape(16, 16, NL)
    phase3 = exchange(2, s3, r3, gy, dev_y, near_y)

    for copy in own_y:
        copy.wait_recv()
    near = halo_send(13, halo.at[:, own_slot], halo.at[:, NEAR], {"gx": gx + 1 - 2 * odd_core})
    far_copy.wait_recv()
    far_z = send_z(9, far_slot)
    score_slab(0, own_slot)
    score_slab(2, own_slot)
    near.wait_recv()
    for y in range(3):
        score_slab(y, NEAR)
    for copy in far_z:
        copy.wait_recv()
    far_y = send_y(11, far_slot, pl.ds(0, 4))

    for copy in phase3:
        copy.wait_recv()
    loads["iz"].wait()
    loads["ix"].wait()
    back = dot_nn(iz_ref[...], r3[...].reshape(768, NL)).astype(BF16)
    v2[:, 0:NL] = back[0:512, :]
    v2[:, NL : 2 * NL] = back[512:1024, :]
    potential = dot_nn(v2[...], ix_ref[...])
    for g in range(4):
        for t in range(2):
            even, odd = swap_halves(
                potential[128 * g : 128 * g + 64, 128 * t : 128 * t + 128],
                potential[128 * g + 64 : 128 * g + 128, 128 * t : 128 * t + 128],
            )
            s4[4 * g + 2 * t] = even.astype(BF16)
            s4[4 * g + 2 * t + 1] = odd.astype(BF16)
    phase4 = exchange(3, s4, r4, me_xz, dev_xz, far_xz)

    score_slab(1, far_slot)
    for copy in far_y:
        copy.wait_recv()
    score_slab(0, far_slot)
    score_slab(2, far_slot)
    after = []
    for name in ("wo", "wup", "wdown"):
        loads[name].wait()
    for c in range(2):
        top = jnp.max(smax[c], axis=1, keepdims=True)

        def mix(slab, acc, c=c, top=top):
            probs = jnp.exp2(scores[slab, c] - top).astype(BF16)
            return acc + dot_nn(probs, vext[slab, 128 * c : 128 * c + 384, :])

        acc = lax.fori_loop(0, 9, mix, jnp.zeros((128, 256), F32))
        attended = (acc[:, 0:128] / acc[:, 128:256]).astype(BF16)
        after.append(feat_ref[c].astype(F32) + dot_nn(attended, wo_ref[...]))

    for copy in phase4:
        copy.wait_recv()
    fields = [[], []]
    for t in range(8):
        first, second = swap_halves(r4[2 * t].astype(F32), r4[2 * t + 1].astype(F32))
        fields[0].append(first.astype(BF16))
        fields[1].append(second.astype(BF16))
    for c in range(2):
        lines = dot_tn(wyz[c], jnp.concatenate(fields[c], axis=1))
        lines = jnp.concatenate(
            [lines[:, 128 * t : 128 * t + 128] * wx[c] for t in range(8)], axis=1
        ).astype(BF16)
        sampled = dot_nt(lines, rep[...])
        norm_scale = lax.rsqrt(jnp.mean(sampled * sampled, axis=1, keepdims=True) + 1e-06)
        joined = after[c] + sampled * norm_scale * gain_ref[...]
        inner = dot_nn(joined.astype(BF16), wup_ref[...])
        inner = (inner * jax.nn.sigmoid(inner)).astype(BF16)
        result = joined + dot_nn(inner, wdown_ref[...])
        out_ref[c] = jnp.where(cols[c][:, 3:4] > 0.5, result, 0.0).astype(BF16)

    for copy in phase2 + phase3 + phase4 + weights + halo_copies:
        copy.wait_send()


def per_device(
    features,
    frac,
    subpoint,
    counts,
    w_query,
    w_key,
    w_value,
    rbf_coef,
    w_out,
    w_charge,
    mode_weight,
    mesh_gain,
    w_up,
    w_down,
):
    mode_rows = jnp.transpose(mode_weight, (0, 2, 1, 3))
    vmem = pl.BlockSpec(memory_space=pltpu.VMEM)
    smem = pl.BlockSpec(memory_space=pltpu.SMEM)
    hbm = pl.BlockSpec(memory_space=pltpu.HBM)
    out = pl.pallas_call(
        kernel,
        out_shape=jax.ShapeDtypeStruct((2, 128, 128), BF16),
        in_specs=[hbm, vmem, vmem, smem, smem, vmem] + [hbm] * 15,
        out_specs=vmem,
        scratch_shapes=[
            pltpu.VMEM((2, 128, 128), BF16),
            pltpu.VMEM((128, 128), BF16),
            pltpu.VMEM((128, 128), BF16),
            pltpu.VMEM((128, 128), BF16),
            pltpu.VMEM((128, 128), BF16),
            pltpu.VMEM((128, 128), BF16),
            pltpu.VMEM((128, 256), BF16),
            pltpu.VMEM((256, 128), BF16),
            pltpu.VMEM((256, 2 * NL), BF16),
            pltpu.VMEM((768, 1024), BF16),
            pltpu.VMEM((192, 256), BF16),
            pltpu.VMEM((256, 192), BF16),
            pltpu.VMEM((1024, 768), BF16),
            pltpu.VMEM((2 * NL, 256), BF16),
            pltpu.VMEM((384, 4 * NL), BF16),
            pltpu.VMEM((2, 3, 24, 768), BF16),
            pltpu.VMEM((2, 24, 768), BF16),
            pltpu.VMEM((2, 2, 24, 768), BF16),
            pltpu.VMEM((4, 144, 2 * NL), BF16),
            pltpu.VMEM((3, 3, 4, 144, 128), BF16),
            pltpu.VMEM((16, 64, 128), BF16),
            pltpu.VMEM((16, 64, 128), BF16),
            pltpu.VMEM((16, 48, NL), BF16),
            pltpu.VMEM((16, 48, NL), BF16),
            pltpu.VMEM((16, 48, NL), BF16),
            pltpu.VMEM((16, 48, NL), BF16),
            pltpu.VMEM((16, 64, 128), BF16),
            pltpu.VMEM((16, 64, 128), BF16),
            pltpu.VMEM((4, 144, 2 * NL), BF16),
            pltpu.VMEM((2, 16, 128), F32),
            pltpu.VMEM((512, 256), BF16),
            pltpu.VMEM((1024, NL), BF16),
            pltpu.VMEM((512, 2 * NL), BF16),
            pltpu.VMEM((2, 64, 128), BF16),
            pltpu.VMEM((2, 128, 128), F32),
            pltpu.VMEM((128, 1024), BF16),
            pltpu.VMEM((2, 128, 16), F32),
            pltpu.VMEM((2, 128, 128), BF16),
            pltpu.VMEM((2, 128, 16), BF16),
            pltpu.VMEM((16, 512), BF16),
            pltpu.VMEM((9, 2, 128, 384), F32),
            pltpu.VMEM((2, 128, 384), F32),
            pltpu.VMEM((9, 512, 256), BF16),
            pltpu.VMEM((2, 128, 128), F32),
            pltpu.SemaphoreType.DMA((4, 16)),
            pltpu.SemaphoreType.DMA((4, 16)),
            pltpu.SemaphoreType.DMA((14,)),
            pltpu.SemaphoreType.DMA((14,)),
            pltpu.SemaphoreType.DMA((4,)),
            pltpu.SemaphoreType.DMA((4,)),
            pltpu.SemaphoreType.DMA((17,)),
            pltpu.SemaphoreType.DMA((2,)),
            pltpu.SemaphoreType.DMA((2,)),
        ],
        compiler_params=pltpu.CompilerParams(
            collective_id=0, has_side_effects=True, vmem_limit_bytes=63 * 1024 * 1024
        ),
    )(
        features.reshape(2, 128, 128),
        jnp.transpose(frac.reshape(2, 3, 128), (1, 0, 2)),
        jnp.transpose(subpoint.reshape(2, 3, 128), (1, 0, 2)),
        counts.reshape(2),
        rbf_coef,
        mesh_gain.reshape(1, 128),
        w_query,
        w_key,
        w_value,
        w_out,
        w_charge,
        w_up,
        w_down,
        mode_rows,
        *tables(),
    )
    return out.reshape(features.shape)


def solution(mesh):
    return jax.shard_map(
        per_device,
        mesh=mesh,
        in_specs=(
            P("gx", "gy", "gz", None, None),
            P("gx", "gy", "gz", None, None),
            P("gx", "gy", "gz", None, None),
            P("gx", "gy", "gz"),
            P(),
            P(),
            P(),
            P(),
            P(),
            P(),
            P(None, "gx", "gy", "gz"),
            P(),
            P(),
            P(),
        ),
        out_specs=P("gx", "gy", "gz", None, None),
        check_vma=False,
    )
```

```python
import functools
import math

import jax
import jax.numpy as jnp
import numpy as np
from jax import lax
from jax.experimental import pallas as pl
from jax.experimental.pallas import tpu as pltpu
from jax.sharding import PartitionSpec as P

MESH = pl.DeviceIdType.MESH
F32 = jnp.float32
BF16 = jnp.bfloat16

D = 128
R = 6
NRBF = 8
MX, MY, MZ = 24, 96, 48
NL = 128
LOG2E = math.log2(math.e)
NEAR = 2
XZ_STEPS = [(4, 1), (4, 0), (5, 1), (3, 1), (5, 0), (3, 0), (6, 1), (2, 1), (6, 0), (2, 0), (7, 1), (1, 1), (7, 0), (1, 0), (0, 1)]
Y_STEPS = [(0, 1), (0, 3), (1, 0), (3, 0), (1, 1), (3, 3), (1, 3), (3, 1), (0, 2), (2, 0), (1, 2), (2, 1), (3, 2), (2, 3), (2, 2)]


def tables():
    gx, ch, px = np.meshgrid(np.arange(4), np.arange(8), np.arange(8), indexing="ij")
    x_pos, x_ch = (6 * gx + px - 1).reshape(-1), ch.reshape(-1)
    lane = np.arange(NL)
    l_ch, l_kx, l_ok = lane // 16, lane % 16, lane % 16 <= MX // 2
    ang = 2 * np.pi / MX * ((x_pos[:, None] * l_kx[None, :]) % MX)
    same = (x_ch[:, None] == l_ch[None, :]) & l_ok[None, :]
    cos_x, sin_x = np.where(same, np.cos(ang), 0.0), np.where(same, np.sin(ang), 0.0)
    fwd_x = np.concatenate([cos_x, -sin_x], axis=1)
    inv_x = np.concatenate([cos_x.T, -sin_x.T], axis=0)

    row = np.arange(384)
    pair_lane = np.arange(2 * NL)
    l_ch, l_kx = pair_lane // 16, pair_lane % 16
    share = np.where(l_kx % (MX // 2) == 0, 0.5, 1.0) * (l_kx <= MX // 2)
    picks = [
        (row[:, None] == (l_ch * MX + kx)[None, :]) * share[None, :] for kx in (l_kx, (MX - l_kx) % MX)
    ]
    pick = np.concatenate(picks, axis=1)

    gz, cell, pz = np.meshgrid(np.arange(4), np.arange(2), np.arange(8), indexing="ij")
    z_pos = (12 * gz + 6 * cell + pz - 1).reshape(-1)
    ang = 2 * np.pi / MZ * ((z_pos[None, :] * np.arange(MZ)[:, None]) % MZ)
    c, s = np.cos(ang), np.sin(ang)
    mat = np.stack([np.stack([c, s], 1), np.stack([-s, c], 1)], axis=1)
    eye = np.eye(8)
    fwd_z = np.einsum("kciz,pq->kcpizq", mat, eye).reshape(MZ * 2 * 8, 2 * 64 * 8)
    mat = np.stack([np.stack([c.T, -s.T], -1), np.stack([s.T, c.T], -1)], axis=0)
    inv_z = np.einsum("czki,pq->czpkiq", mat, eye).reshape(2 * 64 * 8, MZ * 2 * 8)

    gy, py = np.meshgrid(np.arange(16), np.arange(8), indexing="ij")
    y_pos = (6 * gy + py - 1)
    ang = 2 * np.pi / MY * ((y_pos[None] * np.arange(MY)[:, None, None]) % MY)
    c, s = np.cos(ang), np.sin(ang)
    fwd_y = np.stack([np.stack([c, s], 2), np.stack([-s, c], 2)], axis=0)
    fwd_y = fwd_y.reshape(2 * MY, 256)
    ct, st = np.moveaxis(c, 0, -1), np.moveaxis(s, 0, -1)
    inv_y = np.stack([np.stack([ct, -st], 2), np.stack([st, ct], 2)], axis=1)
    inv_y = inv_y.reshape(256, 2 * MY)
    return [jnp.asarray(t, dtype=BF16) for t in (fwd_x, fwd_z, fwd_y, inv_y, inv_z, inv_x, pick)]


def dot_nn(a, b):
    return lax.dot_general(a, b, (((1,), (0,)), ((), ())), preferred_element_type=F32)


def dot_nt(a, b):
    return lax.dot_general(a, b, (((1,), (1,)), ((), ())), preferred_element_type=F32)


def dot_tn(a, b):
    return lax.dot_general(a, b, (((0,), (0,)), ((), ())), preferred_element_type=F32)


def swap_halves(first, second):
    low = lax.broadcasted_iota(jnp.int32, first.shape, 1) < 64
    return (
        jnp.where(low, first, pltpu.roll(second, 64, 1)),
        jnp.where(low, pltpu.roll(first, 64, 1), second),
    )


def stencil(point, sub, frac):
    offset = point - 1.0 - sub
    lower_w = 0.5 * (0.5 - frac) * (0.5 - frac)
    centre_w = 0.75 - frac * frac
    upper_w = 0.5 * (0.5 + frac) * (0.5 + frac)
    zero = jnp.zeros_like(offset)
    return jnp.where(
        offset == -1.0,
        lower_w,
        jnp.where(offset == 0.0, centre_w, jnp.where(offset == 1.0, upper_w, zero)),
    )


def split3(value):
    high = value.astype(BF16).astype(F32)
    rest = value - high
    middle = rest.astype(BF16).astype(F32)
    return high, middle, rest - middle


def kernel(
    feat_hbm,
    frac_ref,
    sub_ref,
    counts_ref,
    coef_ref,
    gain_ref,
    wq_hbm,
    wk_hbm,
    wv_hbm,
    wo_hbm,
    wch_hbm,
    wup_hbm,
    wdown_hbm,
    mode_hbm,
    fx_hbm,
    fz_hbm,
    fy_hbm,
    iy_hbm,
    iz_hbm,
    ix_hbm,
    pick_hbm,
    out_ref,
    feat_ref,
    wq_ref,
    wk_ref,
    wv_ref,
    wo_ref,
    wch_ref,
    wup_ref,
    wdown_ref,
    fx_ref,
    fz_ref,
    fy_ref,
    iy_ref,
    iz_ref,
    ix_ref,
    pick_ref,
    mode_own,
    mode_first,
    mode_rest,
    wsend,
    halo,
    s1,
    r1,
    s2,
    r2,
    s3,
    r3,
    s4,
    r4,
    wrecv,
    aux,
    x1,
    t2,
    v2,
    wyz,
    wx,
    rep,
    cols,
    qs,
    qaug,
    kaug,
    scores,
    dist,
    vext,
    smax,
    send_sem,
    recv_sem,
    hsend,
    hrecv,
    wsem,
    wrsem,
    lsem,
    psend,
    precv,
):
    gx, gy, gz = lax.axis_index("gx"), lax.axis_index("gy"), lax.axis_index("gz")
    me_xz = gz * 4 + gx

    def dev_xz(p):
        return {"gx": lax.rem(p, 4), "gz": lax.div(p, 4)}

    def dev_y(p):
        return {"gy": p}

    def remote(src, dst, ssem, rsem, device):
        return pltpu.make_async_remote_copy(
            src_ref=src, dst_ref=dst, send_sem=ssem, recv_sem=rsem, device_id=device, device_id_type=MESH
        )

    z_chip, core = lax.div(gx, 2) * 4 + gz, lax.rem(gx, 2)
    far_xz, near_y = [], []
    for step, other in XZ_STEPS:
        z = lax.rem(z_chip + step, 8)
        far_xz.append(lax.rem(z, 4) * 4 + lax.div(z, 4) * 2 + (core if other == 0 else 1 - core))
    for step_x, step_y in Y_STEPS:
        near_y.append(lax.rem(lax.div(gy, 4) + step_x, 4) * 4 + lax.rem(lax.rem(gy, 4) + step_y, 4))
    barrier = pltpu.get_barrier_semaphore()
    for p in far_xz:
        pl.semaphore_signal(barrier, inc=1, device_id=dev_xz(p), device_id_type=MESH)
    for p in near_y[::-1]:
        pl.semaphore_signal(barrier, inc=1, device_id=dev_y(p), device_id_type=MESH)

    loads = {}

    def load(index, name, src, dst):
        loads[name] = pltpu.make_async_copy(src, dst, lsem.at[index])
        loads[name].start()

    load(0, "feat", feat_hbm, feat_ref)
    load(1, "wch", wch_hbm, wch_ref)
    load(2, "wq", wq_hbm, wq_ref)
    load(3, "fx", fx_hbm, fx_ref)
    load(4, "fz", fz_hbm, fz_ref)
    load(5, "wk", wk_hbm, wk_ref)
    load(6, "wv", wv_hbm, wv_ref)
    load(7, "mode", mode_hbm, mode_own)
    load(15, "pick", pick_hbm, pick_ref)
    load(8, "fy", fy_hbm, fy_ref)
    load(9, "iy", iy_hbm, iy_ref)
    load(10, "iz", iz_hbm, iz_ref)
    load(11, "ix", ix_hbm, ix_ref)
    load(12, "wo", wo_hbm, wo_ref)
    load(13, "wup", wup_hbm, wup_ref)
    load(14, "wdown", wdown_hbm, wdown_ref)

    mine = lax.div(gx, 2)
    lane_row = lax.broadcasted_iota(jnp.int32, (1, 128), 1)
    aux[...] = jnp.zeros_like(aux)
    for c in range(2):
        sub = jnp.concatenate([sub_ref[d, c : c + 1, :] for d in range(3)], axis=0).astype(F32)
        frac = jnp.concatenate([frac_ref[d, c : c + 1, :].astype(F32) for d in range(3)], axis=0)
        aux[c, 0:3, :] = ((sub + 0.5 + frac) / R).astype(BF16).astype(F32)
        aux[c, 3:4, :] = (lane_row < counts_ref[c]).astype(F32)
        aux[c, 4:7, :] = frac
        aux[c, 7:10, :] = sub
        halo[1, mine, 1 + c, 128:144, :] = aux[c].astype(BF16)
    loads["feat"].wait()
    for c in range(2):
        halo[1, mine, 1 + c, 0:128, :] = feat_ref[c]

    row_i = lax.broadcasted_iota(jnp.int32, (128, 1024), 0)
    lane_i = lax.broadcasted_iota(jnp.int32, (128, 1024), 1)
    rep[...] = (lax.shift_right_logical(lane_i, 3) == row_i).astype(F32).astype(BF16)
    eye = (
        lax.broadcasted_iota(jnp.int32, (128, 128), 0) == lax.broadcasted_iota(jnp.int32, (128, 128), 1)
    ).astype(F32).astype(BF16)
    loads["wch"].wait()
    wch = dot_nn(wch_ref[...], rep[...]).astype(BF16)
    point_rows = lax.broadcasted_iota(jnp.int32, (8, 128), 0).astype(F32)
    point_lanes = lax.bitwise_and(lax.broadcasted_iota(jnp.int32, (128, 128), 1), 7).astype(F32)
    spread = []
    for c in range(2):
        cols[c] = dot_nt(eye, aux[c].astype(BF16))
        col = cols[c]
        wy = stencil(point_rows, aux[c, 8:9, :], aux[c, 5:6, :])
        wz = stencil(point_rows, aux[c, 9:10, :], aux[c, 6:7, :])
        wyz[c] = jnp.concatenate([wz[p : p + 1, :] * wy for p in range(8)], axis=0).astype(BF16)
        wx[c] = stencil(point_lanes, col[:, 7:8], col[:, 4:5])
        wxv = wx[c] * col[:, 3:4]
        charge = dot_nn(feat_ref[c], wch)
        scaled = jnp.concatenate(
            [charge[:, 128 * t : 128 * t + 128] * wxv for t in range(8)], axis=1
        ).astype(BF16)
        spread.append(dot_nn(wyz[c], scaled))
    for t in range(8):
        even, odd = swap_halves(
            spread[0][:, 128 * t : 128 * t + 128], spread[1][:, 128 * t : 128 * t + 128]
        )
        s1[2 * t] = even.astype(BF16)
        s1[2 * t + 1] = odd.astype(BF16)

    def exchange(phase, src, dst, me, device, partners):
        copies = []
        for k, p in enumerate(partners):
            copy = remote(src.at[p], dst.at[me], send_sem.at[phase, k], recv_sem.at[phase, k], device(p))
            copy.start()
            copies.append(copy)
        dst[me] = src[me]
        return copies

    pl.semaphore_wait(barrier, 30)
    phase1 = exchange(0, s1, r1, me_xz, dev_xz, far_xz)

    mirror, is_own = lax.rem(16 - gy, 16), lax.rem(gy, 8) == 0
    first_local = pltpu.make_async_copy(mode_hbm.at[:, 0], mode_first, lsem.at[16])
    first_copy = remote(mode_hbm.at[:, 0], mode_first, psend.at[0], precv.at[0], dev_y(mirror))
    rest_copy = remote(mode_hbm.at[:, pl.ds(1, 2)], mode_rest, psend.at[1], precv.at[1], dev_y(15 - gy))

    @pl.when(is_own)
    def _():
        first_local.start()

    @pl.when(jnp.logical_not(is_own))
    def _():
        first_copy.start()

    rest_copy.start()

    halo_copies = []

    def halo_send(index, src, dst, device):
        copy = remote(src, dst, hsend.at[index], hrecv.at[index], device)
        copy.start()
        halo_copies.append(copy)
        return copy

    own_slot, far_slot = mine, 1 - mine
    inner = pl.ds(1, 2)
    own = halo.at[1, own_slot, inner]
    up_y, down_y = dev_y(lax.rem(gy + 1, 16)), dev_y(lax.rem(gy + 15, 16))
    up_z, down_z = {"gz": lax.rem(gz + 1, 4)}, {"gz": lax.rem(gz + 3, 4)}

    def send_z(index, slot):
        return [
            halo_send(index, halo.at[1, slot, 2], halo.at[1, slot, 0], up_z),
            halo_send(index + 1, halo.at[1, slot, 1], halo.at[1, slot, 3], down_z),
        ]

    def send_y(index, slot, cells):
        return [
            halo_send(index, halo.at[1, slot, cells], halo.at[0, slot, cells], up_y),
            halo_send(index + 1, halo.at[1, slot, cells], halo.at[2, slot, cells], down_y),
        ]


    loads["wq"].wait()
    for c in range(2):
        qs[c] = dot_nn(feat_ref[c], wq_ref[...]).astype(BF16)
        pos = aux[c, 0:3, :]
        qx, qy, qz = pos[0:1, :], pos[1:2, :], pos[2:3, :] + float(c)
        norm = split3(qx * qx + qy * qy + qz * qz)
        one = jnp.ones((1, 128), F32)
        rows = jnp.concatenate(
            [-2.0 * pos, -2.0 * pos, one, one, one, *norm, -2.0 * c * one, -2.0 * c * one, 0.0 * one, 0.0 * one],
            axis=0,
        )
        qaug[c] = dot_nt(eye, rows.astype(BF16)).astype(BF16)
        smax[c] = jnp.full((128, 128), -jnp.inf, F32)

    for copy in phase1:
        copy.wait_send()
    own_z = send_z(0, own_slot)
    far_copy = halo_send(4, own, own, {"gx": 3 - gx})
    loads["mode"].wait()
    loads["pick"].wait()
    at_k = mode_own[...].astype(F32).reshape(144, 768).astype(BF16)
    for t in range(2):
        picked = dot_nn(at_k[:, 384 * t : 384 * t + 384], pick_ref[:, 0 : 2 * NL]).astype(BF16)
        for e in range(2):
            wsend[2 * t + e, :, 0:NL] = picked[:, NL * e : NL * e + NL]

    @pl.when(is_own)
    def _():
        first_local.wait()

    @pl.when(jnp.logical_not(is_own))
    def _():
        first_copy.wait()

    rest_copy.wait()
    first = mode_first[...].astype(F32).reshape(2, 1, 24, 768)
    rest = mode_rest[...].astype(F32)
    at_minus_k = jnp.concatenate([first, rest[:, 1:2], rest[:, 0:1]], axis=1).reshape(144, 768).astype(BF16)
    for t in range(2):
        picked = dot_nn(at_minus_k[:, 384 * t : 384 * t + 384], pick_ref[:, 2 * NL : 4 * NL]).astype(BF16)
        for e in range(2):
            wsend[2 * t + e, :, NL : 2 * NL] = picked[:, NL * e : NL * e + NL]
    weights = []
    for off in (2, 1, 3):
        p = lax.rem(gx + off, 4)
        copy = remote(wsend.at[p], wrecv.at[gx], wsem.at[off], wrsem.at[off], {"gx": p})
        copy.start()
        weights.append(copy)
    wrecv[gx] = wsend[gx]
    own_y = send_y(2, own_slot, inner)

    for copy in phase1:
        copy.wait_recv()
    for g in range(4):
        for t in range(2):
            first, second = swap_halves(r1[4 * g + 2 * t].astype(F32), r1[4 * g + 2 * t + 1].astype(F32))
            x1[128 * g : 128 * g + 64, 128 * t : 128 * t + 128] = first.astype(BF16)
            x1[128 * g + 64 : 128 * g + 128, 128 * t : 128 * t + 128] = second.astype(BF16)
    loads["fx"].wait()
    loads["fz"].wait()
    field = dot_nn(x1[...], fx_ref[...]).astype(BF16)
    t2[0:512, :] = field[:, 0:NL]
    t2[512:1024, :] = field[:, NL : 2 * NL]
    s2[...] = dot_nn(fz_ref[...], t2[...]).astype(BF16).reshape(16, 48, NL)
    phase2 = exchange(1, s2, r2, gy, dev_y, near_y)

    for copy in own_z:
        copy.wait_recv()
    for copy in phase2:
        copy.wait_send()
    own_y += send_y(5, own_slot, 0) + send_y(7, own_slot, 3)
    odd_core = lax.rem(gx, 2)
    near_step = (1 - 2 * odd_core).astype(F32)

    coef = [coef_ref[k] * LOG2E for k in range(NRBF)]
    scale = LOG2E / math.sqrt(D)

    def score_slab(y, x):
        slab = 3 * y + x
        feats = halo[y, x, :, 0:128, :].reshape(512, 128)
        keys = dot_nn(feats, wk_ref[...]).astype(BF16)
        vext[slab, :, 0:128] = dot_nn(feats, wv_ref[...]).astype(BF16)
        vext[slab, :, 128:256] = jnp.ones((512, 128), BF16)
        off_x = 0.0 if x is own_slot else (near_step if x is NEAR else -near_step)
        off_y = float(y - 1)
        one = jnp.ones((1, 128), F32)
        masks = []
        for z in range(4):
            rows = halo[y, x, z, 128:144, :].astype(F32)
            pos = rows[0:3, :]
            kx, ky, kz = pos[0:1, :] + off_x, pos[1:2, :] + off_y, pos[2:3, :] + float(z - 1)
            norm = split3(kx * kx + ky * ky + kz * kz)
            kaug[:, 128 * z : 128 * z + 128] = jnp.concatenate(
                [
                    pos, off_x * one, off_y * one, float(z - 1) * one, *norm, one, one, one,
                    pos[2:3, :], float(z - 1) * one, 0.0 * one, 0.0 * one,
                ],
                axis=0,
            ).astype(BF16)
            masks.append(jnp.where(rows[3:4, :] > 0.5, 0.0, -jnp.inf))
        mask = jnp.concatenate(masks, axis=1)
        for c in range(2):
            scores[slab, c] = dot_nt(qs[c], keys[128 * c : 128 * c + 384, :])
            dist[c] = dot_nn(qaug[c], kaug[:, 128 * c : 128 * c + 384])
            for r in range(0, 128, 16):
                t = jnp.exp2(dist[c, r : r + 16, :] * (-0.08 * LOG2E))
                powers = [t]
                for k in range(NRBF - 2):
                    powers.append(powers[-1] * powers[-1])
                bias = coef[NRBF - 1] * powers[-1] + coef[NRBF - 2]
                for k in range(NRBF - 3, -1, -1):
                    bias = bias * powers[k] + coef[k]
                bias = bias * t
                full = scores[slab, c, r : r + 16, :] * scale + bias + mask[:, 128 * c : 128 * c + 384]
                scores[slab, c, r : r + 16, :] = full
                top = jnp.maximum(jnp.maximum(full[:, 0:128], full[:, 128:256]), full[:, 256:384])
                smax[c, r : r + 16, :] = jnp.maximum(smax[c, r : r + 16, :], top)

    loads["wk"].wait()
    loads["wv"].wait()
    score_slab(1, own_slot)

    loads["fy"].wait()
    for copy in phase2:
        copy.wait_recv()
    lines = jnp.concatenate([r2[:, 16 * j : 16 * j + 16, :].reshape(256, NL) for j in range(3)], axis=1)
    spectrum = dot_nn(fy_ref[...], lines)
    for copy in weights:
        copy.wait_recv()
    for name in ("iy",):
        loads[name].wait()
    received = [wrecv[q].astype(F32) for q in range(4)]

    def lines_of(first_lane):
        return [
            jnp.concatenate(
                [received[q][24 * i : 24 * i + 24, first_lane : first_lane + NL] for q in range(4)], axis=0
            )
            for i in range(6)
        ]

    place = lax.broadcasted_iota(jnp.int32, (MY, MY), 0) + lax.broadcasted_iota(jnp.int32, (MY, MY), 1)
    flip = jnp.logical_or(place == 0, place == MY).astype(F32).astype(BF16)
    minus = dot_nn(flip, jnp.concatenate(lines_of(NL), axis=1).astype(BF16))
    plus = jnp.concatenate(lines_of(0), axis=1)
    norm = 1.0 / (MX * MY * MZ)
    w_real = (plus[:, 0 : 3 * NL] + minus[:, 0 : 3 * NL]) * norm
    w_imag = (plus[:, 3 * NL : 6 * NL] - minus[:, 3 * NL : 6 * NL]) * norm
    real, imag = spectrum[0:MY, :], spectrum[MY : 2 * MY, :]
    mixed = jnp.concatenate(
        [real * w_real - imag * w_imag, real * w_imag + imag * w_real], axis=0
    ).astype(BF16)
    lines = dot_nn(iy_ref[...], mixed).astype(BF16)
    for j in range(3):
        s3[:, 16 * j : 16 * j + 16, :] = lines[:, NL * j : NL * j + NL].reshape(16, 16, NL)
    phase3 = exchange(2, s3, r3, gy, dev_y, near_y)

    for copy in own_y:
        copy.wait_recv()
    near = halo_send(13, halo.at[:, own_slot], halo.at[:, NEAR], {"gx": gx + 1 - 2 * odd_core})
    far_copy.wait_recv()
    far_z = send_z(9, far_slot)
    score_slab(0, own_slot)
    score_slab(2, own_slot)
    near.wait_recv()
    for y in range(3):
        score_slab(y, NEAR)
    for copy in far_z:
        copy.wait_recv()
    far_y = send_y(11, far_slot, pl.ds(0, 4))

    for copy in phase3:
        copy.wait_recv()
    loads["iz"].wait()
    loads["ix"].wait()
    back = dot_nn(iz_ref[...], r3[...].reshape(768, NL)).astype(BF16)
    v2[:, 0:NL] = back[0:512, :]
    v2[:, NL : 2 * NL] = back[512:1024, :]
    potential = dot_nn(v2[...], ix_ref[...])
    for g in range(4):
        for t in range(2):
            even, odd = swap_halves(
                potential[128 * g : 128 * g + 64, 128 * t : 128 * t + 128],
                potential[128 * g + 64 : 128 * g + 128, 128 * t : 128 * t + 128],
            )
            s4[4 * g + 2 * t] = even.astype(BF16)
            s4[4 * g + 2 * t + 1] = odd.astype(BF16)
    phase4 = exchange(3, s4, r4, me_xz, dev_xz, far_xz)

    score_slab(1, far_slot)
    for copy in far_y:
        copy.wait_recv()
    score_slab(0, far_slot)
    score_slab(2, far_slot)
    after = []
    for name in ("wo", "wup", "wdown"):
        loads[name].wait()
    for c in range(2):
        top = jnp.max(smax[c], axis=1, keepdims=True)

        def mix(slab, acc, c=c, top=top):
            probs = jnp.exp2(scores[slab, c] - top).astype(BF16)
            return acc + dot_nn(probs, vext[slab, 128 * c : 128 * c + 384, :])

        acc = lax.fori_loop(0, 9, mix, jnp.zeros((128, 256), F32))
        attended = (acc[:, 0:128] / acc[:, 128:256]).astype(BF16)
        after.append(feat_ref[c].astype(F32) + dot_nn(attended, wo_ref[...]))

    for copy in phase4:
        copy.wait_recv()
    fields = [[], []]
    for t in range(8):
        first, second = swap_halves(r4[2 * t].astype(F32), r4[2 * t + 1].astype(F32))
        fields[0].append(first.astype(BF16))
        fields[1].append(second.astype(BF16))
    for c in range(2):
        lines = dot_tn(wyz[c], jnp.concatenate(fields[c], axis=1))
        lines = jnp.concatenate(
            [lines[:, 128 * t : 128 * t + 128] * wx[c] for t in range(8)], axis=1
        ).astype(BF16)
        sampled = dot_nt(lines, rep[...])
        norm_scale = lax.rsqrt(jnp.mean(sampled * sampled, axis=1, keepdims=True) + 1e-06)
        joined = after[c] + sampled * norm_scale * gain_ref[...]
        inner = dot_nn(joined.astype(BF16), wup_ref[...])
        inner = (inner * jax.nn.sigmoid(inner)).astype(BF16)
        result = joined + dot_nn(inner, wdown_ref[...])
        out_ref[c] = jnp.where(cols[c][:, 3:4] > 0.5, result, 0.0).astype(BF16)

    for copy in phase3 + phase4 + weights + halo_copies:
        copy.wait_send()


def per_device(
    features,
    frac,
    subpoint,
    counts,
    w_query,
    w_key,
    w_value,
    rbf_coef,
    w_out,
    w_charge,
    mode_weight,
    mesh_gain,
    w_up,
    w_down,
):
    mode_rows = jnp.transpose(mode_weight, (0, 2, 1, 3))
    vmem = pl.BlockSpec(memory_space=pltpu.VMEM)
    smem = pl.BlockSpec(memory_space=pltpu.SMEM)
    hbm = pl.BlockSpec(memory_space=pltpu.HBM)
    out = pl.pallas_call(
        kernel,
        out_shape=jax.ShapeDtypeStruct((2, 128, 128), BF16),
        in_specs=[hbm, vmem, vmem, smem, smem, vmem] + [hbm] * 15,
        out_specs=vmem,
        scratch_shapes=[
            pltpu.VMEM((2, 128, 128), BF16),
            pltpu.VMEM((128, 128), BF16),
            pltpu.VMEM((128, 128), BF16),
            pltpu.VMEM((128, 128), BF16),
            pltpu.VMEM((128, 128), BF16),
            pltpu.VMEM((128, 128), BF16),
            pltpu.VMEM((128, 256), BF16),
            pltpu.VMEM((256, 128), BF16),
            pltpu.VMEM((256, 2 * NL), BF16),
            pltpu.VMEM((768, 1024), BF16),
            pltpu.VMEM((192, 256), BF16),
            pltpu.VMEM((256, 192), BF16),
            pltpu.VMEM((1024, 768), BF16),
            pltpu.VMEM((2 * NL, 256), BF16),
            pltpu.VMEM((384, 4 * NL), BF16),
            pltpu.VMEM((2, 3, 24, 768), BF16),
            pltpu.VMEM((2, 24, 768), BF16),
            pltpu.VMEM((2, 2, 24, 768), BF16),
            pltpu.VMEM((4, 144, 2 * NL), BF16),
            pltpu.VMEM((3, 3, 4, 144, 128), BF16),
            pltpu.VMEM((16, 64, 128), BF16),
            pltpu.VMEM((16, 64, 128), BF16),
            pltpu.VMEM((16, 48, NL), BF16),
            pltpu.VMEM((16, 48, NL), BF16),
            pltpu.VMEM((16, 48, NL), BF16),
            pltpu.VMEM((16, 48, NL), BF16),
            pltpu.VMEM((16, 64, 128), BF16),
            pltpu.VMEM((16, 64, 128), BF16),
            pltpu.VMEM((4, 144, 2 * NL), BF16),
            pltpu.VMEM((2, 16, 128), F32),
            pltpu.VMEM((512, 256), BF16),
            pltpu.VMEM((1024, NL), BF16),
            pltpu.VMEM((512, 2 * NL), BF16),
            pltpu.VMEM((2, 64, 128), BF16),
            pltpu.VMEM((2, 128, 128), F32),
            pltpu.VMEM((128, 1024), BF16),
            pltpu.VMEM((2, 128, 16), F32),
            pltpu.VMEM((2, 128, 128), BF16),
            pltpu.VMEM((2, 128, 16), BF16),
            pltpu.VMEM((16, 512), BF16),
            pltpu.VMEM((9, 2, 128, 384), F32),
            pltpu.VMEM((2, 128, 384), F32),
            pltpu.VMEM((9, 512, 256), BF16),
            pltpu.VMEM((2, 128, 128), F32),
            pltpu.SemaphoreType.DMA((4, 16)),
            pltpu.SemaphoreType.DMA((4, 16)),
            pltpu.SemaphoreType.DMA((14,)),
            pltpu.SemaphoreType.DMA((14,)),
            pltpu.SemaphoreType.DMA((4,)),
            pltpu.SemaphoreType.DMA((4,)),
            pltpu.SemaphoreType.DMA((17,)),
            pltpu.SemaphoreType.DMA((2,)),
            pltpu.SemaphoreType.DMA((2,)),
        ],
        compiler_params=pltpu.CompilerParams(
            collective_id=0, has_side_effects=True, vmem_limit_bytes=63 * 1024 * 1024
        ),
    )(
        features.reshape(2, 128, 128),
        jnp.transpose(frac.reshape(2, 3, 128), (1, 0, 2)),
        jnp.transpose(subpoint.reshape(2, 3, 128), (1, 0, 2)),
        counts.reshape(2),
        rbf_coef,
        mesh_gain.reshape(1, 128),
        w_query,
        w_key,
        w_value,
        w_out,
        w_charge,
        w_up,
        w_down,
        mode_rows,
        *tables(),
    )
    return out.reshape(features.shape)


def solution(mesh):
    return jax.shard_map(
        per_device,
        mesh=mesh,
        in_specs=(
            P("gx", "gy", "gz", None, None),
            P("gx", "gy", "gz", None, None),
            P("gx", "gy", "gz", None, None),
            P("gx", "gy", "gz"),
            P(),
            P(),
            P(),
            P(),
            P(),
            P(),
            P(None, "gx", "gy", "gz"),
            P(),
            P(),
            P(),
        ),
        out_specs=P("gx", "gy", "gz", None, None),
        check_vma=False,
    )
```

```python
import functools
import math

import jax
import jax.numpy as jnp
import numpy as np
from jax import lax
from jax.experimental import pallas as pl
from jax.experimental.pallas import tpu as pltpu
from jax.sharding import PartitionSpec as P

MESH = pl.DeviceIdType.MESH
F32 = jnp.float32
BF16 = jnp.bfloat16

D = 128
R = 6
NRBF = 8
MX, MY, MZ = 24, 96, 48
NL = 128
LOG2E = math.log2(math.e)
NEAR = 2
XZ_STEPS = [(4, 1), (4, 0), (5, 1), (3, 1), (5, 0), (3, 0), (6, 1), (2, 1), (6, 0), (2, 0), (7, 1), (1, 1), (7, 0), (1, 0), (0, 1)]
Y_STEPS = [(0, 1), (0, 3), (1, 0), (3, 0), (1, 1), (3, 3), (1, 3), (3, 1), (0, 2), (2, 0), (1, 2), (2, 1), (3, 2), (2, 3), (2, 2)]


def tables():
    gx, ch, px = np.meshgrid(np.arange(4), np.arange(8), np.arange(8), indexing="ij")
    x_pos, x_ch = (6 * gx + px - 1).reshape(-1), ch.reshape(-1)
    lane = np.arange(NL)
    l_ch, l_kx, l_ok = lane // 16, lane % 16, lane % 16 <= MX // 2
    ang = 2 * np.pi / MX * ((x_pos[:, None] * l_kx[None, :]) % MX)
    same = (x_ch[:, None] == l_ch[None, :]) & l_ok[None, :]
    cos_x, sin_x = np.where(same, np.cos(ang), 0.0), np.where(same, np.sin(ang), 0.0)
    fwd_x = np.concatenate([cos_x, -sin_x], axis=1)
    inv_x = np.concatenate([cos_x.T, -sin_x.T], axis=0)

    row = np.arange(384)
    pair_lane = np.arange(2 * NL)
    l_ch, l_kx = pair_lane // 16, pair_lane % 16
    share = np.where(l_kx % (MX // 2) == 0, 0.5, 1.0) * (l_kx <= MX // 2)
    picks = [
        (row[:, None] == (l_ch * MX + kx)[None, :]) * share[None, :] for kx in (l_kx, (MX - l_kx) % MX)
    ]
    pick = np.concatenate(picks, axis=1)

    gz, cell, pz = np.meshgrid(np.arange(4), np.arange(2), np.arange(8), indexing="ij")
    z_pos = (12 * gz + 6 * cell + pz - 1).reshape(-1)
    ang = 2 * np.pi / MZ * ((z_pos[None, :] * np.arange(MZ)[:, None]) % MZ)
    c, s = np.cos(ang), np.sin(ang)
    mat = np.stack([np.stack([c, s], 1), np.stack([-s, c], 1)], axis=1)
    eye = np.eye(8)
    fwd_z = np.einsum("kciz,pq->kcpizq", mat, eye).reshape(MZ * 2 * 8, 2 * 64 * 8)
    mat = np.stack([np.stack([c.T, -s.T], -1), np.stack([s.T, c.T], -1)], axis=0)
    inv_z = np.einsum("czki,pq->czpkiq", mat, eye).reshape(2 * 64 * 8, MZ * 2 * 8)

    gy, py = np.meshgrid(np.arange(16), np.arange(8), indexing="ij")
    y_pos = (6 * gy + py - 1)
    ang = 2 * np.pi / MY * ((y_pos[None] * np.arange(MY)[:, None, None]) % MY)
    c, s = np.cos(ang), np.sin(ang)
    fwd_y = np.stack([np.stack([c, s], 2), np.stack([-s, c], 2)], axis=0)
    fwd_y = fwd_y.reshape(2 * MY, 256)
    ct, st = np.moveaxis(c, 0, -1), np.moveaxis(s, 0, -1)
    inv_y = np.stack([np.stack([ct, -st], 2), np.stack([st, ct], 2)], axis=1)
    inv_y = inv_y.reshape(256, 2 * MY)
    return [jnp.asarray(t, dtype=BF16) for t in (fwd_x, fwd_z, fwd_y, inv_y, inv_z, inv_x, pick)]


def dot_nn(a, b):
    return lax.dot_general(a, b, (((1,), (0,)), ((), ())), preferred_element_type=F32)


def dot_nt(a, b):
    return lax.dot_general(a, b, (((1,), (1,)), ((), ())), preferred_element_type=F32)


def dot_tn(a, b):
    return lax.dot_general(a, b, (((0,), (0,)), ((), ())), preferred_element_type=F32)


def swap_halves(first, second):
    low = lax.broadcasted_iota(jnp.int32, first.shape, 1) < 64
    return (
        jnp.where(low, first, pltpu.roll(second, 64, 1)),
        jnp.where(low, pltpu.roll(first, 64, 1), second),
    )


def stencil(point, sub, frac):
    offset = point - 1.0 - sub
    lower_w = 0.5 * (0.5 - frac) * (0.5 - frac)
    centre_w = 0.75 - frac * frac
    upper_w = 0.5 * (0.5 + frac) * (0.5 + frac)
    zero = jnp.zeros_like(offset)
    return jnp.where(
        offset == -1.0,
        lower_w,
        jnp.where(offset == 0.0, centre_w, jnp.where(offset == 1.0, upper_w, zero)),
    )


def split3(value):
    high = value.astype(BF16).astype(F32)
    rest = value - high
    middle = rest.astype(BF16).astype(F32)
    return high, middle, rest - middle


def kernel(
    feat_hbm,
    frac_ref,
    sub_ref,
    counts_ref,
    coef_ref,
    gain_ref,
    wq_hbm,
    wk_hbm,
    wv_hbm,
    wo_hbm,
    wch_hbm,
    wup_hbm,
    wdown_hbm,
    mode_hbm,
    fx_hbm,
    fz_hbm,
    fy_hbm,
    iy_hbm,
    iz_hbm,
    ix_hbm,
    pick_hbm,
    out_ref,
    feat_ref,
    wq_ref,
    wk_ref,
    wv_ref,
    wo_ref,
    wch_ref,
    wup_ref,
    wdown_ref,
    fx_ref,
    fz_ref,
    fy_ref,
    iy_ref,
    iz_ref,
    ix_ref,
    pick_ref,
    mode_own,
    mode_first,
    mode_rest,
    wsend,
    halo,
    s1,
    r1,
    s2,
    r2,
    s3,
    r3,
    s4,
    r4,
    wrecv,
    aux,
    x1,
    t2,
    v2,
    wyz,
    wx,
    rep,
    rep_t,
    wyz_t,
    cols,
    qs,
    qaug,
    kaug,
    scores,
    dist,
    vext,
    smax,
    send_sem,
    recv_sem,
    hsend,
    hrecv,
    wsem,
    wrsem,
    lsem,
    psend,
    precv,
):
    gx, gy, gz = lax.axis_index("gx"), lax.axis_index("gy"), lax.axis_index("gz")
    me_xz = gz * 4 + gx

    def dev_xz(p):
        return {"gx": lax.rem(p, 4), "gz": lax.div(p, 4)}

    def dev_y(p):
        return {"gy": p}

    def remote(src, dst, ssem, rsem, device):
        return pltpu.make_async_remote_copy(
            src_ref=src, dst_ref=dst, send_sem=ssem, recv_sem=rsem, device_id=device, device_id_type=MESH
        )

    z_chip, core = lax.div(gx, 2) * 4 + gz, lax.rem(gx, 2)
    far_xz, near_y = [], []
    for step, other in XZ_STEPS:
        z = lax.rem(z_chip + step, 8)
        far_xz.append(lax.rem(z, 4) * 4 + lax.div(z, 4) * 2 + (core if other == 0 else 1 - core))
    for step_x, step_y in Y_STEPS:
        near_y.append(lax.rem(lax.div(gy, 4) + step_x, 4) * 4 + lax.rem(lax.rem(gy, 4) + step_y, 4))
    barrier = pltpu.get_barrier_semaphore()
    for p in far_xz:
        pl.semaphore_signal(barrier, inc=1, device_id=dev_xz(p), device_id_type=MESH)
    for p in near_y[::-1]:
        pl.semaphore_signal(barrier, inc=1, device_id=dev_y(p), device_id_type=MESH)

    loads = {}

    def load(index, name, src, dst):
        loads[name] = pltpu.make_async_copy(src, dst, lsem.at[index])
        loads[name].start()

    load(0, "feat", feat_hbm, feat_ref)
    load(1, "wch", wch_hbm, wch_ref)
    load(2, "wq", wq_hbm, wq_ref)
    load(3, "fx", fx_hbm, fx_ref)
    load(4, "fz", fz_hbm, fz_ref)
    load(5, "wk", wk_hbm, wk_ref)
    load(6, "wv", wv_hbm, wv_ref)
    load(7, "mode", mode_hbm, mode_own)
    load(15, "pick", pick_hbm, pick_ref)
    load(8, "fy", fy_hbm, fy_ref)
    load(9, "iy", iy_hbm, iy_ref)
    load(10, "iz", iz_hbm, iz_ref)
    load(11, "ix", ix_hbm, ix_ref)
    load(12, "wo", wo_hbm, wo_ref)
    load(13, "wup", wup_hbm, wup_ref)
    load(14, "wdown", wdown_hbm, wdown_ref)

    mine = lax.div(gx, 2)
    lane_row = lax.broadcasted_iota(jnp.int32, (1, 128), 1)
    aux[...] = jnp.zeros_like(aux)
    for c in range(2):
        sub = jnp.concatenate([sub_ref[d, c : c + 1, :] for d in range(3)], axis=0).astype(F32)
        frac = jnp.concatenate([frac_ref[d, c : c + 1, :].astype(F32) for d in range(3)], axis=0)
        aux[c, 0:3, :] = ((sub + 0.5 + frac) / R).astype(BF16).astype(F32)
        aux[c, 3:4, :] = (lane_row < counts_ref[c]).astype(F32)
        aux[c, 4:7, :] = frac
        aux[c, 7:10, :] = sub
        halo[1, mine, 1 + c, 128:144, :] = aux[c].astype(BF16)
    loads["feat"].wait()
    for c in range(2):
        halo[1, mine, 1 + c, 0:128, :] = feat_ref[c]

    row_i = lax.broadcasted_iota(jnp.int32, (128, 1024), 0)
    lane_i = lax.broadcasted_iota(jnp.int32, (128, 1024), 1)
    rep[...] = (lax.shift_right_logical(lane_i, 3) == row_i).astype(F32).astype(BF16)
    eye = (
        lax.broadcasted_iota(jnp.int32, (128, 128), 0) == lax.broadcasted_iota(jnp.int32, (128, 128), 1)
    ).astype(F32).astype(BF16)
    loads["wch"].wait()
    wch = dot_nn(wch_ref[...], rep[...]).astype(BF16)
    point_rows = lax.broadcasted_iota(jnp.int32, (8, 128), 0).astype(F32)
    point_lanes = lax.bitwise_and(lax.broadcasted_iota(jnp.int32, (128, 128), 1), 7).astype(F32)
    spread = []
    for c in range(2):
        cols[c] = dot_nt(eye, aux[c].astype(BF16))
        col = cols[c]
        wy = stencil(point_rows, aux[c, 8:9, :], aux[c, 5:6, :])
        wz = stencil(point_rows, aux[c, 9:10, :], aux[c, 6:7, :])
        wyz[c] = jnp.concatenate([wz[p : p + 1, :] * wy for p in range(8)], axis=0).astype(BF16)
        wx[c] = stencil(point_lanes, col[:, 7:8], col[:, 4:5])
        wxv = wx[c] * col[:, 3:4]
        charge = dot_nn(feat_ref[c], wch)
        scaled = jnp.concatenate(
            [charge[:, 128 * t : 128 * t + 128] * wxv for t in range(8)], axis=1
        ).astype(BF16)
        spread.append(dot_nn(wyz[c], scaled))
    for t in range(8):
        even, odd = swap_halves(
            spread[0][:, 128 * t : 128 * t + 128], spread[1][:, 128 * t : 128 * t + 128]
        )
        s1[2 * t] = even.astype(BF16)
        s1[2 * t + 1] = odd.astype(BF16)

    def exchange(phase, src, dst, me, device, partners):
        copies = []
        for k, p in enumerate(partners):
            copy = remote(src.at[p], dst.at[me], send_sem.at[phase, k], recv_sem.at[phase, k], device(p))
            copy.start()
            copies.append(copy)
        dst[me] = src[me]
        return copies

    pl.semaphore_wait(barrier, 30)
    phase1 = exchange(0, s1, r1, me_xz, dev_xz, far_xz)

    mirror, is_own = lax.rem(16 - gy, 16), lax.rem(gy, 8) == 0
    first_local = pltpu.make_async_copy(mode_hbm.at[:, 0], mode_first, lsem.at[16])
    first_copy = remote(mode_hbm.at[:, 0], mode_first, psend.at[0], precv.at[0], dev_y(mirror))
    rest_copy = remote(mode_hbm.at[:, pl.ds(1, 2)], mode_rest, psend.at[1], precv.at[1], dev_y(15 - gy))

    @pl.when(is_own)
    def _():
        first_local.start()

    @pl.when(jnp.logical_not(is_own))
    def _():
        first_copy.start()

    rest_copy.start()

    halo_copies = []

    def halo_send(index, src, dst, device):
        copy = remote(src, dst, hsend.at[index], hrecv.at[index], device)
        copy.start()
        halo_copies.append(copy)
        return copy

    own_slot, far_slot = mine, 1 - mine
    inner = pl.ds(1, 2)
    own = halo.at[1, own_slot, inner]
    up_y, down_y = dev_y(lax.rem(gy + 1, 16)), dev_y(lax.rem(gy + 15, 16))
    up_z, down_z = {"gz": lax.rem(gz + 1, 4)}, {"gz": lax.rem(gz + 3, 4)}

    def send_z(index, slot):
        return [
            halo_send(index, halo.at[1, slot, 2], halo.at[1, slot, 0], up_z),
            halo_send(index + 1, halo.at[1, slot, 1], halo.at[1, slot, 3], down_z),
        ]

    def send_y(index, slot, cells):
        return [
            halo_send(index, halo.at[1, slot, cells], halo.at[0, slot, cells], up_y),
            halo_send(index + 1, halo.at[1, slot, cells], halo.at[2, slot, cells], down_y),
        ]


    row_t = lax.broadcasted_iota(jnp.int32, (1024, 128), 0)
    lane_t = lax.broadcasted_iota(jnp.int32, (1024, 128), 1)
    rep_t[...] = (lax.shift_right_logical(row_t, 3) == lane_t).astype(F32).astype(BF16)
    for c in range(2):
        wyz_t[c] = dot_nt(eye, wyz[c]).astype(BF16)

    loads["wq"].wait()
    for c in range(2):
        qs[c] = dot_nn(feat_ref[c], wq_ref[...]).astype(BF16)
        pos = aux[c, 0:3, :]
        qx, qy, qz = pos[0:1, :], pos[1:2, :], pos[2:3, :] + float(c)
        norm = split3(qx * qx + qy * qy + qz * qz)
        one = jnp.ones((1, 128), F32)
        rows = jnp.concatenate(
            [-2.0 * pos, -2.0 * pos, one, one, one, *norm, -2.0 * c * one, -2.0 * c * one, 0.0 * one, 0.0 * one],
            axis=0,
        )
        qaug[c] = dot_nt(eye, rows.astype(BF16)).astype(BF16)
        smax[c] = jnp.full((128, 128), -jnp.inf, F32)

    for copy in phase1:
        copy.wait_send()
    own_z = send_z(0, own_slot)
    far_copy = halo_send(4, own, own, {"gx": 3 - gx})
    loads["mode"].wait()
    loads["pick"].wait()
    at_k = mode_own[...].astype(F32).reshape(144, 768).astype(BF16)
    for t in range(2):
        picked = dot_nn(at_k[:, 384 * t : 384 * t + 384], pick_ref[:, 0 : 2 * NL]).astype(BF16)
        for e in range(2):
            wsend[2 * t + e, :, 0:NL] = picked[:, NL * e : NL * e + NL]

    @pl.when(is_own)
    def _():
        first_local.wait()

    @pl.when(jnp.logical_not(is_own))
    def _():
        first_copy.wait()

    rest_copy.wait()
    first = mode_first[...].astype(F32).reshape(2, 1, 24, 768)
    rest = mode_rest[...].astype(F32)
    at_minus_k = jnp.concatenate([first, rest[:, 1:2], rest[:, 0:1]], axis=1).reshape(144, 768).astype(BF16)
    for t in range(2):
        picked = dot_nn(at_minus_k[:, 384 * t : 384 * t + 384], pick_ref[:, 2 * NL : 4 * NL]).astype(BF16)
        for e in range(2):
            wsend[2 * t + e, :, NL : 2 * NL] = picked[:, NL * e : NL * e + NL]
    weights = []
    for off in (2, 1, 3):
        p = lax.rem(gx + off, 4)
        copy = remote(wsend.at[p], wrecv.at[gx], wsem.at[off], wrsem.at[off], {"gx": p})
        copy.start()
        weights.append(copy)
    wrecv[gx] = wsend[gx]
    own_y = send_y(2, own_slot, inner)

    for copy in phase1:
        copy.wait_recv()
    for g in range(4):
        for t in range(2):
            first, second = swap_halves(r1[4 * g + 2 * t].astype(F32), r1[4 * g + 2 * t + 1].astype(F32))
            x1[128 * g : 128 * g + 64, 128 * t : 128 * t + 128] = first.astype(BF16)
            x1[128 * g + 64 : 128 * g + 128, 128 * t : 128 * t + 128] = second.astype(BF16)
    loads["fx"].wait()
    loads["fz"].wait()
    field = dot_nn(x1[...], fx_ref[...]).astype(BF16)
    t2[0:512, :] = field[:, 0:NL]
    t2[512:1024, :] = field[:, NL : 2 * NL]
    s2[...] = dot_nn(fz_ref[...], t2[...]).astype(BF16).reshape(16, 48, NL)
    phase2 = exchange(1, s2, r2, gy, dev_y, near_y)

    for copy in own_z:
        copy.wait_recv()
    for copy in phase2:
        copy.wait_send()
    own_y += send_y(5, own_slot, 0) + send_y(7, own_slot, 3)
    odd_core = lax.rem(gx, 2)
    near_step = (1 - 2 * odd_core).astype(F32)

    coef = [coef_ref[k] * LOG2E for k in range(NRBF)]
    scale = LOG2E / math.sqrt(D)

    def score_slab(y, x):
        slab = 3 * y + x
        feats = halo[y, x, :, 0:128, :].reshape(512, 128)
        keys = dot_nn(feats, wk_ref[...]).astype(BF16)
        vext[slab, :, 0:128] = dot_nn(feats, wv_ref[...]).astype(BF16)
        vext[slab, :, 128:256] = jnp.ones((512, 128), BF16)
        off_x = 0.0 if x is own_slot else (near_step if x is NEAR else -near_step)
        off_y = float(y - 1)
        one = jnp.ones((1, 128), F32)
        masks = []
        for z in range(4):
            rows = halo[y, x, z, 128:144, :].astype(F32)
            pos = rows[0:3, :]
            kx, ky, kz = pos[0:1, :] + off_x, pos[1:2, :] + off_y, pos[2:3, :] + float(z - 1)
            norm = split3(kx * kx + ky * ky + kz * kz)
            kaug[:, 128 * z : 128 * z + 128] = jnp.concatenate(
                [
                    pos, off_x * one, off_y * one, float(z - 1) * one, *norm, one, one, one,
                    pos[2:3, :], float(z - 1) * one, 0.0 * one, 0.0 * one,
                ],
                axis=0,
            ).astype(BF16)
            masks.append(jnp.where(rows[3:4, :] > 0.5, 0.0, -jnp.inf))
        mask = jnp.concatenate(masks, axis=1)
        for c in range(2):
            scores[slab, c] = dot_nt(qs[c], keys[128 * c : 128 * c + 384, :])
            dist[c] = dot_nn(qaug[c], kaug[:, 128 * c : 128 * c + 384])
            for r in range(0, 128, 16):
                t = jnp.exp2(dist[c, r : r + 16, :] * (-0.08 * LOG2E))
                powers = [t]
                for k in range(NRBF - 2):
                    powers.append(powers[-1] * powers[-1])
                bias = coef[NRBF - 1] * powers[-1] + coef[NRBF - 2]
                for k in range(NRBF - 3, -1, -1):
                    bias = bias * powers[k] + coef[k]
                bias = bias * t
                full = scores[slab, c, r : r + 16, :] * scale + bias + mask[:, 128 * c : 128 * c + 384]
                scores[slab, c, r : r + 16, :] = full
                top = jnp.maximum(jnp.maximum(full[:, 0:128], full[:, 128:256]), full[:, 256:384])
                smax[c, r : r + 16, :] = jnp.maximum(smax[c, r : r + 16, :], top)

    loads["wk"].wait()
    loads["wv"].wait()
    score_slab(1, own_slot)

    loads["fy"].wait()
    for copy in phase2:
        copy.wait_recv()
    lines = jnp.concatenate([r2[:, 16 * j : 16 * j + 16, :].reshape(256, NL) for j in range(3)], axis=1)
    spectrum = dot_nn(fy_ref[...], lines)
    for copy in weights:
        copy.wait_recv()
    for name in ("iy",):
        loads[name].wait()
    received = [wrecv[q].astype(F32) for q in range(4)]

    def lines_of(first_lane):
        return [
            jnp.concatenate(
                [received[q][24 * i : 24 * i + 24, first_lane : first_lane + NL] for q in range(4)], axis=0
            )
            for i in range(6)
        ]

    place = lax.broadcasted_iota(jnp.int32, (MY, MY), 0) + lax.broadcasted_iota(jnp.int32, (MY, MY), 1)
    flip = jnp.logical_or(place == 0, place == MY).astype(F32).astype(BF16)
    minus = dot_nn(flip, jnp.concatenate(lines_of(NL), axis=1).astype(BF16))
    plus = jnp.concatenate(lines_of(0), axis=1)
    norm = 1.0 / (MX * MY * MZ)
    w_real = (plus[:, 0 : 3 * NL] + minus[:, 0 : 3 * NL]) * norm
    w_imag = (plus[:, 3 * NL : 6 * NL] - minus[:, 3 * NL : 6 * NL]) * norm
    real, imag = spectrum[0:MY, :], spectrum[MY : 2 * MY, :]
    mixed = jnp.concatenate(
        [real * w_real - imag * w_imag, real * w_imag + imag * w_real], axis=0
    ).astype(BF16)
    lines = dot_nn(iy_ref[...], mixed).astype(BF16)
    for j in range(3):
        s3[:, 16 * j : 16 * j + 16, :] = lines[:, NL * j : NL * j + NL].reshape(16, 16, NL)
    phase3 = exchange(2, s3, r3, gy, dev_y, near_y)

    for copy in own_y:
        copy.wait_recv()
    near = halo_send(13, halo.at[:, own_slot], halo.at[:, NEAR], {"gx": gx + 1 - 2 * odd_core})
    far_copy.wait_recv()
    far_z = send_z(9, far_slot)
    score_slab(0, own_slot)
    score_slab(2, own_slot)
    near.wait_recv()
    for y in range(3):
        score_slab(y, NEAR)
    for copy in far_z:
        copy.wait_recv()
    far_y = send_y(11, far_slot, pl.ds(0, 4))

    for copy in phase3:
        copy.wait_recv()
    loads["iz"].wait()
    loads["ix"].wait()
    back = dot_nn(iz_ref[...], r3[...].reshape(768, NL)).astype(BF16)
    v2[:, 0:NL] = back[0:512, :]
    v2[:, NL : 2 * NL] = back[512:1024, :]
    potential = dot_nn(v2[...], ix_ref[...])
    for g in range(4):
        for t in range(2):
            even, odd = swap_halves(
                potential[128 * g : 128 * g + 64, 128 * t : 128 * t + 128],
                potential[128 * g + 64 : 128 * g + 128, 128 * t : 128 * t + 128],
            )
            s4[4 * g + 2 * t] = even.astype(BF16)
            s4[4 * g + 2 * t + 1] = odd.astype(BF16)
    phase4 = exchange(3, s4, r4, me_xz, dev_xz, far_xz)

    score_slab(1, far_slot)
    for copy in far_y:
        copy.wait_recv()
    score_slab(0, far_slot)
    score_slab(2, far_slot)
    after = []
    for name in ("wo", "wup", "wdown"):
        loads[name].wait()
    for c in range(2):
        top = jnp.max(smax[c], axis=1, keepdims=True)

        def mix(slab, acc, c=c, top=top):
            probs = jnp.exp2(scores[slab, c] - top).astype(BF16)
            return acc + dot_nn(probs, vext[slab, 128 * c : 128 * c + 384, :])

        acc = lax.fori_loop(0, 9, mix, jnp.zeros((128, 256), F32))
        attended = (acc[:, 0:128] / acc[:, 128:256]).astype(BF16)
        after.append(feat_ref[c].astype(F32) + dot_nn(attended, wo_ref[...]))

    for copy in phase4:
        copy.wait_recv()
    fields = [[], []]
    for t in range(8):
        first, second = swap_halves(r4[2 * t].astype(F32), r4[2 * t + 1].astype(F32))
        fields[0].append(first.astype(BF16))
        fields[1].append(second.astype(BF16))
    for c in range(2):
        lines = dot_nn(wyz_t[c], jnp.concatenate(fields[c], axis=1))
        lines = jnp.concatenate(
            [lines[:, 128 * t : 128 * t + 128] * wx[c] for t in range(8)], axis=1
        ).astype(BF16)
        sampled = dot_nn(lines, rep_t[...])
        norm_scale = lax.rsqrt(jnp.mean(sampled * sampled, axis=1, keepdims=True) + 1e-06)
        joined = after[c] + sampled * norm_scale * gain_ref[...]
        inner = dot_nn(joined.astype(BF16), wup_ref[...])
        inner = (inner * jax.nn.sigmoid(inner)).astype(BF16)
        result = joined + dot_nn(inner, wdown_ref[...])
        out_ref[c] = jnp.where(cols[c][:, 3:4] > 0.5, result, 0.0).astype(BF16)

    for copy in phase3 + phase4 + weights + halo_copies:
        copy.wait_send()


def per_device(
    features,
    frac,
    subpoint,
    counts,
    w_query,
    w_key,
    w_value,
    rbf_coef,
    w_out,
    w_charge,
    mode_weight,
    mesh_gain,
    w_up,
    w_down,
):
    mode_rows = jnp.transpose(mode_weight, (0, 2, 1, 3))
    vmem = pl.BlockSpec(memory_space=pltpu.VMEM)
    smem = pl.BlockSpec(memory_space=pltpu.SMEM)
    hbm = pl.BlockSpec(memory_space=pltpu.HBM)
    out = pl.pallas_call(
        kernel,
        out_shape=jax.ShapeDtypeStruct((2, 128, 128), BF16),
        in_specs=[hbm, vmem, vmem, smem, smem, vmem] + [hbm] * 15,
        out_specs=vmem,
        scratch_shapes=[
            pltpu.VMEM((2, 128, 128), BF16),
            pltpu.VMEM((128, 128), BF16),
            pltpu.VMEM((128, 128), BF16),
            pltpu.VMEM((128, 128), BF16),
            pltpu.VMEM((128, 128), BF16),
            pltpu.VMEM((128, 128), BF16),
            pltpu.VMEM((128, 256), BF16),
            pltpu.VMEM((256, 128), BF16),
            pltpu.VMEM((256, 2 * NL), BF16),
            pltpu.VMEM((768, 1024), BF16),
            pltpu.VMEM((192, 256), BF16),
            pltpu.VMEM((256, 192), BF16),
            pltpu.VMEM((1024, 768), BF16),
            pltpu.VMEM((2 * NL, 256), BF16),
            pltpu.VMEM((384, 4 * NL), BF16),
            pltpu.VMEM((2, 3, 24, 768), BF16),
            pltpu.VMEM((2, 24, 768), BF16),
            pltpu.VMEM((2, 2, 24, 768), BF16),
            pltpu.VMEM((4, 144, 2 * NL), BF16),
            pltpu.VMEM((3, 3, 4, 144, 128), BF16),
            pltpu.VMEM((16, 64, 128), BF16),
            pltpu.VMEM((16, 64, 128), BF16),
            pltpu.VMEM((16, 48, NL), BF16),
            pltpu.VMEM((16, 48, NL), BF16),
            pltpu.VMEM((16, 48, NL), BF16),
            pltpu.VMEM((16, 48, NL), BF16),
            pltpu.VMEM((16, 64, 128), BF16),
            pltpu.VMEM((16, 64, 128), BF16),
            pltpu.VMEM((4, 144, 2 * NL), BF16),
            pltpu.VMEM((2, 16, 128), F32),
            pltpu.VMEM((512, 256), BF16),
            pltpu.VMEM((1024, NL), BF16),
            pltpu.VMEM((512, 2 * NL), BF16),
            pltpu.VMEM((2, 64, 128), BF16),
            pltpu.VMEM((2, 128, 128), F32),
            pltpu.VMEM((128, 1024), BF16),
            pltpu.VMEM((1024, 128), BF16),
            pltpu.VMEM((2, 128, 64), BF16),
            pltpu.VMEM((2, 128, 16), F32),
            pltpu.VMEM((2, 128, 128), BF16),
            pltpu.VMEM((2, 128, 16), BF16),
            pltpu.VMEM((16, 512), BF16),
            pltpu.VMEM((9, 2, 128, 384), F32),
            pltpu.VMEM((2, 128, 384), F32),
            pltpu.VMEM((9, 512, 256), BF16),
            pltpu.VMEM((2, 128, 128), F32),
            pltpu.SemaphoreType.DMA((4, 16)),
            pltpu.SemaphoreType.DMA((4, 16)),
            pltpu.SemaphoreType.DMA((14,)),
            pltpu.SemaphoreType.DMA((14,)),
            pltpu.SemaphoreType.DMA((4,)),
            pltpu.SemaphoreType.DMA((4,)),
            pltpu.SemaphoreType.DMA((17,)),
            pltpu.SemaphoreType.DMA((2,)),
            pltpu.SemaphoreType.DMA((2,)),
        ],
        compiler_params=pltpu.CompilerParams(
            collective_id=0, has_side_effects=True, vmem_limit_bytes=63 * 1024 * 1024
        ),
    )(
        features.reshape(2, 128, 128),
        jnp.transpose(frac.reshape(2, 3, 128), (1, 0, 2)),
        jnp.transpose(subpoint.reshape(2, 3, 128), (1, 0, 2)),
        counts.reshape(2),
        rbf_coef,
        mesh_gain.reshape(1, 128),
        w_query,
        w_key,
        w_value,
        w_out,
        w_charge,
        w_up,
        w_down,
        mode_rows,
        *tables(),
    )
    return out.reshape(features.shape)


def solution(mesh):
    return jax.shard_map(
        per_device,
        mesh=mesh,
        in_specs=(
            P("gx", "gy", "gz", None, None),
            P("gx", "gy", "gz", None, None),
            P("gx", "gy", "gz", None, None),
            P("gx", "gy", "gz"),
            P(),
            P(),
            P(),
            P(),
            P(),
            P(),
            P(None, "gx", "gy", "gz"),
            P(),
            P(),
            P(),
        ),
        out_specs=P("gx", "gy", "gz", None, None),
        check_vma=False,
    )
```
